256 devices in a mesh: tm: 4 (over x_lo, core), space: 64 (over y, z, x_hi).
Axes of the slice: x: 4 (x_hi: 2, x_lo: 2; x = x_hi * 2 + x_lo), y: 4, z: 8, core: 2. Of those that a mesh axis runs over, the one named last changes fastest.
Arguments:
- starts: float32 [8, 64, 256, 128], P('tm', None, 'space'), may hold values from -6 to 6
- volume_op: float32 [64, 64], replicated, as said below
- face_ops: float32 [6, 64, 64], replicated, may hold values from -0.24 to 0.24
- neighbours: int32 [4, 128], replicated, may hold values from 0 to 127, as said below
Outputs:
- new_starts: float32 [8, 64, 256, 128], P('tm', None, 'space')
- end_values: float32 [8, 64, 256, 128], P('tm', None, 'space')
The draws below stay inside these ranges and needn't reach their ends.
Inputs may be any that keep to these rules, and one draw needn't show every extreme that they name: The 128 columns of a layer form a periodic 8 x 16 grid under a relabeling drawn from the seed; neighbours[0] and neighbours[1] are the two neighbours along the first direction, neighbours[2] and neighbours[3] along the second; each row is a permutation. `volume_op`: the diagonal is negative.
All inputs are finite; a program needn't handle non-finite values.
Results may differ from the reference program's by a relative error of at most 0.0001.
Values sent between devices are 32-bit elements; how exact they have to be, the bound alone decides.
No kernel may reach another device: no remote copies, remote signals or barrier semaphores. Data moves between devices by JAX's collectives and lax.ppermute only.
A program may use at most 128 MiB of HBM per device.

```python
import math
import jax
import jax.numpy as jnp
from jax import lax

VALUES = 64
SLICES = 8
ITERS = 2
PY = 8
PZ = 16
EP = 128
NX = 256


def draw_volume_op(key, part):
    key = jax.random.fold_in(key, 11)
    rate_key, off_key = jax.random.split(key)
    decay = jnp.exp(jax.random.uniform(rate_key, (VALUES,), jnp.float32, jnp.log(0.05), jnp.log(2.0)))
    spread = 0.04 * jax.random.normal(off_key, (VALUES, VALUES), jnp.float32)
    eye = jnp.eye(VALUES, dtype=jnp.float32)
    return spread * (1.0 - eye) - eye * (decay[None, :] + 0.3 * jnp.abs(spread))


def draw_neighbours(key, part):
    key = jax.random.fold_in(key, 23)
    labels = jax.random.permutation(key, EP).astype(jnp.int32)
    places = jnp.arange(EP, dtype=jnp.int32)
    first = places // PZ
    second = places % PZ
    beside = jnp.stack([(first + PY - 1) % PY * PZ + second, (first + 1) % PY * PZ + second, first * PZ + (second + PZ - 1) % PZ, first * PZ + (second + 1) % PZ])
    return jnp.zeros((4, EP), jnp.int32).at[:, labels].set(labels[beside])


def shard_levels(stream_key, dims, pieces, low, high):
    def one(position, blocks):
        draws = jax.random.uniform(jax.random.fold_in(jax.random.fold_in(stream_key, 6), position), (blocks,), jnp.float32, low / len(pieces), high / len(pieces))
        return jnp.repeat(jnp.exp(draws), dims[position] // blocks).reshape((-1,) + (1,) * (len(dims) - position - 1))

    level = one(*pieces[0])
    for cut in pieces[1:]:
        level = level * one(*cut)
    return level


def centred(own_key, extent, width, reach, shards=(), held_as=jnp.bfloat16):
    gain = shard_levels(own_key, extent, shards, -0.22, 0.18) if shards else 1.0
    values = jax.random.normal(own_key, extent, jnp.float32) * width * gain
    return jnp.minimum(jnp.maximum(values, -reach), reach).astype(held_as)


def setup_inputs(seed: int = 0) -> dict:
    splits = jax.random.split(jax.random.key(seed), 5)
    return {
        "starts": centred(splits[0], (SLICES, VALUES, NX, EP), 1.0, 6.0, ((0, 4), (2, 64)), jnp.float32),
        "volume_op": draw_volume_op(jax.random.fold_in(splits[4], 71), 0),
        "face_ops": centred(splits[2], (6, VALUES, VALUES), 0.04, 0.24, (), jnp.float32),
        "neighbours": draw_neighbours(jax.random.fold_in(splits[4], 71), 0),
    }


slice_length = 0.25
highest = lax.Precision.HIGHEST

def lagrange_integral(points, which, lower, upper):
    coefficients = [1.0]
    divisor = 1.0
    for other in range(4):
        if other != which:
            product = [0.0] * (len(coefficients) + 1)
            for power in range(len(coefficients)):
                product[power + 1] = product[power + 1] + coefficients[power]
                product[power] = product[power] - coefficients[power] * points[other]
            coefficients = product
            divisor = divisor * (points[which] - points[other])
    integral = 0.0
    for power in range(len(coefficients)):
        integral = integral + coefficients[power] * (upper ** (power + 1) - lower ** (power + 1)) / (power + 1)
    return integral / divisor

def sdc_tables():
    offset = 0.5 / math.sqrt(5.0)
    points = [0.0, 0.5 - offset, 0.5 + offset, 1.0]
    widths = [slice_length * (points[m + 1] - points[m]) for m in range(3)]
    weights = []
    for m in range(3):
        entries = []
        for j in range(4):
            entries.append(float(slice_length * lagrange_integral(points, j, points[m], points[m + 1])))
        weights.append(entries)
    return (widths, weights)

def apply_one(field, volume_op, face_ops, neighbours):
    padded = jnp.pad(field, ((0, 0), (1, 1), (0, 0)))
    result = jnp.einsum('ij,jxp->ixp', volume_op, field, precision=highest)
    result = result + jnp.einsum('ij,jxp->ixp', face_ops[0], padded[:, :-2], precision=highest)
    result = result + jnp.einsum('ij,jxp->ixp', face_ops[1], padded[:, 2:], precision=highest)
    for side in range(4):
        across = jnp.take(field, neighbours[side], axis=2)
        result = result + jnp.einsum('ij,jxp->ixp', face_ops[side + 2], across, precision=highest)
    return result

def sweep(start, old, slope, widths, weights):
    fresh = [old[0]]
    value = start
    values = [start]
    for m in range(3):
        if m > 0:
            fresh.append(slope(value))
        integral = weights[m][0] * old[0]
        for j in range(1, 4):
            integral = integral + weights[m][j] * old[j]
        value = value + widths[m] * (fresh[m] - old[m]) + integral
        values.append(value)
    return (values, fresh)

def reference(starts, volume_op, face_ops, neighbours):
    widths, weights = sdc_tables()

    def slope(states):
        return lax.map(lambda field: apply_one(field, volume_op, face_ops, neighbours), states)
    current = starts
    nodes = [starts, starts, starts, starts]
    ends = starts
    for turn in range(ITERS):
        stacked = slope(jnp.concatenate(nodes, axis=0))
        old = [stacked[m * SLICES:(m + 1) * SLICES] for m in range(4)]
        first_values, first_slopes = sweep(current, old, slope, widths, weights)
        second = first_slopes + [slope(first_values[3])]
        second_values, second_slopes = sweep(current, second, slope, widths, weights)
        ends = second_values[3]
        correction = ends - (current + slice_length * old[0])
        chained = [starts[0]]
        for index in range(SLICES - 1):
            value = chained[-1]
            chained.append(value + slice_length * apply_one(value, volume_op, face_ops, neighbours) + correction[index])
        updated = jnp.stack(chained)
        change = updated - current
        nodes = [updated] + [second_values[m] + change for m in range(1, 4)]
        current = updated
    return (current, ends)
```

```python
import functools
import math

import jax
import jax.numpy as jnp
import numpy as np
from jax import lax
from jax.experimental import pallas as pl
from jax.experimental.pallas import tpu as pltpu
from jax.sharding import Mesh
from jax.sharding import PartitionSpec as P

PY, PZ = 8, 16
COLS = PY * PZ
UNITS = 64
SLICES = 8
OWN = 64
HALO = 20
WIN = OWN + 2 * HALO
PAD = 2
LAYERS = WIN + 2 * PAD
BASE = PAD + HALO
CHAIN1 = 16
CHAIN2 = 8
TAU = 0.25
highest = lax.Precision.HIGHEST
f32, bf16 = jnp.float32, jnp.bfloat16


def lagrange_integral(points, which, lower, upper):
    coefficients = [1.0]
    divisor = 1.0
    for other in range(4):
        if other != which:
            product = [0.0] * (len(coefficients) + 1)
            for power in range(len(coefficients)):
                product[power + 1] = product[power + 1] + coefficients[power]
                product[power] = product[power] - coefficients[power] * points[other]
            coefficients = product
            divisor = divisor * (points[which] - points[other])
    integral = 0.0
    for power in range(len(coefficients)):
        integral = integral + coefficients[power] * (
            upper ** (power + 1) - lower ** (power + 1)
        ) / (power + 1)
    return integral / divisor


def sdc_tables():
    offset = 0.5 / math.sqrt(5.0)
    points = [0.0, 0.5 - offset, 0.5 + offset, 1.0]
    widths = [TAU * (points[m + 1] - points[m]) for m in range(3)]
    weights = [
        [float(TAU * lagrange_integral(points, j, points[m], points[m + 1])) for j in range(4)]
        for m in range(3)
    ]
    return widths, weights


def modes():
    pairs = [(ka, kb) for kb in range(1, PZ // 2) for ka in range(PY)]
    pairs += [(ka, kb) for kb in (0, PZ // 2) for ka in range(1, PY // 2)]
    single = [((0, 0), (PY // 2, 0)), ((0, PZ // 2), (PY // 2, PZ // 2))]
    places = np.arange(COLS)
    a, b = places // PZ, places % PZ

    def angle(k):
        return 2.0 * np.pi * (((k[0] * a * (PZ // PY) + k[1] * b) % PZ) / PZ)

    def turn(k):
        return 2.0 * np.pi * k[0] / PY, 2.0 * np.pi * k[1] / PZ

    basis = np.zeros((2 * UNITS, COLS))
    table = np.zeros((UNITS, 8))
    for u, k in enumerate(pairs):
        scale = math.sqrt(2.0 / COLS)
        basis[u] = scale * np.cos(angle(k))
        basis[UNITS + u] = scale * np.sin(angle(k))
        al, be = turn(k)
        table[u, :6] = [np.cos(al), np.cos(be), np.cos(al), np.cos(be), np.sin(al), np.sin(be)]
    for i, (k, other) in enumerate(single):
        u = len(pairs) + i
        scale = math.sqrt(1.0 / COLS)
        basis[u] = scale * np.cos(angle(k))
        basis[UNITS + u] = scale * np.cos(angle(other))
        al, be = turn(k)
        al2, be2 = turn(other)
        table[u, :6] = [np.cos(al), np.cos(be), np.cos(al2), np.cos(be2), 0.0, 0.0]
    return basis.astype(np.float32), table.astype(np.float32)


def look_up(table, index):
    return jnp.take_along_axis(table, index, axis=1)


def forward_kernel(x_ref, nb_ref, basis_ref, out_ref, dt_ref):
    along_a = jnp.broadcast_to(nb_ref[1:2, :], (8, COLS))
    along_b = jnp.broadcast_to(nb_ref[3:4, :], (8, COLS))
    place = lax.broadcasted_iota(jnp.int32, (8, COLS), 1)
    column = jnp.zeros((8, COLS), jnp.int32)
    for bit in range(4):
        column = jnp.where((place >> bit) & 1 == 1, look_up(along_b, column), column)
        if bit < 3:
            along_b = look_up(along_b, along_b)
    for bit in range(3):
        column = jnp.where((place >> (4 + bit)) & 1 == 1, look_up(along_a, column), column)
        if bit < 2:
            along_a = look_up(along_a, along_a)
    row = lax.broadcasted_iota(jnp.int32, (COLS, COLS), 0)
    one_hot = jnp.where(jnp.broadcast_to(column[0:1, :], (COLS, COLS)) == row, 1.0, 0.0)
    dt = lax.dot_general(
        basis_ref[...], one_hot, (((1,), (1,)), ((), ())),
        precision=highest, preferred_element_type=f32,
    )
    dt_ref[...] = dt
    parts = []
    for l in range(4):
        for s in range(2):
            parts.append(x_ref[s, pl.ds(l, 64, stride=4), :])
    stacked = jnp.concatenate(parts, axis=0)
    result = lax.dot_general(
        dt, stacked, (((1,), (1,)), ((), ())),
        precision=highest, preferred_element_type=f32,
    )
    low = lax.broadcasted_iota(jnp.int32, (UNITS, COLS), 1) < 64
    for k in range(4):
        even = result[:UNITS, k * 128:(k + 1) * 128]
        odd = result[UNITS:, k * 128:(k + 1) * 128]
        out_ref[:, 2 * k, :] = jnp.where(low, even, pltpu.roll(odd, 64, 1))
        out_ref[:, 2 * k + 1, :] = jnp.where(low, pltpu.roll(even, 64, 1), odd)


def backward_kernel(z_ref, dt_ref, new_ref, end_ref):
    dt = dt_ref[...]
    zero = jnp.zeros((UNITS, COLS), f32)
    top, bottom = dt[:UNITS], dt[UNITS:]
    weight = jnp.concatenate(
        [
            jnp.concatenate([top, zero], axis=1),
            jnp.concatenate([zero, top], axis=1),
            jnp.concatenate([bottom, zero], axis=1),
            jnp.concatenate([zero, bottom], axis=1),
        ],
        axis=0,
    )
    rows = []
    for pair in range(8):
        block = jnp.concatenate([z_ref[:, 2 * pair, :], z_ref[:, 2 * pair + 1, :]], axis=0)
        turned = block.T
        rows.append(jnp.concatenate([turned[:64], turned[64:]], axis=1))
    result = jnp.dot(
        jnp.concatenate(rows, axis=0), weight, precision=highest, preferred_element_type=f32
    )
    for pair in range(8):
        ref = new_ref if pair < 4 else end_ref
        l = pair % 4
        for s in range(2):
            ref[s, pl.ds(l, 64, stride=4), :] = result[
                pair * 64:(pair + 1) * 64, s * 128:(s + 1) * 128
            ]


def split(x):
    high = x.astype(bf16)
    low = (x - high.astype(f32)).astype(bf16)
    return high, low


def chunks(first, last, most=34):
    count = last - first
    pieces = -(-count // most)
    size = -(-count // pieces)
    size += size % 2
    out = []
    at = first
    while at < last:
        n = min(size, last - at)
        out.append((at, n))
        at += n
    return out


def middle_kernel(r_ref, lo_ref, hi_ref, vol_ref, face_ref, par_ref, flag_ref, out_ref,
                  w_ref, mask_ref, *bufs):
    widths, S = sdc_tables()
    h0, h1, h2 = widths
    first = flag_ref[0, 0] == 1
    last = flag_ref[0, 1] == 1

    fa, fb = face_ref[2] + face_ref[3], face_ref[4] + face_ref[5]
    ga, gb = face_ref[3] - face_ref[2], face_ref[5] - face_ref[4]
    vol = vol_ref[...]
    mcc = vol + par_ref[0, 0] * fa + par_ref[0, 1] * fb
    mss = vol + par_ref[0, 2] * fa + par_ref[0, 3] * fb
    mcs = par_ref[0, 4] * ga + par_ref[0, 5] * gb
    zero = jnp.zeros((64, 64), f32)

    def block(a, b, c, d):
        return jnp.concatenate(
            [jnp.concatenate([a, b], axis=1), jnp.concatenate([c, d], axis=1)], axis=0
        )

    w = jnp.concatenate(
        [
            block(mcc, mcs, -mcs, mss).T,
            block(face_ref[0], zero, zero, face_ref[0]).T,
            block(face_ref[1], zero, zero, face_ref[1]).T,
        ],
        axis=1,
    )
    w_high, w_low = split(w)
    w_ref[0:128, :] = w_high
    w_ref[128:256, :] = w_high
    w_ref[256:384, :] = w_low

    low_edge = jnp.where(first, BASE, 0)
    high_edge = jnp.where(last, BASE + OWN, LAYERS)
    layer = lax.broadcasted_iota(jnp.int32, (LAYERS * 8, 128), 0) // 8
    mask_ref[...] = jnp.where((layer >= low_edge) & (layer < high_edge), 1.0, 0.0)

    for buf in bufs:
        buf[...] = jnp.zeros_like(buf)
    s_, f_, w1_, w2_, w3_, g1_, g2_, p1_, p2_, v_, v2_, d1_, d2_, b_, r_, lr_ = bufs

    for t in range(4):
        for l in range(4):
            for ref, count, at in (
                (lo_ref, HALO // 4, PAD),
                (r_ref, OWN // 4, BASE),
                (hi_ref, HALO // 4, BASE + OWN),
            ):
                for q in range(count):
                    row = (at + 4 * q + l) * 8 + 2 * t
                    s_[row:row + 2, :] = ref[t, q, 2 * l:2 * l + 2, :]

    def product(x):
        high, low = split(x)
        return jnp.dot(
            jnp.concatenate([high, low, high], axis=1), w_ref[...], preferred_element_type=f32
        )

    def batched(src, reach, then):
        for at, n in chunks(BASE - reach, BASE + OWN + reach):
            acc = product(src[(at - 1) * 8:(at + n + 1) * 8, :])
            here = slice(at * 8, (at + n) * 8)
            y = acc[8:-8, :128] + acc[:-16, 128:256] + acc[16:, 256:]
            then(here, y * mask_ref[here, :])

    def one(i, y):
        f_[i, :] = y
        w1_[i, :] = s_[i, :] + h0 * y

    def two(i, y):
        g1_[i, :] = y
        w2_[i, :] = w1_[i, :] + h1 * y

    def three(i, y):
        g2_[i, :] = y
        w3_[i, :] = w2_[i, :] + h2 * y

    def make_four(start, zeroth):
        def four(i, y):
            g0, g1, g2 = zeroth[i, :], g1_[i, :], g2_[i, :]
            v_[i, :] = start[i, :] + (S[0][0] * g0 + S[0][1] * g1 + S[0][2] * g2 + S[0][3] * y)
            p1_[i, :] = S[1][0] * g0 + (S[1][1] - h1) * g1 + S[1][2] * g2 + S[1][3] * y
            p2_[i, :] = S[2][0] * g0 + S[2][1] * g1 + (S[2][2] - h2) * g2 + S[2][3] * y

        return four

    def five(i, y):
        d1_[i, :] = y - f_[i, :]
        v2_[i, :] = v_[i, :] + (h1 * y + p1_[i, :])

    def six(i, y):
        d2_[i, :] = y - f_[i, :]
        v3 = v2_[i, :] + (h2 * y + p2_[i, :])
        v_[i, :] = v3
        b_[i, :] = v3 - (s_[i, :] + TAU * f_[i, :])

    def seven(i, y):
        d1, d2, d3 = d1_[i, :], d2_[i, :], y - f_[i, :]
        w1_[i, :] = S[0][1] * d1 + S[0][2] * d2 + S[0][3] * d3
        p1_[i, :] = (S[1][1] - h1) * d1 + S[1][2] * d2 + S[1][3] * d3
        p2_[i, :] = S[2][1] * d1 + (S[2][2] - h2) * d2 + S[2][3] * d3

    batched(s_, 18, one)
    batched(w1_, 17, two)
    batched(w2_, 16, three)
    batched(w3_, 15, make_four(s_, f_))
    batched(v_, 14, five)
    batched(v2_, 13, six)
    batched(v_, 12, seven)

    def chain(reach, steps, addend, store):
        runs = (OWN + 2 * reach) // 8
        base = (BASE - reach) * 8

        def rows(q, n):
            return pl.ds(base + q * 8 + n, 8, stride=runs * 8)

        def take(ref, n):
            return jnp.concatenate([ref[rows(q, n), :] for q in range(runs)], axis=0)

        mask = take(mask_ref, 0)
        value = take(s_, 0)
        for n in range(steps):
            acc = product(value)
            below, above = acc[:, 128:256], acc[:, 256:]
            below = jnp.concatenate([pltpu.roll(below[-8:], 1, 0), below[:-8]], axis=0)
            above = jnp.concatenate([above[8:], pltpu.roll(above[:8], 7, 0)], axis=0)
            y = (acc[:, :128] + below + above) * mask
            for q in range(runs):
                store(rows(q, n), value[q * 8:(q + 1) * 8], y[q * 8:(q + 1) * 8])
            if n < 7:
                value = value + TAU * y + take(addend, n)
        return value, rows, runs

    def keep_first(i, value, y):
        r_[i, :] = value
        lr_[i, :] = y
        w3_[i, :] = value + h0 * y + w1_[i, :]

    chain(CHAIN1, 8, b_, keep_first)

    def eight(i, y):
        g1_[i, :] = y
        w2_[i, :] = w3_[i, :] + (h1 * y + p1_[i, :])

    def nine(i, y):
        g2_[i, :] = y
        w1_[i, :] = w2_[i, :] + (h2 * y + p2_[i, :])

    def eleven(i, y):
        v2_[i, :] = v_[i, :] + (h1 * y + p1_[i, :])

    def twelve(i, y):
        v3 = v2_[i, :] + (h2 * y + p2_[i, :])
        v_[i, :] = v3
        b_[i, :] = v3 - (r_[i, :] + TAU * lr_[i, :])

    batched(w3_, 11, eight)
    batched(w2_, 10, nine)
    batched(w1_, 9, make_four(r_, lr_))
    batched(v_, 8, eleven)
    batched(v2_, 8, twelve)

    def keep_second(i, value, y):
        f_[i, :] = value

    value, rows, runs = chain(CHAIN2, 7, b_, keep_second)
    for q in range(runs):
        f_[rows(q, 7), :] = value[q * 8:(q + 1) * 8]

    for o, ref in enumerate((f_, v_)):
        for t in range(4):
            for l in range(4):
                for q in range(OWN // 4):
                    row = (BASE + 4 * q + l) * 8 + 2 * t
                    out_ref[t, q, o * 8 + 2 * l:o * 8 + 2 * l + 2, :] = ref[row:row + 2, :]


def vmem():
    return pl.BlockSpec(memory_space=pltpu.VMEM)


def smem():
    return pl.BlockSpec(memory_space=pltpu.SMEM)


def shards(basis, table, starts, volume_op, face_ops, neighbours):
    y = lax.axis_index("y")
    unit = lax.axis_index("tm") * 16 + lax.axis_index("zx")
    params = lax.dynamic_slice(jnp.asarray(table), (unit, 0), (1, 8))
    flags = jnp.stack([y == 0, y == lax.axis_size("y") - 1]).astype(jnp.int32).reshape(1, 2)

    sent, dt = pl.pallas_call(
        forward_kernel,
        out_shape=(
            jax.ShapeDtypeStruct((UNITS, 8, 128), f32),
            jax.ShapeDtypeStruct((COLS, COLS), f32),
        ),
        in_specs=[vmem()] * 3,
        out_specs=(vmem(), vmem()),
        name="forward",
    )(starts.reshape(2, 256, 128), neighbours, jnp.asarray(basis))
    got = lax.all_to_all(sent, ("tm", "zx"), 0, 0, tiled=True).reshape(4, 16, 8, 128)
    count = HALO // 4
    up = [(i, i + 1) for i in range(3)]
    down = [(i + 1, i) for i in range(3)]
    below = lax.ppermute(got[:, 16 - count:], "y", up)
    above = lax.ppermute(got[:, :count], "y", down)
    back = pl.pallas_call(
        middle_kernel,
        out_shape=jax.ShapeDtypeStruct((4, 16, 16, 128), f32),
        in_specs=[vmem()] * 5 + [smem()] * 2,
        out_specs=vmem(),
        scratch_shapes=[
            pltpu.VMEM((384, 384), bf16),
            pltpu.VMEM((LAYERS * 8, 128), f32),
        ] + [pltpu.VMEM((LAYERS * 8, 128), f32)] * 16,
        compiler_params=pltpu.CompilerParams(vmem_limit_bytes=32 * 1024 * 1024),
        name="sweeps",
    )(got, below, above, volume_op, face_ops, params, flags)
    home = lax.all_to_all(back.reshape(UNITS, 16, 128), ("tm", "zx"), 0, 0, tiled=True)
    new, end = pl.pallas_call(
        backward_kernel,
        out_shape=(jax.ShapeDtypeStruct((2, 256, 128), f32),) * 2,
        in_specs=[vmem()] * 2,
        out_specs=(vmem(), vmem()),
        name="backward",
    )(home, dt)
    return new.reshape(2, 64, 4, 128), end.reshape(2, 64, 4, 128)


def solution(mesh):
    finer = Mesh(mesh.devices.reshape(4, 4, 16), ("tm", "y", "zx"))
    basis, table = modes()
    placed = P("tm", None, ("y", "zx"), None)
    return jax.shard_map(
        functools.partial(shards, basis, table),
        mesh=finer,
        in_specs=(placed, P(), P(), P()),
        out_specs=(placed, placed),
        check_vma=False,
    )
```

```python
import functools
import math

import jax
import jax.numpy as jnp
import ml_dtypes
import numpy as np
from jax import lax
from jax.experimental import pallas as pl
from jax.experimental.pallas import tpu as pltpu
from jax.sharding import Mesh
from jax.sharding import PartitionSpec as P

PY, PZ = 8, 16
COLS = PY * PZ
UNITS = 64
SLICES = 8
OWN = 64
HALO = 20
WIN = OWN + 2 * HALO
PAD = 2
LAYERS = WIN + 2 * PAD
BASE = PAD + HALO
CHAIN1 = 16
CHAIN2 = 8
TAU = 0.25
f32, bf16 = jnp.float32, jnp.bfloat16


def lagrange_integral(points, which, lower, upper):
    coefficients = [1.0]
    divisor = 1.0
    for other in range(4):
        if other != which:
            product = [0.0] * (len(coefficients) + 1)
            for power in range(len(coefficients)):
                product[power + 1] = product[power + 1] + coefficients[power]
                product[power] = product[power] - coefficients[power] * points[other]
            coefficients = product
            divisor = divisor * (points[which] - points[other])
    integral = 0.0
    for power in range(len(coefficients)):
        integral = integral + coefficients[power] * (
            upper ** (power + 1) - lower ** (power + 1)
        ) / (power + 1)
    return integral / divisor


def sdc_tables():
    offset = 0.5 / math.sqrt(5.0)
    points = [0.0, 0.5 - offset, 0.5 + offset, 1.0]
    widths = [TAU * (points[m + 1] - points[m]) for m in range(3)]
    weights = [
        [float(TAU * lagrange_integral(points, j, points[m], points[m + 1])) for j in range(4)]
        for m in range(3)
    ]
    return widths, weights


def modes():
    pairs = [(ka, kb) for kb in range(1, PZ // 2) for ka in range(PY)]
    pairs += [(ka, kb) for kb in (0, PZ // 2) for ka in range(1, PY // 2)]
    single = [((0, 0), (PY // 2, 0)), ((0, PZ // 2), (PY // 2, PZ // 2))]
    places = np.arange(COLS)
    a, b = places // PZ, places % PZ

    def angle(k):
        return 2.0 * np.pi * (((k[0] * a * (PZ // PY) + k[1] * b) % PZ) / PZ)

    def turn(k):
        return 2.0 * np.pi * k[0] / PY, 2.0 * np.pi * k[1] / PZ

    basis = np.zeros((2 * UNITS, COLS))
    table = np.zeros((UNITS, 8))
    for u, k in enumerate(pairs):
        scale = math.sqrt(2.0 / COLS)
        basis[u] = scale * np.cos(angle(k))
        basis[UNITS + u] = scale * np.sin(angle(k))
        al, be = turn(k)
        table[u, :6] = [np.cos(al), np.cos(be), np.cos(al), np.cos(be), np.sin(al), np.sin(be)]
    for i, (k, other) in enumerate(single):
        u = len(pairs) + i
        scale = math.sqrt(1.0 / COLS)
        basis[u] = scale * np.cos(angle(k))
        basis[UNITS + u] = scale * np.cos(angle(other))
        al, be = turn(k)
        al2, be2 = turn(other)
        table[u, :6] = [np.cos(al), np.cos(be), np.cos(al2), np.cos(be2), 0.0, 0.0]
    basis = basis.astype(np.float32)
    high = basis.astype(ml_dtypes.bfloat16)
    low = (basis - high.astype(np.float32)).astype(ml_dtypes.bfloat16)
    return np.concatenate([high, low], axis=0), table.astype(np.float32)


def look_up(table, index):
    return jnp.take_along_axis(table, index, axis=1)


def split(x):
    high = x.astype(bf16)
    low = (x - high.astype(f32)).astype(bf16)
    return high, low


def forward_kernel(x_hbm, nb_hbm, basis_hbm, out_ref, dt_ref, x_ref, nb_ref, basis_ref, sems):
    copies = [
        pltpu.make_async_copy(src, dst, sems.at[i])
        for i, (src, dst) in enumerate(
            ((nb_hbm, nb_ref), (basis_hbm, basis_ref), (x_hbm, x_ref))
        )
    ]
    for copy in copies:
        copy.start()
    copies[0].wait()
    along_a = jnp.broadcast_to(nb_ref[1:2, :], (8, COLS))
    along_b = jnp.broadcast_to(nb_ref[3:4, :], (8, COLS))
    place = lax.broadcasted_iota(jnp.int32, (8, COLS), 1)
    column = jnp.zeros((8, COLS), jnp.int32)
    for bit in range(4):
        column = jnp.where((place >> bit) & 1 == 1, look_up(along_b, column), column)
        if bit < 3:
            along_b = look_up(along_b, along_b)
    for bit in range(3):
        column = jnp.where((place >> (4 + bit)) & 1 == 1, look_up(along_a, column), column)
        if bit < 2:
            along_a = look_up(along_a, along_a)
    row = lax.broadcasted_iota(jnp.int32, (COLS, COLS), 0)
    hit = jnp.broadcast_to(column[0:1, :], (COLS, COLS)) == row
    one_hot = jnp.where(hit, 1.0, 0.0).astype(bf16)
    copies[1].wait()
    dt = lax.dot_general(
        basis_ref[...], one_hot, (((1,), (1,)), ((), ())), preferred_element_type=f32
    ).astype(bf16)
    dt_ref[...] = dt
    copies[2].wait()
    parts = []
    for l in range(4):
        for s in range(2):
            parts.append(x_ref[s, pl.ds(l, 64, stride=4), :])
    high, low = split(jnp.concatenate(parts, axis=0))
    result = lax.dot_general(
        jnp.concatenate([dt[:128], dt[:128], dt[128:]], axis=1),
        jnp.concatenate([high, low, high], axis=1),
        (((1,), (1,)), ((), ())), preferred_element_type=f32,
    )
    left = lax.broadcasted_iota(jnp.int32, (UNITS, COLS), 1) < 64
    for k in range(4):
        even = result[:UNITS, k * 128:(k + 1) * 128]
        odd = result[UNITS:, k * 128:(k + 1) * 128]
        out_ref[:, 2 * k, :] = jnp.where(left, even, pltpu.roll(odd, 64, 1))
        out_ref[:, 2 * k + 1, :] = jnp.where(left, pltpu.roll(even, 64, 1), odd)


def backward_kernel(z_ref, dt_ref, new_hbm, end_hbm, new_ref, end_ref, sems):
    zero = jnp.zeros((UNITS, COLS), bf16)

    def weight(dt):
        top, bottom = dt[:UNITS], dt[UNITS:]
        return jnp.concatenate(
            [
                jnp.concatenate([top, zero], axis=1),
                jnp.concatenate([zero, top], axis=1),
                jnp.concatenate([bottom, zero], axis=1),
                jnp.concatenate([zero, bottom], axis=1),
            ],
            axis=0,
        )

    high_dt, low_dt = weight(dt_ref[0:128, :]), weight(dt_ref[128:256, :])
    weights = jnp.concatenate([high_dt, high_dt, low_dt], axis=0)
    copies = []
    for o, (ref, hbm) in enumerate(((new_ref, new_hbm), (end_ref, end_hbm))):
        rows = []
        for l in range(4):
            pair = 4 * o + l
            block = jnp.concatenate([z_ref[:, 2 * pair, :], z_ref[:, 2 * pair + 1, :]], axis=0)
            turned = block.T
            rows.append(jnp.concatenate([turned[:64], turned[64:]], axis=1))
        high, low = split(jnp.concatenate(rows, axis=0))
        result = jnp.dot(
            jnp.concatenate([high, low, high], axis=1), weights, preferred_element_type=f32
        )
        for l in range(4):
            for s in range(2):
                ref[s, pl.ds(l, 64, stride=4), :] = result[
                    l * 64:(l + 1) * 64, s * 128:(s + 1) * 128
                ]
        copies.append(pltpu.make_async_copy(ref, hbm, sems.at[o]))
        copies[-1].start()
    for copy in copies:
        copy.wait()


def chunks(first, last, most=34):
    count = last - first
    pieces = -(-count // most)
    size = -(-count // pieces)
    size += size % 2
    out = []
    at = first
    while at < last:
        n = min(size, last - at)
        out.append((at, n))
        at += n
    return out


def prepare_kernel(vol_ref, face_ref, table_ref, place_ref, wa_ref, wb_ref, mask_ref):
    unit = place_ref[0, 0]
    y = place_ref[0, 1]
    fa, fb = face_ref[2] + face_ref[3], face_ref[4] + face_ref[5]
    ga, gb = face_ref[3] - face_ref[2], face_ref[5] - face_ref[4]
    vol = vol_ref[...]
    mcc = vol + table_ref[unit, 0] * fa + table_ref[unit, 1] * fb
    mss = vol + table_ref[unit, 2] * fa + table_ref[unit, 3] * fb
    mcs = table_ref[unit, 4] * ga + table_ref[unit, 5] * gb
    zero = jnp.zeros((64, 64), f32)

    def block(a, b, c, d):
        return jnp.concatenate(
            [jnp.concatenate([a, b], axis=1), jnp.concatenate([c, d], axis=1)], axis=0
        ).T

    m_high, m_low = split(block(mcc, mcs, -mcs, mss))
    f0_high, f0_low = split(block(face_ref[0], zero, zero, face_ref[0]))
    f1_high, f1_low = split(block(face_ref[1], zero, zero, face_ref[1]))
    both = jnp.concatenate([f1_high, m_high], axis=1)
    wa_ref[0:128, :] = both
    wa_ref[128:256, :] = both
    wa_ref[256:384, :] = jnp.concatenate([f1_low, m_low], axis=1)
    wb_ref[0:128, :] = jnp.concatenate([f0_high, f0_low], axis=1)
    wb_ref[128:256, :] = jnp.concatenate([f0_high, jnp.zeros_like(f0_low)], axis=1)

    low_edge = jnp.where(y == 0, BASE, 0)
    high_edge = jnp.where(y == 3, BASE + OWN, LAYERS)
    layer = lax.broadcasted_iota(jnp.int32, (LAYERS * 8, 128), 0) // 8
    mask_ref[...] = jnp.where((layer >= low_edge) & (layer < high_edge), 1.0, 0.0)


def middle_kernel(r_ref, lo_ref, hi_ref, wa_ref, wb_ref, mask_ref, out_ref, *bufs):
    widths, S = sdc_tables()
    h0, h1, h2 = widths

    for buf in bufs:
        buf[...] = jnp.zeros_like(buf)
    s_, f_, w1_, w2_, w3_, g1_, g2_, p1_, p2_, v_, v2_, d1_, d2_, b_, r_, lr_ = bufs

    for t in range(4):
        for l in range(4):
            for ref, count, at in (
                (lo_ref, HALO // 4, PAD),
                (r_ref, OWN // 4, BASE),
                (hi_ref, HALO // 4, BASE + OWN),
            ):
                for q in range(count):
                    row = (at + 4 * q + l) * 8 + 2 * t
                    s_[row:row + 2, :] = ref[t, q, 2 * l:2 * l + 2, :]

    def product(x):
        high, low = split(x)
        acc = jnp.dot(
            jnp.concatenate([high, low, high], axis=1), wa_ref[...], preferred_element_type=f32
        )
        up = jnp.dot(
            jnp.concatenate([high, low], axis=1), wb_ref[...], preferred_element_type=f32
        )
        return acc[:, 128:], up[:, :128] + up[:, 128:], acc[:, :128]

    def one_chunk(src, then, at, n):
        own, up, down = product(src(slice((at - 1) * 8, (at + n + 1) * 8)))
        here = slice(at * 8, (at + n) * 8)
        y = own[8:-8] + up[:-16] + down[16:]
        then(here, y * mask_ref[here, :])

    def batched(src, reach, then):
        for at, n in chunks(BASE - reach, BASE + OWN + reach):
            one_chunk(lambda i: src[i, :], then, at, n)

    def one(i, y):
        f_[i, :] = y
        w1_[i, :] = s_[i, :] + h0 * y

    def two(i, y):
        g1_[i, :] = y
        w2_[i, :] = w1_[i, :] + h1 * y

    def three(i, y):
        g2_[i, :] = y
        w3_[i, :] = w2_[i, :] + h2 * y

    def make_four(start, zeroth):
        def four(i, y):
            g0, g1, g2 = zeroth[i, :], g1_[i, :], g2_[i, :]
            v_[i, :] = start[i, :] + (S[0][0] * g0 + S[0][1] * g1 + S[0][2] * g2 + S[0][3] * y)
            p1_[i, :] = S[1][0] * g0 + (S[1][1] - h1) * g1 + S[1][2] * g2 + S[1][3] * y
            p2_[i, :] = S[2][0] * g0 + S[2][1] * g1 + (S[2][2] - h2) * g2 + S[2][3] * y

        return four

    def five(i, y):
        d1_[i, :] = y - f_[i, :]
        v2_[i, :] = v_[i, :] + (h1 * y + p1_[i, :])

    def six(i, y):
        d2_[i, :] = y - f_[i, :]
        v3 = v2_[i, :] + (h2 * y + p2_[i, :])
        v_[i, :] = v3
        b_[i, :] = v3 - (s_[i, :] + TAU * f_[i, :])

    def seven(i, y):
        d1, d2, d3 = d1_[i, :], d2_[i, :], y - f_[i, :]
        w1_[i, :] = S[0][1] * d1 + S[0][2] * d2 + S[0][3] * d3
        p1_[i, :] = (S[1][1] - h1) * d1 + S[1][2] * d2 + S[1][3] * d3
        p2_[i, :] = S[2][1] * d1 + (S[2][2] - h2) * d2 + S[2][3] * d3

    batched(s_, 18, one)
    batched(w1_, 17, two)
    batched(w2_, 16, three)
    batched(w3_, 15, make_four(s_, f_))
    batched(v_, 14, five)
    batched(v2_, 13, six)
    pieces = chunks(BASE - 12, BASE + OWN + 12, 12)

    def last_of_one(n):
        for at, count in pieces[n:n + 1]:
            one_chunk(lambda i: v_[i, :], seven, at, count)

    def chain(reach, steps, addend, store, beside):
        runs = (OWN + 2 * reach) // 8
        base = (BASE - reach) * 8

        def rows(q, n):
            return pl.ds(base + q * 8 + n, 8, stride=runs * 8)

        def take(ref, n):
            return jnp.concatenate([ref[rows(q, n), :] for q in range(runs)], axis=0)

        mask = take(mask_ref, 0)
        value = take(s_, 0)
        for n in range(steps):
            beside(n)
            own, up, down = product(value)
            up = jnp.concatenate([pltpu.roll(up[-8:], 1, 0), up[:-8]], axis=0)
            down = jnp.concatenate([down[8:], pltpu.roll(down[:8], 7, 0)], axis=0)
            y = (own + up + down) * mask
            for q in range(runs):
                store(rows(q, n), value[q * 8:(q + 1) * 8], y[q * 8:(q + 1) * 8])
            if n < 7:
                value = value + TAU * y + take(addend, n)
        return value, rows, runs

    def keep_first(i, value, y):
        r_[i, :] = value
        lr_[i, :] = y

    chain(CHAIN1, 8, b_, keep_first, last_of_one)

    def eight(i, y):
        g1_[i, :] = y
        w2_[i, :] = w3_[i, :] + (h1 * y + p1_[i, :])

    def nine(i, y):
        g2_[i, :] = y
        w1_[i, :] = w2_[i, :] + (h2 * y + p2_[i, :])

    def eleven(i, y):
        v2_[i, :] = v_[i, :] + (h1 * y + p1_[i, :])

    def twelve(i, y):
        v3 = v2_[i, :] + (h2 * y + p2_[i, :])
        v_[i, :] = v3
        b_[i, :] = v3 - (r_[i, :] + TAU * lr_[i, :])

    for at, n in chunks(BASE - 12, BASE + OWN + 12):
        i = slice(at * 8, (at + n) * 8)
        w3_[i, :] = r_[i, :] + (h0 * lr_[i, :] + w1_[i, :])
    batched(w3_, 11, eight)
    batched(w2_, 10, nine)
    batched(w1_, 9, make_four(r_, lr_))
    batched(v_, 8, eleven)
    batched(v2_, 8, twelve)

    def keep_second(i, value, y):
        f_[i, :] = value

    def deliver(o, ref, t):
        for l in range(4):
            for q in range(OWN // 4):
                row = (BASE + 4 * q + l) * 8 + 2 * t
                out_ref[t, q, o * 8 + 2 * l:o * 8 + 2 * l + 2, :] = ref[row:row + 2, :]

    def ends(n):
        if n < 4:
            deliver(1, v_, n)

    value, rows, runs = chain(CHAIN2, 7, b_, keep_second, ends)
    for q in range(runs):
        f_[rows(q, 7), :] = value[q * 8:(q + 1) * 8]
    for t in range(4):
        deliver(0, f_, t)


def vmem():
    return pl.BlockSpec(memory_space=pltpu.VMEM)


def smem():
    return pl.BlockSpec(memory_space=pltpu.SMEM)


def anywhere():
    return pl.BlockSpec(memory_space=pl.ANY)


def grant(mib):
    return pltpu.CompilerParams(vmem_limit_bytes=mib * 1024 * 1024)


def shards(basis, table, starts, volume_op, face_ops, neighbours):
    unit = lax.axis_index("tm") * 16 + lax.axis_index("zx")
    place = jnp.stack([unit, lax.axis_index("y")]).astype(jnp.int32).reshape(1, 2)

    sent, dt = pl.pallas_call(
        forward_kernel,
        out_shape=(
            jax.ShapeDtypeStruct((UNITS, 8, 128), f32),
            jax.ShapeDtypeStruct((2 * COLS, COLS), bf16),
        ),
        in_specs=[anywhere()] * 3,
        out_specs=(vmem(), vmem()),
        scratch_shapes=[
            pltpu.VMEM((2, 256, 128), f32),
            pltpu.VMEM((4, COLS), jnp.int32),
            pltpu.VMEM((2 * COLS, COLS), bf16),
            pltpu.SemaphoreType.DMA((3,)),
        ],
        name="forward",
    )(starts.reshape(2, 256, 128), neighbours, jnp.asarray(basis))
    wa, wb, mask = pl.pallas_call(
        prepare_kernel,
        out_shape=(
            jax.ShapeDtypeStruct((384, 256), bf16),
            jax.ShapeDtypeStruct((256, 256), bf16),
            jax.ShapeDtypeStruct((LAYERS * 8, 128), f32),
        ),
        in_specs=[vmem(), vmem(), smem(), smem()],
        out_specs=(vmem(),) * 3,
        compiler_params=grant(8),
        cost_estimate=pl.CostEstimate(
            flops=2 * 10**9, bytes_accessed=4 * 10**6, transcendentals=0
        ),
        name="prepare",
    )(volume_op, face_ops, jnp.asarray(table), place)
    got = lax.all_to_all(sent, ("tm", "zx"), 0, 0, tiled=True).reshape(4, 16, 8, 128)
    got, wa, wb, mask = lax.optimization_barrier((got, wa, wb, mask))
    count = HALO // 4
    up = [(i, i + 1) for i in range(3)]
    down = [(i + 1, i) for i in range(3)]
    below = lax.ppermute(got[:, 16 - count:], "y", up)
    above = lax.ppermute(got[:, :count], "y", down)
    back = pl.pallas_call(
        middle_kernel,
        out_shape=jax.ShapeDtypeStruct((4, 16, 16, 128), f32),
        in_specs=[vmem()] * 6,
        out_specs=vmem(),
        scratch_shapes=[pltpu.VMEM((LAYERS * 8, 128), f32)] * 16,
        compiler_params=grant(16),
        name="sweeps",
    )(got, below, above, wa, wb, mask)
    home = lax.all_to_all(back.reshape(UNITS, 16, 128), ("tm", "zx"), 0, 0, tiled=True)
    new, end = pl.pallas_call(
        backward_kernel,
        out_shape=(jax.ShapeDtypeStruct((2, 256, 128), f32),) * 2,
        in_specs=[vmem()] * 2,
        out_specs=(anywhere(),) * 2,
        scratch_shapes=[
            pltpu.VMEM((2, 256, 128), f32),
            pltpu.VMEM((2, 256, 128), f32),
            pltpu.SemaphoreType.DMA((2,)),
        ],
        compiler_params=grant(8),
        name="backward",
    )(home, dt)
    return new.reshape(2, 64, 4, 128), end.reshape(2, 64, 4, 128)


def solution(mesh):
    finer = Mesh(mesh.devices.reshape(4, 4, 16), ("tm", "y", "zx"))
    basis, table = modes()
    placed = P("tm", None, ("y", "zx"), None)
    return jax.shard_map(
        functools.partial(shards, basis, table),
        mesh=finer,
        in_specs=(placed, P(), P(), P()),
        out_specs=(placed, placed),
        check_vma=False,
    )
```

```python
import functools
import math

import jax
import jax.numpy as jnp
import ml_dtypes
import numpy as np
from jax import lax
from jax.experimental import pallas as pl
from jax.experimental.pallas import tpu as pltpu
from jax.sharding import Mesh
from jax.sharding import PartitionSpec as P

PY, PZ = 8, 16
COLS = PY * PZ
UNITS = 64
SLICES = 8
OWN = 64
HALO = 20
WIN = OWN + 2 * HALO
PAD = 2
LAYERS = WIN + 2 * PAD
BASE = PAD + HALO
CHAIN1 = 16
CHAIN2 = 8
TAU = 0.25
f32, bf16 = jnp.float32, jnp.bfloat16


def lagrange_integral(points, which, lower, upper):
    coefficients = [1.0]
    divisor = 1.0
    for other in range(4):
        if other != which:
            product = [0.0] * (len(coefficients) + 1)
            for power in range(len(coefficients)):
                product[power + 1] = product[power + 1] + coefficients[power]
                product[power] = product[power] - coefficients[power] * points[other]
            coefficients = product
            divisor = divisor * (points[which] - points[other])
    integral = 0.0
    for power in range(len(coefficients)):
        integral = integral + coefficients[power] * (
            upper ** (power + 1) - lower ** (power + 1)
        ) / (power + 1)
    return integral / divisor


def sdc_tables():
    offset = 0.5 / math.sqrt(5.0)
    points = [0.0, 0.5 - offset, 0.5 + offset, 1.0]
    widths = [TAU * (points[m + 1] - points[m]) for m in range(3)]
    weights = [
        [float(TAU * lagrange_integral(points, j, points[m], points[m + 1])) for j in range(4)]
        for m in range(3)
    ]
    return widths, weights


def modes():
    pairs = [(ka, kb) for kb in range(1, PZ // 2) for ka in range(PY)]
    pairs += [(ka, kb) for kb in (0, PZ // 2) for ka in range(1, PY // 2)]
    single = [((0, 0), (PY // 2, 0)), ((0, PZ // 2), (PY // 2, PZ // 2))]
    places = np.arange(COLS)
    a, b = places // PZ, places % PZ

    def angle(k):
        return 2.0 * np.pi * (((k[0] * a * (PZ // PY) + k[1] * b) % PZ) / PZ)

    def turn(k):
        return 2.0 * np.pi * k[0] / PY, 2.0 * np.pi * k[1] / PZ

    basis = np.zeros((2 * UNITS, COLS))
    table = np.zeros((UNITS, 8))
    for u, k in enumerate(pairs):
        scale = math.sqrt(2.0 / COLS)
        basis[u] = scale * np.cos(angle(k))
        basis[UNITS + u] = scale * np.sin(angle(k))
        al, be = turn(k)
        table[u, :6] = [np.cos(al), np.cos(be), np.cos(al), np.cos(be), np.sin(al), np.sin(be)]
    for i, (k, other) in enumerate(single):
        u = len(pairs) + i
        scale = math.sqrt(1.0 / COLS)
        basis[u] = scale * np.cos(angle(k))
        basis[UNITS + u] = scale * np.cos(angle(other))
        al, be = turn(k)
        al2, be2 = turn(other)
        table[u, :6] = [np.cos(al), np.cos(be), np.cos(al2), np.cos(be2), 0.0, 0.0]
    basis = basis.astype(np.float32)
    high = basis.astype(ml_dtypes.bfloat16)
    low = (basis - high.astype(np.float32)).astype(ml_dtypes.bfloat16)
    return np.concatenate([high, low], axis=0), table.astype(np.float32)


def look_up(table, index):
    return jnp.take_along_axis(table, index, axis=1)


def split(x):
    high = x.astype(bf16)
    low = (x - high.astype(f32)).astype(bf16)
    return high, low


def forward_kernel(x_hbm, nb_hbm, basis_hbm, out_ref, dt_ref, x_ref, nb_ref, basis_ref, sems):
    copies = [
        pltpu.make_async_copy(src, dst, sems.at[i])
        for i, (src, dst) in enumerate(
            ((nb_hbm, nb_ref), (basis_hbm, basis_ref), (x_hbm, x_ref))
        )
    ]
    for copy in copies:
        copy.start()
    copies[0].wait()
    along_a = jnp.broadcast_to(nb_ref[1:2, :], (8, COLS))
    along_b = jnp.broadcast_to(nb_ref[3:4, :], (8, COLS))
    place = lax.broadcasted_iota(jnp.int32, (8, COLS), 1)
    column = jnp.zeros((8, COLS), jnp.int32)
    for bit in range(4):
        column = jnp.where((place >> bit) & 1 == 1, look_up(along_b, column), column)
        if bit < 3:
            along_b = look_up(along_b, along_b)
    for bit in range(3):
        column = jnp.where((place >> (4 + bit)) & 1 == 1, look_up(along_a, column), column)
        if bit < 2:
            along_a = look_up(along_a, along_a)
    row = lax.broadcasted_iota(jnp.int32, (COLS, COLS), 0)
    hit = jnp.broadcast_to(column[0:1, :], (COLS, COLS)) == row
    one_hot = jnp.where(hit, 1.0, 0.0).astype(bf16)
    copies[1].wait()
    dt = lax.dot_general(
        basis_ref[...], one_hot, (((1,), (1,)), ((), ())), preferred_element_type=f32
    ).astype(bf16)
    dt_ref[...] = dt
    copies[2].wait()
    parts = []
    for l in range(4):
        for s in range(2):
            parts.append(x_ref[s, pl.ds(l, 64, stride=4), :])
    high, low = split(jnp.concatenate(parts, axis=0))
    result = lax.dot_general(
        jnp.concatenate([dt[:128], dt[:128], dt[128:]], axis=1),
        jnp.concatenate([high, low, high], axis=1),
        (((1,), (1,)), ((), ())), preferred_element_type=f32,
    )
    left = lax.broadcasted_iota(jnp.int32, (UNITS, COLS), 1) < 64
    for k in range(4):
        even = result[:UNITS, k * 128:(k + 1) * 128]
        odd = result[UNITS:, k * 128:(k + 1) * 128]
        out_ref[:, 2 * k, :] = jnp.where(left, even, pltpu.roll(odd, 64, 1))
        out_ref[:, 2 * k + 1, :] = jnp.where(left, pltpu.roll(even, 64, 1), odd)


def backward_kernel(z_ref, dt_ref, new_hbm, end_hbm, new_ref, end_ref, sems):
    zero = jnp.zeros((UNITS, COLS), bf16)

    def weight(dt):
        top, bottom = dt[:UNITS], dt[UNITS:]
        return jnp.concatenate(
            [
                jnp.concatenate([top, zero], axis=1),
                jnp.concatenate([zero, top], axis=1),
                jnp.concatenate([bottom, zero], axis=1),
                jnp.concatenate([zero, bottom], axis=1),
            ],
            axis=0,
        )

    high_dt, low_dt = weight(dt_ref[0:128, :]), weight(dt_ref[128:256, :])
    weights = jnp.concatenate([high_dt, high_dt, low_dt], axis=0)
    copies = []
    for o, (ref, hbm) in enumerate(((new_ref, new_hbm), (end_ref, end_hbm))):
        rows = []
        for l in range(4):
            pair = 4 * o + l
            block = jnp.concatenate([z_ref[:, 2 * pair, :], z_ref[:, 2 * pair + 1, :]], axis=0)
            turned = block.T
            rows.append(jnp.concatenate([turned[:64], turned[64:]], axis=1))
        high, low = split(jnp.concatenate(rows, axis=0))
        result = jnp.dot(
            jnp.concatenate([high, low, high], axis=1), weights, preferred_element_type=f32
        )
        for l in range(4):
            for s in range(2):
                ref[s, pl.ds(l, 64, stride=4), :] = result[
                    l * 64:(l + 1) * 64, s * 128:(s + 1) * 128
                ]
        copies.append(pltpu.make_async_copy(ref, hbm, sems.at[o]))
        copies[-1].start()
    for copy in copies:
        copy.wait()


def chunks(first, last, most=34):
    count = last - first
    pieces = -(-count // most)
    size = -(-count // pieces)
    size += size % 2
    out = []
    at = first
    while at < last:
        n = min(size, last - at)
        out.append((at, n))
        at += n
    return out


def prepare_kernel(vol_ref, face_ref, table_ref, place_ref, wa_ref, wb_ref, mask_ref):
    unit = place_ref[0, 0]
    y = place_ref[0, 1]
    fa, fb = face_ref[2] + face_ref[3], face_ref[4] + face_ref[5]
    ga, gb = face_ref[3] - face_ref[2], face_ref[5] - face_ref[4]
    vol = vol_ref[...]
    mcc = vol + table_ref[unit, 0] * fa + table_ref[unit, 1] * fb
    mss = vol + table_ref[unit, 2] * fa + table_ref[unit, 3] * fb
    mcs = table_ref[unit, 4] * ga + table_ref[unit, 5] * gb
    zero = jnp.zeros((64, 64), f32)

    def block(a, b, c, d):
        return jnp.concatenate(
            [jnp.concatenate([a, b], axis=1), jnp.concatenate([c, d], axis=1)], axis=0
        ).T

    m_high, m_low = split(block(mcc, mcs, -mcs, mss))
    f0_high, f0_low = split(block(face_ref[0], zero, zero, face_ref[0]))
    f1_high, f1_low = split(block(face_ref[1], zero, zero, face_ref[1]))
    both = jnp.concatenate([f1_high, m_high], axis=1)
    wa_ref[0:128, :] = both
    wa_ref[128:256, :] = both
    wa_ref[256:384, :] = jnp.concatenate([f1_low, m_low], axis=1)
    wb_ref[0:128, :] = jnp.concatenate([f0_high, f0_low], axis=1)
    wb_ref[128:256, :] = jnp.concatenate([f0_high, jnp.zeros_like(f0_low)], axis=1)

    low_edge = jnp.where(y == 0, BASE, 0)
    high_edge = jnp.where(y == 3, BASE + OWN, LAYERS)
    layer = lax.broadcasted_iota(jnp.int32, (LAYERS * 8, 128), 0) // 8
    mask_ref[...] = jnp.where((layer >= low_edge) & (layer < high_edge), 1.0, 0.0)


def middle_kernel(r_ref, lo_ref, hi_ref, wa_ref, wb_ref, mask_ref, out_ref, *bufs):
    widths, S = sdc_tables()
    h0, h1, h2 = widths

    for buf in bufs:
        buf[...] = jnp.zeros_like(buf)
    s_, f_, w1_, w2_, w3_, g1_, g2_, p1_, p2_, v_, v2_, d1_, d2_, b_, r_, lr_ = bufs

    for t in range(4):
        for l in range(4):
            for ref, count, at, factor in (
                (lo_ref, HALO // 4, PAD, mask_ref[0:2, :]),
                (r_ref, OWN // 4, BASE, None),
                (hi_ref, HALO // 4, BASE + OWN, mask_ref[LAYERS * 8 - 2:, :]),
            ):
                for q in range(count):
                    row = (at + 4 * q + l) * 8 + 2 * t
                    part = ref[t, q, 2 * l:2 * l + 2, :]
                    s_[row:row + 2, :] = part if factor is None else part * factor

    def product(x):
        high, low = split(x)
        acc = jnp.dot(
            jnp.concatenate([high, low, high], axis=1), wa_ref[...], preferred_element_type=f32
        )
        up = jnp.dot(
            jnp.concatenate([high, low], axis=1), wb_ref[...], preferred_element_type=f32
        )
        return acc[:, 128:], up[:, :128] + up[:, 128:], acc[:, :128]

    def one_chunk(src, then, at, n):
        own, up, down = product(src(slice((at - 1) * 8, (at + n + 1) * 8)))
        here = slice(at * 8, (at + n) * 8)
        y = own[8:-8] + up[:-16] + down[16:]
        then(here, y * mask_ref[here, :])

    def batched(src, reach, then):
        for at, n in chunks(BASE - reach, BASE + OWN + reach):
            one_chunk(lambda i: src[i, :], then, at, n)

    def one(i, y):
        f_[i, :] = y
        w1_[i, :] = s_[i, :] + h0 * y

    def two(i, y):
        g1_[i, :] = y
        w2_[i, :] = w1_[i, :] + h1 * y

    def three(i, y):
        g2_[i, :] = y
        w3_[i, :] = w2_[i, :] + h2 * y

    def make_four(start, zeroth):
        def four(i, y):
            g0, g1, g2 = zeroth[i, :], g1_[i, :], g2_[i, :]
            v_[i, :] = start[i, :] + (S[0][0] * g0 + S[0][1] * g1 + S[0][2] * g2 + S[0][3] * y)
            p1_[i, :] = S[1][0] * g0 + (S[1][1] - h1) * g1 + S[1][2] * g2 + S[1][3] * y
            p2_[i, :] = S[2][0] * g0 + S[2][1] * g1 + (S[2][2] - h2) * g2 + S[2][3] * y

        return four

    def five(i, y):
        d1_[i, :] = y - f_[i, :]
        v2_[i, :] = v_[i, :] + (h1 * y + p1_[i, :])

    def six(i, y):
        d2_[i, :] = y - f_[i, :]
        v3 = v2_[i, :] + (h2 * y + p2_[i, :])
        v_[i, :] = v3
        b_[i, :] = v3 - (s_[i, :] + TAU * f_[i, :])

    def seven(i, y):
        d1, d2, d3 = d1_[i, :], d2_[i, :], y - f_[i, :]
        w1_[i, :] = S[0][1] * d1 + S[0][2] * d2 + S[0][3] * d3
        p1_[i, :] = (S[1][1] - h1) * d1 + S[1][2] * d2 + S[1][3] * d3
        p2_[i, :] = S[2][1] * d1 + (S[2][2] - h2) * d2 + S[2][3] * d3

    batched(s_, 18, one)
    batched(w1_, 17, two)
    batched(w2_, 16, three)
    batched(w3_, 15, make_four(s_, f_))
    batched(v_, 14, five)
    batched(v2_, 13, six)
    pieces = chunks(BASE - 12, BASE + OWN + 12, 12)

    def last_of_one(n):
        for at, count in pieces[n:n + 1]:
            one_chunk(lambda i: v_[i, :], seven, at, count)

    def chain(reach, steps, addend, store, beside):
        runs = (OWN + 2 * reach) // 8
        base = (BASE - reach) * 8

        def rows(q, n):
            return pl.ds(base + q * 8 + n, 8, stride=runs * 8)

        def take(ref, n):
            return jnp.concatenate([ref[rows(q, n), :] for q in range(runs)], axis=0)

        mask = take(mask_ref, 0)
        value = take(s_, 0)
        for n in range(steps):
            beside(n)
            own, up, down = product(value)
            up = jnp.concatenate([pltpu.roll(up[-8:], 1, 0), up[:-8]], axis=0)
            down = jnp.concatenate([down[8:], pltpu.roll(down[:8], 7, 0)], axis=0)
            y = (own + up + down) * mask
            for q in range(runs):
                store(rows(q, n), value[q * 8:(q + 1) * 8], y[q * 8:(q + 1) * 8])
            if n < 7:
                value = value + TAU * y + take(addend, n)
        return value, rows, runs

    def keep_first(i, value, y):
        r_[i, :] = value
        lr_[i, :] = y

    chain(CHAIN1, 8, b_, keep_first, last_of_one)

    def eight(i, y):
        g1_[i, :] = y
        w2_[i, :] = w3_[i, :] + (h1 * y + p1_[i, :])

    def nine(i, y):
        g2_[i, :] = y
        w1_[i, :] = w2_[i, :] + (h2 * y + p2_[i, :])

    def eleven(i, y):
        v2_[i, :] = v_[i, :] + (h1 * y + p1_[i, :])

    def twelve(i, y):
        v3 = v2_[i, :] + (h2 * y + p2_[i, :])
        v_[i, :] = v3
        b_[i, :] = v3 - (r_[i, :] + TAU * lr_[i, :])

    for at, n in chunks(BASE - 12, BASE + OWN + 12):
        i = slice(at * 8, (at + n) * 8)
        w3_[i, :] = r_[i, :] + (h0 * lr_[i, :] + w1_[i, :])
    batched(w3_, 11, eight)
    batched(w2_, 10, nine)
    batched(w1_, 9, make_four(r_, lr_))
    batched(v_, 8, eleven)
    batched(v2_, 8, twelve)

    def keep_second(i, value, y):
        f_[i, :] = value

    def deliver(o, ref, t):
        for l in range(4):
            for q in range(OWN // 4):
                row = (BASE + 4 * q + l) * 8 + 2 * t
                out_ref[t, q, o * 8 + 2 * l:o * 8 + 2 * l + 2, :] = ref[row:row + 2, :]

    def ends(n):
        if n < 4:
            deliver(1, v_, n)

    value, rows, runs = chain(CHAIN2, 7, b_, keep_second, ends)
    for q in range(runs):
        f_[rows(q, 7), :] = value[q * 8:(q + 1) * 8]
    for t in range(4):
        deliver(0, f_, t)


def vmem():
    return pl.BlockSpec(memory_space=pltpu.VMEM)


def smem():
    return pl.BlockSpec(memory_space=pltpu.SMEM)


def anywhere():
    return pl.BlockSpec(memory_space=pl.ANY)


def grant(mib):
    return pltpu.CompilerParams(vmem_limit_bytes=mib * 1024 * 1024)


def shards(basis, table, starts, volume_op, face_ops, neighbours):
    unit = lax.axis_index("tm") * 16 + lax.axis_index("zx")
    place = jnp.stack([unit, lax.axis_index("y")]).astype(jnp.int32).reshape(1, 2)

    sent, dt = pl.pallas_call(
        forward_kernel,
        out_shape=(
            jax.ShapeDtypeStruct((UNITS, 8, 128), f32),
            jax.ShapeDtypeStruct((2 * COLS, COLS), bf16),
        ),
        in_specs=[anywhere()] * 3,
        out_specs=(vmem(), vmem()),
        scratch_shapes=[
            pltpu.VMEM((2, 256, 128), f32),
            pltpu.VMEM((4, COLS), jnp.int32),
            pltpu.VMEM((2 * COLS, COLS), bf16),
            pltpu.SemaphoreType.DMA((3,)),
        ],
        name="forward",
    )(starts.reshape(2, 256, 128), neighbours, jnp.asarray(basis))
    wa, wb, mask = pl.pallas_call(
        prepare_kernel,
        out_shape=(
            jax.ShapeDtypeStruct((384, 256), bf16),
            jax.ShapeDtypeStruct((256, 256), bf16),
            jax.ShapeDtypeStruct((LAYERS * 8, 128), f32),
        ),
        in_specs=[vmem(), vmem(), smem(), smem()],
        out_specs=(vmem(),) * 3,
        compiler_params=grant(8),
        cost_estimate=pl.CostEstimate(
            flops=2 * 10**9, bytes_accessed=4 * 10**6, transcendentals=0
        ),
        name="prepare",
    )(volume_op, face_ops, jnp.asarray(table), place)
    got = lax.all_to_all(sent, ("tm", "zx"), 0, 0, tiled=True).reshape(4, 16, 8, 128)
    got, wa, wb, mask = lax.optimization_barrier((got, wa, wb, mask))
    count = HALO // 4
    odd = lax.axis_index("y") % 2 == 1
    low, high = got[:, :count], got[:, 16 - count:]
    first = lax.ppermute(jnp.where(odd, low, high), "y", [(0, 1), (1, 0), (2, 3), (3, 2)])
    second = lax.ppermute(jnp.where(odd, high, low), "y", [(1, 2), (2, 1), (3, 0), (0, 3)])
    below, above = jnp.where(odd, first, second), jnp.where(odd, second, first)
    back = pl.pallas_call(
        middle_kernel,
        out_shape=jax.ShapeDtypeStruct((4, 16, 16, 128), f32),
        in_specs=[vmem()] * 6,
        out_specs=vmem(),
        scratch_shapes=[pltpu.VMEM((LAYERS * 8, 128), f32)] * 16,
        compiler_params=grant(16),
        name="sweeps",
    )(got, below, above, wa, wb, mask)
    home = lax.all_to_all(back.reshape(UNITS, 16, 128), ("tm", "zx"), 0, 0, tiled=True)
    new, end = pl.pallas_call(
        backward_kernel,
        out_shape=(jax.ShapeDtypeStruct((2, 256, 128), f32),) * 2,
        in_specs=[vmem()] * 2,
        out_specs=(anywhere(),) * 2,
        scratch_shapes=[
            pltpu.VMEM((2, 256, 128), f32),
            pltpu.VMEM((2, 256, 128), f32),
            pltpu.SemaphoreType.DMA((2,)),
        ],
        compiler_params=grant(8),
        name="backward",
    )(home, dt)
    return new.reshape(2, 64, 4, 128), end.reshape(2, 64, 4, 128)


def solution(mesh):
    finer = Mesh(mesh.devices.reshape(4, 4, 16), ("tm", "y", "zx"))
    basis, table = modes()
    placed = P("tm", None, ("y", "zx"), None)
    return jax.shard_map(
        functools.partial(shards, basis, table),
        mesh=finer,
        in_specs=(placed, P(), P(), P()),
        out_specs=(placed, placed),
        check_vma=False,
    )
```

```python
import functools
import math

import jax
import jax.numpy as jnp
import ml_dtypes
import numpy as np
from jax import lax
from jax.experimental import pallas as pl
from jax.experimental.pallas import tpu as pltpu
from jax.sharding import Mesh
from jax.sharding import PartitionSpec as P

PY, PZ = 8, 16
COLS = PY * PZ
UNITS = 64
SLICES = 8
OWN = 64
HALO = 20
WIN = OWN + 2 * HALO
PAD = 2
LAYERS = WIN + 2 * PAD
BASE = PAD + HALO
CHAIN1 = 16
CHAIN2 = 8
TAU = 0.25
f32, bf16 = jnp.float32, jnp.bfloat16


def lagrange_integral(points, which, lower, upper):
    coefficients = [1.0]
    divisor = 1.0
    for other in range(4):
        if other != which:
            product = [0.0] * (len(coefficients) + 1)
            for power in range(len(coefficients)):
                product[power + 1] = product[power + 1] + coefficients[power]
                product[power] = product[power] - coefficients[power] * points[other]
            coefficients = product
            divisor = divisor * (points[which] - points[other])
    integral = 0.0
    for power in range(len(coefficients)):
        integral = integral + coefficients[power] * (
            upper ** (power + 1) - lower ** (power + 1)
        ) / (power + 1)
    return integral / divisor


def sdc_tables():
    offset = 0.5 / math.sqrt(5.0)
    points = [0.0, 0.5 - offset, 0.5 + offset, 1.0]
    widths = [TAU * (points[m + 1] - points[m]) for m in range(3)]
    weights = [
        [float(TAU * lagrange_integral(points, j, points[m], points[m + 1])) for j in range(4)]
        for m in range(3)
    ]
    return widths, weights


def modes():
    pairs = [(ka, kb) for kb in range(1, PZ // 2) for ka in range(PY)]
    pairs += [(ka, kb) for kb in (0, PZ // 2) for ka in range(1, PY // 2)]
    single = [((0, 0), (PY // 2, 0)), ((0, PZ // 2), (PY // 2, PZ // 2))]
    places = np.arange(COLS)
    a, b = places // PZ, places % PZ

    def angle(k):
        return 2.0 * np.pi * (((k[0] * a * (PZ // PY) + k[1] * b) % PZ) / PZ)

    def turn(k):
        return 2.0 * np.pi * k[0] / PY, 2.0 * np.pi * k[1] / PZ

    basis = np.zeros((2 * UNITS, COLS))
    table = np.zeros((UNITS, 8))
    for u, k in enumerate(pairs):
        scale = math.sqrt(2.0 / COLS)
        basis[u] = scale * np.cos(angle(k))
        basis[UNITS + u] = scale * np.sin(angle(k))
        al, be = turn(k)
        table[u, :6] = [np.cos(al), np.cos(be), np.cos(al), np.cos(be), np.sin(al), np.sin(be)]
    for i, (k, other) in enumerate(single):
        u = len(pairs) + i
        scale = math.sqrt(1.0 / COLS)
        basis[u] = scale * np.cos(angle(k))
        basis[UNITS + u] = scale * np.cos(angle(other))
        al, be = turn(k)
        al2, be2 = turn(other)
        table[u, :6] = [np.cos(al), np.cos(be), np.cos(al2), np.cos(be2), 0.0, 0.0]
    basis = basis.astype(np.float32)
    high = basis.astype(ml_dtypes.bfloat16)
    low = (basis - high.astype(np.float32)).astype(ml_dtypes.bfloat16)
    return np.concatenate([high, low], axis=0), table.astype(np.float32)


def look_up(table, index):
    return jnp.take_along_axis(table, index, axis=1)


def split(x):
    high = x.astype(bf16)
    low = (x - high.astype(f32)).astype(bf16)
    return high, low


def forward_kernel(x_hbm, nb_hbm, basis_hbm, out_ref, dt_ref, x_ref, nb_ref, basis_ref, sems):
    copies = [
        pltpu.make_async_copy(src, dst, sems.at[i])
        for i, (src, dst) in enumerate(
            ((nb_hbm, nb_ref), (basis_hbm, basis_ref), (x_hbm, x_ref))
        )
    ]
    for copy in copies:
        copy.start()
    copies[0].wait()
    a1 = jnp.broadcast_to(nb_ref[1:2, :], (8, COLS))
    b1 = jnp.broadcast_to(nb_ref[3:4, :], (8, COLS))
    place = lax.broadcasted_iota(jnp.int32, (8, COLS), 1)
    times = lax.broadcasted_iota(jnp.int32, (8, COLS), 0)
    a2, b2 = look_up(a1, a1), look_up(b1, b1)
    a4, b4 = look_up(a2, a2), look_up(b2, b2)
    b8 = look_up(b4, b4)
    along = jnp.where(times & 1 == 1, a1, place)
    along = jnp.where(times & 2 == 2, look_up(a2, along), along)
    along = jnp.where(times & 4 == 4, look_up(a4, along), along)
    column = jnp.zeros((8, COLS), jnp.int32)
    for bit, table in ((1, b1), (2, b2), (4, b4), (8, b8)):
        column = jnp.where(place & bit == bit, look_up(table, column), column)
    column = jnp.where(place // PZ == times, look_up(along, column), 0)
    column = jnp.sum(column, axis=0, keepdims=True)
    row = lax.broadcasted_iota(jnp.int32, (COLS, COLS), 0)
    hit = jnp.broadcast_to(column, (COLS, COLS)) == row
    one_hot = jnp.where(hit, 1.0, 0.0).astype(bf16)
    copies[1].wait()
    dt = lax.dot_general(
        basis_ref[...], one_hot, (((1,), (1,)), ((), ())), preferred_element_type=f32
    ).astype(bf16)
    dt_ref[...] = dt
    copies[2].wait()
    parts = []
    for l in range(4):
        for s in range(2):
            parts.append(x_ref[s, pl.ds(l, 64, stride=4), :])
    high, low = split(jnp.concatenate(parts, axis=0))
    result = lax.dot_general(
        jnp.concatenate([dt[:128], dt[:128], dt[128:]], axis=1),
        jnp.concatenate([high, low, high], axis=1),
        (((1,), (1,)), ((), ())), preferred_element_type=f32,
    )
    left = lax.broadcasted_iota(jnp.int32, (UNITS, COLS), 1) < 64
    for k in range(4):
        even = result[:UNITS, k * 128:(k + 1) * 128]
        odd = result[UNITS:, k * 128:(k + 1) * 128]
        out_ref[:, 2 * k, :] = jnp.where(left, even, pltpu.roll(odd, 64, 1))
        out_ref[:, 2 * k + 1, :] = jnp.where(left, pltpu.roll(even, 64, 1), odd)


def backward_kernel(z_ref, dt_ref, new_hbm, end_hbm, new_ref, end_ref, sems):
    zero = jnp.zeros((UNITS, COLS), bf16)

    def weight(dt):
        top, bottom = dt[:UNITS], dt[UNITS:]
        return jnp.concatenate(
            [
                jnp.concatenate([top, zero], axis=1),
                jnp.concatenate([zero, top], axis=1),
                jnp.concatenate([bottom, zero], axis=1),
                jnp.concatenate([zero, bottom], axis=1),
            ],
            axis=0,
        )

    high_dt, low_dt = weight(dt_ref[0:128, :]), weight(dt_ref[128:256, :])
    weights = jnp.concatenate([high_dt, high_dt, low_dt], axis=0)
    copies = []
    for o, (ref, hbm) in enumerate(((new_ref, new_hbm), (end_ref, end_hbm))):
        rows = []
        for l in range(4):
            pair = 4 * o + l
            block = jnp.concatenate([z_ref[:, 2 * pair, :], z_ref[:, 2 * pair + 1, :]], axis=0)
            turned = block.T
            rows.append(jnp.concatenate([turned[:64], turned[64:]], axis=1))
        for half in range(2):
            part = slice(half * 32, half * 32 + 32)
            high, low = split(jnp.concatenate([row[part] for row in rows], axis=0))
            result = jnp.dot(
                jnp.concatenate([high, low, high], axis=1), weights, preferred_element_type=f32
            )
            for l in range(4):
                for s in range(2):
                    ref[s, pl.ds(half * 128 + l, 32, stride=4), :] = result[
                        l * 32:(l + 1) * 32, s * 128:(s + 1) * 128
                    ]
            lines = pl.ds(half * 128, 128)
            copies.append(
                pltpu.make_async_copy(
                    ref.at[:, lines], hbm.at[:, lines], sems.at[2 * o + half]
                )
            )
            copies[-1].start()
    for copy in copies:
        copy.wait()


def chunks(first, last, most=34):
    count = last - first
    size = -(-count // -(-count // most))
    size += size % 2
    return [(at, min(size, last - at)) for at in range(first, last, size)]


def prepare_kernel(vol_ref, face_ref, table_ref, place_ref, wa_ref, wb_ref, ends_ref):
    unit = place_ref[0, 0]
    fa, fb = face_ref[2] + face_ref[3], face_ref[4] + face_ref[5]
    ga, gb = face_ref[3] - face_ref[2], face_ref[5] - face_ref[4]
    vol = vol_ref[...]
    mcc = vol + table_ref[unit, 0] * fa + table_ref[unit, 1] * fb
    mss = vol + table_ref[unit, 2] * fa + table_ref[unit, 3] * fb
    mcs = table_ref[unit, 4] * ga + table_ref[unit, 5] * gb
    zero = jnp.zeros((64, 64), f32)

    def block(a, b, c, d):
        return jnp.concatenate(
            [jnp.concatenate([a, b], axis=1), jnp.concatenate([c, d], axis=1)], axis=0
        ).T

    m_high, m_low = split(block(mcc, mcs, -mcs, mss))
    f0_high, f0_low = split(block(face_ref[0], zero, zero, face_ref[0]))
    f1_high, f1_low = split(block(face_ref[1], zero, zero, face_ref[1]))
    both = jnp.concatenate([f1_high, m_high], axis=1)
    wa_ref[0:128, :] = both
    wa_ref[128:256, :] = both
    wa_ref[256:384, :] = jnp.concatenate([f1_low, m_low], axis=1)
    wb_ref[0:128, :] = jnp.concatenate([f0_high, f0_low], axis=1)
    wb_ref[128:256, :] = jnp.concatenate([f0_high, jnp.zeros_like(f0_low)], axis=1)
    ends_ref[0:8, :] = jnp.full((8, 128), jnp.where(place_ref[0, 1] == 0, 1.0, 0.0))
    ends_ref[8:16, :] = jnp.full((8, 128), jnp.where(place_ref[0, 1] == 3, 1.0, 0.0))


def middle_kernel(r_ref, lo_ref, hi_ref, wa_ref, wb_ref, ends_ref, out_ref, *bufs):
    widths, S = sdc_tables()
    h0, h1, h2 = widths
    at_bottom = ends_ref[0:8, :] > 0.5
    at_top = ends_ref[8:16, :] > 0.5

    s_, f_, w1_, w2_, w3_, g1_, g2_, p1_, p2_, v_, v2_, d1_, d2_, b_, r_, lr_ = bufs
    b_[...] = jnp.zeros_like(b_)

    for t in range(4):
        for l in range(4):
            for ref, count, at in (
                (lo_ref, HALO // 4, PAD),
                (r_ref, OWN // 4, BASE),
                (hi_ref, HALO // 4, BASE + OWN),
            ):
                for q in range(count):
                    row = (at + 4 * q + l) * 8 + 2 * t
                    s_[row:row + 2, :] = ref[t, q, 2 * l:2 * l + 2, :]

    def product(x):
        high, low = split(x)
        acc = jnp.dot(
            jnp.concatenate([high, low, high], axis=1), wa_ref[...], preferred_element_type=f32
        )
        up = jnp.dot(
            jnp.concatenate([high, low], axis=1), wb_ref[...], preferred_element_type=f32
        )
        return acc[:, 128:], up[:, :128] + up[:, 128:], acc[:, :128]

    def cut(rows, i, ends):
        if not 0 <= i < rows.shape[0] // 8:
            return rows
        part = jnp.where(ends, 0.0, rows[i * 8:i * 8 + 8])
        around = [rows[:i * 8], part, rows[i * 8 + 8:]]
        return jnp.concatenate([r for r in around if r.shape[0]], axis=0)

    def pieces(take, reach, then, most=34):
        edge = None
        for at, n in chunks(BASE - reach - 1, BASE + OWN + reach + 1, most):
            own, up, down = product(take(slice(at * 8, (at + n) * 8)))
            up = cut(up, BASE - 1 - at, at_bottom)
            down = cut(down, BASE + OWN - at, at_top)
            if edge is None:
                here = slice((at + 1) * 8, (at + n - 1) * 8)
                y = own[8:-8] + up[:-16] + down[16:]
            else:
                here = slice((at - 1) * 8, (at + n - 1) * 8)
                y = (
                    jnp.concatenate([edge[0], own[:-8]], axis=0)
                    + jnp.concatenate([edge[1], up[:-16]], axis=0)
                    + down
                )
            edge = own[-8:], up[-16:]
            then(here, y)
            yield

    def batched(src, reach, then):
        for _ in pieces(lambda i: src[i, :], reach, then):
            pass

    def one(i, y):
        f_[i, :] = y
        w1_[i, :] = s_[i, :] + h0 * y

    def two(i, y):
        g1_[i, :] = y
        w2_[i, :] = w1_[i, :] + h1 * y

    def three(i, y):
        g2_[i, :] = y
        w3_[i, :] = w2_[i, :] + h2 * y

    def make_four(start, zeroth):
        def four(i, y):
            g0, g1, g2 = zeroth[i, :], g1_[i, :], g2_[i, :]
            v_[i, :] = start[i, :] + (S[0][0] * g0 + S[0][1] * g1 + S[0][2] * g2 + S[0][3] * y)
            p1_[i, :] = S[1][0] * g0 + (S[1][1] - h1) * g1 + S[1][2] * g2 + S[1][3] * y
            p2_[i, :] = S[2][0] * g0 + S[2][1] * g1 + (S[2][2] - h2) * g2 + S[2][3] * y

        return four

    def five(i, y):
        d1_[i, :] = y - f_[i, :]
        v2_[i, :] = v_[i, :] + (h1 * y + p1_[i, :])

    def six(i, y):
        d2_[i, :] = y - f_[i, :]
        v3 = v2_[i, :] + (h2 * y + p2_[i, :])
        v_[i, :] = v3
        b_[i, :] = v3 - (s_[i, :] + TAU * f_[i, :])

    def seven(i, y):
        d1, d2, d3 = d1_[i, :], d2_[i, :], y - f_[i, :]
        w1_[i, :] = S[0][1] * d1 + S[0][2] * d2 + S[0][3] * d3
        p1_[i, :] = (S[1][1] - h1) * d1 + S[1][2] * d2 + S[1][3] * d3
        p2_[i, :] = S[2][1] * d1 + (S[2][2] - h2) * d2 + S[2][3] * d3

    batched(s_, 17, one)
    batched(w1_, 16, two)
    batched(w2_, 15, three)
    batched(w3_, 14, make_four(s_, f_))
    batched(v_, 13, five)
    batched(v2_, 12, six)
    rest = pieces(lambda i: v_[i, :], 11, seven, 12)

    def last_of_one(n):
        next(rest, None)

    def chain(reach, steps, addend, store, beside):
        runs = (OWN + 2 * reach) // 8
        base = (BASE - reach) * 8

        def rows(q, n):
            return pl.ds(base + q * 8 + n, 8, stride=runs * 8)

        def take(ref, n):
            return jnp.concatenate([ref[rows(q, n), :] for q in range(runs)], axis=0)

        sublane = lax.broadcasted_iota(jnp.int32, (8, 128), 0)

        def cut_one(rows, layer, ends):
            return cut(rows, layer % runs, ends & (sublane == layer // runs))

        value = take(s_, 0)
        for n in range(steps):
            beside(n)
            own, up, down = product(value)
            up = cut_one(up, reach - 1, at_bottom)
            down = cut_one(down, reach + OWN, at_top)
            up = jnp.concatenate([pltpu.roll(up[-8:], 1, 0), up[:-8]], axis=0)
            down = jnp.concatenate([down[8:], pltpu.roll(down[:8], 7, 0)], axis=0)
            y = own + up + down
            for q in range(runs):
                store(rows(q, n), value[q * 8:(q + 1) * 8], y[q * 8:(q + 1) * 8])
            if n < 7:
                value = value + TAU * y + take(addend, n)
        return value, rows, runs

    def keep_first(i, value, y):
        r_[i, :] = value
        lr_[i, :] = y

    chain(CHAIN1, 8, b_, keep_first, last_of_one)

    def eight(i, y):
        g1_[i, :] = y
        w2_[i, :] = w3_[i, :] + (h1 * y + p1_[i, :])

    def nine(i, y):
        g2_[i, :] = y
        w1_[i, :] = w2_[i, :] + (h2 * y + p2_[i, :])

    def eleven(i, y):
        v2_[i, :] = v_[i, :] + (h1 * y + p1_[i, :])

    def twelve(i, y):
        v3 = v2_[i, :] + (h2 * y + p2_[i, :])
        v_[i, :] = v3
        b_[i, :] = v3 - (r_[i, :] + TAU * lr_[i, :])

    def first_value(i):
        value = r_[i, :] + (h0 * lr_[i, :] + w1_[i, :])
        w3_[i, :] = value
        return value

    for _ in pieces(first_value, 10, eight):
        pass
    batched(w2_, 9, nine)
    batched(w1_, 8, make_four(r_, lr_))
    batched(v_, 7, eleven)
    batched(v2_, 6, twelve)

    def keep_second(i, value, y):
        f_[i, :] = value

    def deliver(o, ref, t):
        for l in range(4):
            for q in range(OWN // 4):
                row = (BASE + 4 * q + l) * 8 + 2 * t
                out_ref[t, q, o * 8 + 2 * l:o * 8 + 2 * l + 2, :] = ref[row:row + 2, :]

    def ends(n):
        if n < 4:
            deliver(1, v_, n)

    value, rows, runs = chain(CHAIN2, 7, b_, keep_second, ends)
    for q in range(runs):
        f_[rows(q, 7), :] = value[q * 8:(q + 1) * 8]
    for t in range(4):
        deliver(0, f_, t)


def vmem():
    return pl.BlockSpec(memory_space=pltpu.VMEM)


def smem():
    return pl.BlockSpec(memory_space=pltpu.SMEM)


def anywhere():
    return pl.BlockSpec(memory_space=pl.ANY)


def grant(mib):
    return pltpu.CompilerParams(vmem_limit_bytes=mib * 1024 * 1024)


def shards(basis, table, starts, volume_op, face_ops, neighbours):
    unit = lax.axis_index("tm") * 16 + lax.axis_index("zx")
    place = jnp.stack([unit, lax.axis_index("y")]).astype(jnp.int32).reshape(1, 2)

    sent, dt = pl.pallas_call(
        forward_kernel,
        out_shape=(
            jax.ShapeDtypeStruct((UNITS, 8, 128), f32),
            jax.ShapeDtypeStruct((2 * COLS, COLS), bf16),
        ),
        in_specs=[anywhere()] * 3,
        out_specs=(vmem(), vmem()),
        scratch_shapes=[
            pltpu.VMEM((2, 256, 128), f32),
            pltpu.VMEM((4, COLS), jnp.int32),
            pltpu.VMEM((2 * COLS, COLS), bf16),
            pltpu.SemaphoreType.DMA((3,)),
        ],
        name="forward",
    )(starts.reshape(2, 256, 128), neighbours, jnp.asarray(basis))
    wa, wb, ends = pl.pallas_call(
        prepare_kernel,
        out_shape=(
            jax.ShapeDtypeStruct((384, 256), bf16),
            jax.ShapeDtypeStruct((256, 256), bf16),
            jax.ShapeDtypeStruct((16, 128), f32),
        ),
        in_specs=[vmem(), vmem(), smem(), smem()],
        out_specs=(vmem(),) * 3,
        compiler_params=grant(8),
        cost_estimate=pl.CostEstimate(
            flops=2 * 10**9, bytes_accessed=4 * 10**6, transcendentals=0
        ),
        name="prepare",
    )(volume_op, face_ops, jnp.asarray(table), place)
    got = lax.all_to_all(sent, ("tm", "zx"), 0, 0, tiled=True).reshape(4, 16, 8, 128)
    got, wa, wb, ends = lax.optimization_barrier((got, wa, wb, ends))
    count = HALO // 4
    odd = lax.axis_index("y") % 2 == 1
    low, high = got[:, :count], got[:, 16 - count:]
    first = lax.ppermute(jnp.where(odd, low, high), "y", [(0, 1), (1, 0), (2, 3), (3, 2)])
    second = lax.ppermute(jnp.where(odd, high, low), "y", [(1, 2), (2, 1), (3, 0), (0, 3)])
    below, above = jnp.where(odd, first, second), jnp.where(odd, second, first)
    back = pl.pallas_call(
        middle_kernel,
        out_shape=jax.ShapeDtypeStruct((4, 16, 16, 128), f32),
        in_specs=[vmem()] * 6,
        out_specs=vmem(),
        scratch_shapes=[pltpu.VMEM((LAYERS * 8, 128), f32)] * 16,
        compiler_params=grant(16),
        name="sweeps",
    )(got, below, above, wa, wb, ends)
    home = lax.all_to_all(back.reshape(UNITS, 16, 128), ("tm", "zx"), 0, 0, tiled=True)
    new, end = pl.pallas_call(
        backward_kernel,
        out_shape=(jax.ShapeDtypeStruct((2, 256, 128), f32),) * 2,
        in_specs=[vmem()] * 2,
        out_specs=(anywhere(),) * 2,
        scratch_shapes=[
            pltpu.VMEM((2, 256, 128), f32),
            pltpu.VMEM((2, 256, 128), f32),
            pltpu.SemaphoreType.DMA((4,)),
        ],
        compiler_params=grant(8),
        name="backward",
    )(home, dt)
    return new.reshape(2, 64, 4, 128), end.reshape(2, 64, 4, 128)


def solution(mesh):
    finer = Mesh(mesh.devices.reshape(4, 4, 16), ("tm", "y", "zx"))
    basis, table = modes()
    placed = P("tm", None, ("y", "zx"), None)
    return jax.shard_map(
        functools.partial(shards, basis, table),
        mesh=finer,
        in_specs=(placed, P(), P(), P()),
        out_specs=(placed, placed),
        check_vma=False,
    )
```

```python
import functools
import math

import jax
import jax.numpy as jnp
import ml_dtypes
import numpy as np
from jax import lax
from jax.experimental import pallas as pl
from jax.experimental.pallas import tpu as pltpu
from jax.sharding import Mesh
from jax.sharding import PartitionSpec as P

PY, PZ = 8, 16
COLS = PY * PZ
UNITS = 64
SLICES = 8
OWN = 64
HALO = 20
WIN = OWN + 2 * HALO
PAD = 2
LAYERS = WIN + 2 * PAD
BASE = PAD + HALO
CHAIN1 = 16
CHAIN2 = 8
TAU = 0.25
f32, bf16 = jnp.float32, jnp.bfloat16


def lagrange_integral(points, which, lower, upper):
    coefficients = [1.0]
    divisor = 1.0
    for other in range(4):
        if other != which:
            product = [0.0] * (len(coefficients) + 1)
            for power in range(len(coefficients)):
                product[power + 1] = product[power + 1] + coefficients[power]
                product[power] = product[power] - coefficients[power] * points[other]
            coefficients = product
            divisor = divisor * (points[which] - points[other])
    integral = 0.0
    for power in range(len(coefficients)):
        integral = integral + coefficients[power] * (
            upper ** (power + 1) - lower ** (power + 1)
        ) / (power + 1)
    return integral / divisor


def sdc_tables():
    offset = 0.5 / math.sqrt(5.0)
    points = [0.0, 0.5 - offset, 0.5 + offset, 1.0]
    widths = [TAU * (points[m + 1] - points[m]) for m in range(3)]
    weights = [
        [float(TAU * lagrange_integral(points, j, points[m], points[m + 1])) for j in range(4)]
        for m in range(3)
    ]
    return widths, weights


def modes():
    pairs = [(ka, kb) for kb in range(1, PZ // 2) for ka in range(PY)]
    pairs += [(ka, kb) for kb in (0, PZ // 2) for ka in range(1, PY // 2)]
    single = [((0, 0), (PY // 2, 0)), ((0, PZ // 2), (PY // 2, PZ // 2))]
    places = np.arange(COLS)
    a, b = places // PZ, places % PZ

    def angle(k):
        return 2.0 * np.pi * (((k[0] * a * (PZ // PY) + k[1] * b) % PZ) / PZ)

    def turn(k):
        return 2.0 * np.pi * k[0] / PY, 2.0 * np.pi * k[1] / PZ

    basis = np.zeros((2 * UNITS, COLS))
    table = np.zeros((UNITS, 8))
    for u, k in enumerate(pairs):
        scale = math.sqrt(2.0 / COLS)
        basis[u] = scale * np.cos(angle(k))
        basis[UNITS + u] = scale * np.sin(angle(k))
        al, be = turn(k)
        table[u, :6] = [np.cos(al), np.cos(be), np.cos(al), np.cos(be), np.sin(al), np.sin(be)]
    for i, (k, other) in enumerate(single):
        u = len(pairs) + i
        scale = math.sqrt(1.0 / COLS)
        basis[u] = scale * np.cos(angle(k))
        basis[UNITS + u] = scale * np.cos(angle(other))
        al, be = turn(k)
        al2, be2 = turn(other)
        table[u, :6] = [np.cos(al), np.cos(be), np.cos(al2), np.cos(be2), 0.0, 0.0]
    basis = basis.astype(np.float32)
    high = basis.astype(ml_dtypes.bfloat16)
    low = (basis - high.astype(np.float32)).astype(ml_dtypes.bfloat16)
    return np.concatenate([high, low], axis=0), table.astype(np.float32)


def look_up(table, index):
    return jnp.take_along_axis(table, index, axis=1)


def split(x):
    high = x.astype(bf16)
    low = (x - high.astype(f32)).astype(bf16)
    return high, low


def forward_kernel(x_hbm, nb_hbm, basis_hbm, out_ref, dt_ref, x_ref, nb_ref, basis_ref, sems):
    copies = [
        pltpu.make_async_copy(src, dst, sems.at[i])
        for i, (src, dst) in enumerate(
            ((nb_hbm, nb_ref), (basis_hbm, basis_ref), (x_hbm, x_ref))
        )
    ]
    for copy in copies:
        copy.start()
    copies[0].wait()
    a1 = jnp.broadcast_to(nb_ref[1:2, :], (8, COLS))
    b1 = jnp.broadcast_to(nb_ref[3:4, :], (8, COLS))
    place = lax.broadcasted_iota(jnp.int32, (8, COLS), 1)
    times = lax.broadcasted_iota(jnp.int32, (8, COLS), 0)
    a2, b2 = look_up(a1, a1), look_up(b1, b1)
    a4, b4 = look_up(a2, a2), look_up(b2, b2)
    b8 = look_up(b4, b4)
    along = jnp.where(times & 1 == 1, a1, place)
    along = jnp.where(times & 2 == 2, look_up(a2, along), along)
    along = jnp.where(times & 4 == 4, look_up(a4, along), along)
    column = jnp.zeros((8, COLS), jnp.int32)
    for bit, table in ((1, b1), (2, b2), (4, b4), (8, b8)):
        column = jnp.where(place & bit == bit, look_up(table, column), column)
    column = jnp.where(place // PZ == times, look_up(along, column), 0)
    column = jnp.sum(column, axis=0, keepdims=True)
    row = lax.broadcasted_iota(jnp.int32, (COLS, COLS), 0)
    hit = jnp.broadcast_to(column, (COLS, COLS)) == row
    one_hot = jnp.where(hit, 1.0, 0.0).astype(bf16)
    copies[1].wait()
    dt = lax.dot_general(
        basis_ref[...], one_hot, (((1,), (1,)), ((), ())), preferred_element_type=f32
    ).astype(bf16)
    dt_ref[...] = dt
    copies[2].wait()
    parts = []
    for l in range(4):
        for s in range(2):
            parts.append(x_ref[s, pl.ds(l, 64, stride=4), :])
    high, low = split(jnp.concatenate(parts, axis=0))
    result = lax.dot_general(
        jnp.concatenate([dt[:128], dt[:128], dt[128:]], axis=1),
        jnp.concatenate([high, low, high], axis=1),
        (((1,), (1,)), ((), ())), preferred_element_type=f32,
    )
    left = lax.broadcasted_iota(jnp.int32, (UNITS, COLS), 1) < 64
    for k in range(4):
        even = result[:UNITS, k * 128:(k + 1) * 128]
        odd = result[UNITS:, k * 128:(k + 1) * 128]
        out_ref[:, 2 * k, :] = jnp.where(left, even, pltpu.roll(odd, 64, 1))
        out_ref[:, 2 * k + 1, :] = jnp.where(left, pltpu.roll(even, 64, 1), odd)


def backward_kernel(z_ref, dt_ref, new_hbm, end_hbm, new_ref, end_ref, sems):
    zero = jnp.zeros((UNITS, COLS), bf16)

    def weight(dt):
        top, bottom = dt[:UNITS], dt[UNITS:]
        return jnp.concatenate(
            [
                jnp.concatenate([top, zero], axis=1),
                jnp.concatenate([zero, top], axis=1),
                jnp.concatenate([bottom, zero], axis=1),
                jnp.concatenate([zero, bottom], axis=1),
            ],
            axis=0,
        )

    high_dt, low_dt = weight(dt_ref[0:128, :]), weight(dt_ref[128:256, :])
    weights = jnp.concatenate([high_dt, high_dt, low_dt], axis=0)
    copies = []
    for o, (ref, hbm) in enumerate(((new_ref, new_hbm), (end_ref, end_hbm))):
        rows = []
        for l in range(4):
            pair = 4 * o + l
            block = jnp.concatenate([z_ref[:, 2 * pair, :], z_ref[:, 2 * pair + 1, :]], axis=0)
            turned = block.T
            rows.append(jnp.concatenate([turned[:64], turned[64:]], axis=1))
        for half in range(2):
            part = slice(half * 32, half * 32 + 32)
            high, low = split(jnp.concatenate([row[part] for row in rows], axis=0))
            result = jnp.dot(
                jnp.concatenate([high, low, high], axis=1), weights, preferred_element_type=f32
            )
            for l in range(4):
                for s in range(2):
                    ref[s, pl.ds(half * 128 + l, 32, stride=4), :] = result[
                        l * 32:(l + 1) * 32, s * 128:(s + 1) * 128
                    ]
            lines = pl.ds(half * 128, 128)
            copies.append(
                pltpu.make_async_copy(
                    ref.at[:, lines], hbm.at[:, lines], sems.at[2 * o + half]
                )
            )
            copies[-1].start()
    for copy in copies:
        copy.wait()


def chunks(first, last, most=34):
    count = last - first
    size = -(-count // -(-count // most))
    size += size % 2
    return [(at, min(size, last - at)) for at in range(first, last, size)]


def prepare_kernel(vol_ref, face_ref, table_ref, place_ref, wa_ref, wb_ref, ends_ref):
    unit = place_ref[0, 0]
    fa, fb = face_ref[2] + face_ref[3], face_ref[4] + face_ref[5]
    ga, gb = face_ref[3] - face_ref[2], face_ref[5] - face_ref[4]
    vol = vol_ref[...]
    mcc = vol + table_ref[unit, 0] * fa + table_ref[unit, 1] * fb
    mss = vol + table_ref[unit, 2] * fa + table_ref[unit, 3] * fb
    mcs = table_ref[unit, 4] * ga + table_ref[unit, 5] * gb
    zero = jnp.zeros((64, 64), f32)

    def block(a, b, c, d):
        return jnp.concatenate(
            [jnp.concatenate([a, b], axis=1), jnp.concatenate([c, d], axis=1)], axis=0
        ).T

    m_high, m_low = split(block(mcc, mcs, -mcs, mss))
    f0_high, f0_low = split(block(face_ref[0], zero, zero, face_ref[0]))
    f1_high, f1_low = split(block(face_ref[1], zero, zero, face_ref[1]))
    both = jnp.concatenate([f1_high, m_high], axis=1)
    wa_ref[0:128, :] = both
    wa_ref[128:256, :] = both
    wa_ref[256:384, :] = jnp.concatenate([f1_low, m_low], axis=1)
    wb_ref[0:128, :] = jnp.concatenate([f0_high, f0_low], axis=1)
    wb_ref[128:256, :] = jnp.concatenate([f0_high, jnp.zeros_like(f0_low)], axis=1)
    ends_ref[0:8, :] = jnp.full((8, 128), jnp.where(place_ref[0, 1] == 0, 1.0, 0.0))
    ends_ref[8:16, :] = jnp.full((8, 128), jnp.where(place_ref[0, 1] == 3, 1.0, 0.0))


NAMES = "s f d1 d2 v3 b w1 w2 w3 g1 g2 p1 p2 v v2 r lr".split()
WHOLE = "s f d1 d2 v3 b".split()
RIMS = "w1 w2 w3 g1 g2 p1 p2 v v2".split()
RIM = 8
HANDED = (len(WHOLE) * OWN + len(RIMS) * 2 * RIM) * 8


def handed():
    at = 0
    for name in WHOLE:
        yield name, BASE * 8, at, OWN * 8
        at += OWN * 8
    for name in RIMS:
        for first in (BASE, BASE + OWN - RIM):
            yield name, first * 8, at, RIM * 8
            at += RIM * 8


class Sweeps:
    def __init__(self, wa_ref, wb_ref, bufs, ends_ref=None):
        self.wa, self.wb, self.ends = wa_ref, wb_ref, ends_ref
        self.bufs = dict(zip(NAMES, bufs))

    def at_ends(self):
        return self.ends[0:8, :] > 0.5, self.ends[8:16, :] > 0.5

    def fill(self, ref, at, count):
        for t in range(4):
            for l in range(4):
                for q in range(count):
                    row = (at + 4 * q + l) * 8 + 2 * t
                    self.bufs["s"][row:row + 2, :] = ref[t, q, 2 * l:2 * l + 2, :]

    def product(self, x):
        high, low = split(x)
        acc = jnp.dot(
            jnp.concatenate([high, low, high], axis=1), self.wa[...],
            preferred_element_type=f32,
        )
        up = jnp.dot(
            jnp.concatenate([high, low], axis=1), self.wb[...], preferred_element_type=f32
        )
        return acc[:, 128:], up[:, :128] + up[:, 128:], acc[:, :128]

    def pieces(self, take, first, last, then, most=34):
        edge = None
        for at, n in chunks(first - 1, last + 1, most):
            own, up, down = self.product(take(slice(at * 8, (at + n) * 8)))
            if self.ends is not None:
                up = cut(up, BASE - 1 - at, self.at_ends()[0])
                down = cut(down, BASE + OWN - at, self.at_ends()[1])
            if edge is None:
                here = slice((at + 1) * 8, (at + n - 1) * 8)
                y = own[8:-8] + up[:-16] + down[16:]
            else:
                here = slice((at - 1) * 8, (at + n - 1) * 8)
                y = (
                    jnp.concatenate([edge[0], own[:-8]], axis=0)
                    + jnp.concatenate([edge[1], up[:-16]], axis=0)
                    + down
                )
            edge = own[-8:], up[-16:]
            then(here, y)
            yield

    def batched(self, name, first, last, then):
        src = self.bufs[name]
        for _ in self.pieces(lambda i: src[i, :], first, last, then):
            pass

    def make_four(self, start, zeroth):
        S = sdc_tables()[1]
        h1, h2 = sdc_tables()[0][1:]
        B = self.bufs

        def four(i, y):
            g0, g1, g2 = B[zeroth][i, :], B["g1"][i, :], B["g2"][i, :]
            B["v"][i, :] = B[start][i, :] + (
                S[0][0] * g0 + S[0][1] * g1 + S[0][2] * g2 + S[0][3] * y
            )
            B["p1"][i, :] = S[1][0] * g0 + (S[1][1] - h1) * g1 + S[1][2] * g2 + S[1][3] * y
            B["p2"][i, :] = S[2][0] * g0 + S[2][1] * g1 + (S[2][2] - h2) * g2 + S[2][3] * y

        return four

    def first_iteration(self):
        h0, h1, h2 = sdc_tables()[0]
        B = self.bufs

        def one(i, y):
            B["f"][i, :] = y
            B["w1"][i, :] = B["s"][i, :] + h0 * y

        def two(i, y):
            B["g1"][i, :] = y
            B["w2"][i, :] = B["w1"][i, :] + h1 * y

        def three(i, y):
            B["g2"][i, :] = y
            B["w3"][i, :] = B["w2"][i, :] + h2 * y

        def five(i, y):
            B["d1"][i, :] = y - B["f"][i, :]
            B["v2"][i, :] = B["v"][i, :] + (h1 * y + B["p1"][i, :])

        def six(i, y):
            B["d2"][i, :] = y - B["f"][i, :]
            v3 = B["v2"][i, :] + (h2 * y + B["p2"][i, :])
            B["v3"][i, :] = v3
            B["b"][i, :] = v3 - (B["s"][i, :] + TAU * B["f"][i, :])

        return (
            ("s", one), ("w1", two), ("w2", three), ("w3", self.make_four("s", "f")),
            ("v", five), ("v2", six),
        )


def cut(rows, i, where):
    if not 0 <= i < rows.shape[0] // 8:
        return rows
    part = jnp.where(where, 0.0, rows[i * 8:i * 8 + 8])
    around = [rows[:i * 8], part, rows[i * 8 + 8:]]
    return jnp.concatenate([r for r in around if r.shape[0]], axis=0)


def inner_kernel(r_ref, wa_ref, wb_ref, out_ref, *bufs):
    sweeps = Sweeps(wa_ref, wb_ref, bufs)
    sweeps.fill(r_ref, BASE, OWN // 4)
    for m, (name, then) in enumerate(sweeps.first_iteration(), 1):
        sweeps.batched(name, BASE + m, BASE + OWN - m, then)
    rows_done = {"s": 0, "f": 1, "w1": 1, "g1": 2, "w2": 2, "g2": 3, "w3": 3, "v": 4,
                 "p1": 4, "p2": 4, "d1": 5, "v2": 5, "d2": 6, "v3": 6, "b": 6}
    for name, row, at, count in handed():
        low = max(row, (BASE + rows_done[name]) * 8)
        high = min(row + count, (BASE + OWN - rows_done[name]) * 8)
        if low > row:
            out_ref[at:at + low - row, :] = jnp.zeros((low - row, 128), f32)
        out_ref[at + low - row:at + high - row, :] = sweeps.bufs[name][low:high, :]
        if high < row + count:
            rest = row + count - high
            out_ref[at + count - rest:at + count, :] = jnp.zeros((rest, 128), f32)


def middle_kernel(done_ref, lo_ref, hi_ref, wa_ref, wb_ref, ends_ref, out_ref, *bufs):
    widths, S = sdc_tables()
    h0, h1, h2 = widths
    sweeps = Sweeps(wa_ref, wb_ref, bufs, ends_ref)
    at_bottom, at_top = sweeps.at_ends()
    product, batched, pieces = sweeps.product, sweeps.batched, sweeps.pieces
    s_, f_, d1_, d2_, v3_, b_, w1_, w2_, w3_, g1_, g2_, p1_, p2_, v_, v2_, r_, lr_ = bufs
    b_[...] = jnp.zeros_like(b_)
    for name, row, at, count in handed():
        sweeps.bufs[name][row:row + count, :] = done_ref[at:at + count, :]
    sweeps.fill(lo_ref, PAD, HALO // 4)
    sweeps.fill(hi_ref, BASE + OWN, HALO // 4)

    for m, (name, then) in enumerate(sweeps.first_iteration(), 1):
        reach = 18 - m
        batched(name, BASE - reach, BASE + m, then)
        batched(name, BASE + OWN - m, BASE + OWN + reach, then)

    def seven(i, y):
        d1, d2, d3 = d1_[i, :], d2_[i, :], y - f_[i, :]
        w1_[i, :] = S[0][1] * d1 + S[0][2] * d2 + S[0][3] * d3
        p1_[i, :] = (S[1][1] - h1) * d1 + S[1][2] * d2 + S[1][3] * d3
        p2_[i, :] = S[2][1] * d1 + (S[2][2] - h2) * d2 + S[2][3] * d3

    rest = pieces(lambda i: v3_[i, :], BASE - 11, BASE + OWN + 11, seven, 12)

    def last_of_one(n):
        next(rest, None)

    def chain(reach, steps, addend, store, beside):
        runs = (OWN + 2 * reach) // 8
        base = (BASE - reach) * 8

        def rows(q, n):
            return pl.ds(base + q * 8 + n, 8, stride=runs * 8)

        def take(ref, n):
            return jnp.concatenate([ref[rows(q, n), :] for q in range(runs)], axis=0)

        sublane = lax.broadcasted_iota(jnp.int32, (8, 128), 0)

        def cut_one(rows, layer, ends):
            return cut(rows, layer % runs, ends & (sublane == layer // runs))

        value = take(s_, 0)
        for n in range(steps):
            beside(n)
            own, up, down = product(value)
            up = cut_one(up, reach - 1, at_bottom)
            down = cut_one(down, reach + OWN, at_top)
            up = jnp.concatenate([pltpu.roll(up[-8:], 1, 0), up[:-8]], axis=0)
            down = jnp.concatenate([down[8:], pltpu.roll(down[:8], 7, 0)], axis=0)
            y = own + up + down
            for q in range(runs):
                store(rows(q, n), value[q * 8:(q + 1) * 8], y[q * 8:(q + 1) * 8])
            if n < 7:
                value = (value + take(addend, n)) + TAU * y
        return value, rows, runs

    def keep_first(i, value, y):
        r_[i, :] = value
        lr_[i, :] = y

    chain(CHAIN1, 8, b_, keep_first, last_of_one)

    def eight(i, y):
        g1_[i, :] = y
        w2_[i, :] = w3_[i, :] + (h1 * y + p1_[i, :])

    def nine(i, y):
        g2_[i, :] = y
        w1_[i, :] = w2_[i, :] + (h2 * y + p2_[i, :])

    def eleven(i, y):
        v2_[i, :] = v_[i, :] + (h1 * y + p1_[i, :])

    def twelve(i, y):
        v3 = v2_[i, :] + (h2 * y + p2_[i, :])
        v3_[i, :] = v3
        b_[i, :] = v3 - (r_[i, :] + TAU * lr_[i, :])

    def first_value(i):
        value = r_[i, :] + (h0 * lr_[i, :] + w1_[i, :])
        w3_[i, :] = value
        return value

    for _ in pieces(first_value, BASE - 10, BASE + OWN + 10, eight):
        pass
    batched("w2", BASE - 9, BASE + OWN + 9, nine)
    batched("w1", BASE - 8, BASE + OWN + 8, sweeps.make_four("r", "lr"))
    batched("v", BASE - 7, BASE + OWN + 7, eleven)
    batched("v2", BASE - 6, BASE + OWN + 6, twelve)

    def keep_second(i, value, y):
        f_[i, :] = value

    def deliver(o, ref, t):
        for l in range(4):
            for q in range(OWN // 4):
                row = (BASE + 4 * q + l) * 8 + 2 * t
                out_ref[t, q, o * 8 + 2 * l:o * 8 + 2 * l + 2, :] = ref[row:row + 2, :]

    def ends(n):
        if n < 4:
            deliver(1, v3_, n)

    value, rows, runs = chain(CHAIN2, 7, b_, keep_second, ends)
    for q in range(runs):
        f_[rows(q, 7), :] = value[q * 8:(q + 1) * 8]
    for t in range(4):
        deliver(0, f_, t)


def vmem():
    return pl.BlockSpec(memory_space=pltpu.VMEM)


def smem():
    return pl.BlockSpec(memory_space=pltpu.SMEM)


def anywhere():
    return pl.BlockSpec(memory_space=pl.ANY)


def grant(mib):
    return pltpu.CompilerParams(vmem_limit_bytes=mib * 1024 * 1024)


def shards(basis, table, starts, volume_op, face_ops, neighbours):
    unit = lax.axis_index("tm") * 16 + lax.axis_index("zx")
    place = jnp.stack([unit, lax.axis_index("y")]).astype(jnp.int32).reshape(1, 2)

    sent, dt = pl.pallas_call(
        forward_kernel,
        out_shape=(
            jax.ShapeDtypeStruct((UNITS, 8, 128), f32),
            jax.ShapeDtypeStruct((2 * COLS, COLS), bf16),
        ),
        in_specs=[anywhere()] * 3,
        out_specs=(vmem(), vmem()),
        scratch_shapes=[
            pltpu.VMEM((2, 256, 128), f32),
            pltpu.VMEM((4, COLS), jnp.int32),
            pltpu.VMEM((2 * COLS, COLS), bf16),
            pltpu.SemaphoreType.DMA((3,)),
        ],
        name="forward",
    )(starts.reshape(2, 256, 128), neighbours, jnp.asarray(basis))
    wa, wb, ends = pl.pallas_call(
        prepare_kernel,
        out_shape=(
            jax.ShapeDtypeStruct((384, 256), bf16),
            jax.ShapeDtypeStruct((256, 256), bf16),
            jax.ShapeDtypeStruct((16, 128), f32),
        ),
        in_specs=[vmem(), vmem(), smem(), smem()],
        out_specs=(vmem(),) * 3,
        compiler_params=grant(8),
        cost_estimate=pl.CostEstimate(
            flops=2 * 10**9, bytes_accessed=4 * 10**6, transcendentals=0
        ),
        name="prepare",
    )(volume_op, face_ops, jnp.asarray(table), place)
    got = lax.all_to_all(sent, ("tm", "zx"), 0, 0, tiled=True).reshape(4, 16, 8, 128)
    got, wa, wb, ends = lax.optimization_barrier((got, wa, wb, ends))
    count = HALO // 4
    odd = lax.axis_index("y") % 2 == 1
    low, high = got[:, :count], got[:, 16 - count:]
    first = lax.ppermute(jnp.where(odd, low, high), "y", [(0, 1), (1, 0), (2, 3), (3, 2)])
    second = lax.ppermute(jnp.where(odd, high, low), "y", [(1, 2), (2, 1), (3, 0), (0, 3)])
    below, above = jnp.where(odd, first, second), jnp.where(odd, second, first)
    done = pl.pallas_call(
        inner_kernel,
        out_shape=jax.ShapeDtypeStruct((HANDED, 128), f32),
        in_specs=[vmem()] * 3,
        out_specs=vmem(),
        scratch_shapes=[pltpu.VMEM((LAYERS * 8, 128), f32)] * len(NAMES),
        compiler_params=grant(16),
        cost_estimate=pl.CostEstimate(
            flops=3 * 10**9, bytes_accessed=8 * 10**6, transcendentals=0
        ),
        name="inner",
    )(got, wa, wb)
    back = pl.pallas_call(
        middle_kernel,
        out_shape=jax.ShapeDtypeStruct((4, 16, 16, 128), f32),
        in_specs=[vmem()] * 6,
        out_specs=vmem(),
        scratch_shapes=[pltpu.VMEM((LAYERS * 8, 128), f32)] * len(NAMES),
        compiler_params=grant(16),
        name="sweeps",
    )(done, below, above, wa, wb, ends)
    home = lax.all_to_all(back.reshape(UNITS, 16, 128), ("tm", "zx"), 0, 0, tiled=True)
    new, end = pl.pallas_call(
        backward_kernel,
        out_shape=(jax.ShapeDtypeStruct((2, 256, 128), f32),) * 2,
        in_specs=[vmem()] * 2,
        out_specs=(anywhere(),) * 2,
        scratch_shapes=[
            pltpu.VMEM((2, 256, 128), f32),
            pltpu.VMEM((2, 256, 128), f32),
            pltpu.SemaphoreType.DMA((4,)),
        ],
        compiler_params=grant(8),
        name="backward",
    )(home, dt)
    return new.reshape(2, 64, 4, 128), end.reshape(2, 64, 4, 128)


def solution(mesh):
    finer = Mesh(mesh.devices.reshape(4, 4, 16), ("tm", "y", "zx"))
    basis, table = modes()
    placed = P("tm", None, ("y", "zx"), None)
    return jax.shard_map(
        functools.partial(shards, basis, table),
        mesh=finer,
        in_specs=(placed, P(), P(), P()),
        out_specs=(placed, placed),
        check_vma=False,
    )
```

```python
import functools
import math

import jax
import jax.numpy as jnp
import ml_dtypes
import numpy as np
from jax import lax
from jax.experimental import pallas as pl
from jax.experimental.pallas import tpu as pltpu
from jax.sharding import Mesh
from jax.sharding import PartitionSpec as P

PY, PZ = 8, 16
COLS = PY * PZ
UNITS = 64
SLICES = 8
OWN = 64
HALO = 20
WIN = OWN + 2 * HALO
PAD = 2
LAYERS = WIN + 2 * PAD
BASE = PAD + HALO
CHAIN1 = 16
CHAIN2 = 8
TAU = 0.25
f32, bf16 = jnp.float32, jnp.bfloat16


def lagrange_integral(points, which, lower, upper):
    coefficients = [1.0]
    divisor = 1.0
    for other in range(4):
        if other != which:
            product = [0.0] * (len(coefficients) + 1)
            for power in range(len(coefficients)):
                product[power + 1] = product[power + 1] + coefficients[power]
                product[power] = product[power] - coefficients[power] * points[other]
            coefficients = product
            divisor = divisor * (points[which] - points[other])
    integral = 0.0
    for power in range(len(coefficients)):
        integral = integral + coefficients[power] * (
            upper ** (power + 1) - lower ** (power + 1)
        ) / (power + 1)
    return integral / divisor


def sdc_tables():
    offset = 0.5 / math.sqrt(5.0)
    points = [0.0, 0.5 - offset, 0.5 + offset, 1.0]
    widths = [TAU * (points[m + 1] - points[m]) for m in range(3)]
    weights = [
        [float(TAU * lagrange_integral(points, j, points[m], points[m + 1])) for j in range(4)]
        for m in range(3)
    ]
    return widths, weights


def modes():
    pairs = [(ka, kb) for kb in range(1, PZ // 2) for ka in range(PY)]
    pairs += [(ka, kb) for kb in (0, PZ // 2) for ka in range(1, PY // 2)]
    single = [((0, 0), (PY // 2, 0)), ((0, PZ // 2), (PY // 2, PZ // 2))]
    places = np.arange(COLS)
    a, b = places // PZ, places % PZ

    def angle(k):
        return 2.0 * np.pi * (((k[0] * a * (PZ // PY) + k[1] * b) % PZ) / PZ)

    def turn(k):
        return 2.0 * np.pi * k[0] / PY, 2.0 * np.pi * k[1] / PZ

    basis = np.zeros((2 * UNITS, COLS))
    table = np.zeros((UNITS, 8))
    for u, k in enumerate(pairs):
        scale = math.sqrt(2.0 / COLS)
        basis[u] = scale * np.cos(angle(k))
        basis[UNITS + u] = scale * np.sin(angle(k))
        al, be = turn(k)
        table[u, :6] = [np.cos(al), np.cos(be), np.cos(al), np.cos(be), np.sin(al), np.sin(be)]
    for i, (k, other) in enumerate(single):
        u = len(pairs) + i
        scale = math.sqrt(1.0 / COLS)
        basis[u] = scale * np.cos(angle(k))
        basis[UNITS + u] = scale * np.cos(angle(other))
        al, be = turn(k)
        al2, be2 = turn(other)
        table[u, :6] = [np.cos(al), np.cos(be), np.cos(al2), np.cos(be2), 0.0, 0.0]
    basis = basis.astype(np.float32)
    high = basis.astype(ml_dtypes.bfloat16)
    low = (basis - high.astype(np.float32)).astype(ml_dtypes.bfloat16)
    return np.concatenate([high, low], axis=0), table.astype(np.float32)


def look_up(table, index):
    return jnp.take_along_axis(table, index, axis=1)


def split(x):
    high = x.astype(bf16)
    low = (x - high.astype(f32)).astype(bf16)
    return high, low


def forward_kernel(x_hbm, nb_hbm, basis_hbm, out_ref, dt_ref, x_ref, nb_ref, basis_ref, sems):
    copies = [
        pltpu.make_async_copy(src, dst, sems.at[i])
        for i, (src, dst) in enumerate(
            ((nb_hbm, nb_ref), (basis_hbm, basis_ref), (x_hbm, x_ref))
        )
    ]
    for copy in copies:
        copy.start()
    copies[0].wait()
    a1 = jnp.broadcast_to(nb_ref[1:2, :], (8, COLS))
    b1 = jnp.broadcast_to(nb_ref[3:4, :], (8, COLS))
    place = lax.broadcasted_iota(jnp.int32, (8, COLS), 1)
    times = lax.broadcasted_iota(jnp.int32, (8, COLS), 0)
    a2, b2 = look_up(a1, a1), look_up(b1, b1)
    a4, b4 = look_up(a2, a2), look_up(b2, b2)
    b8 = look_up(b4, b4)
    along = jnp.where(times & 1 == 1, a1, place)
    along = jnp.where(times & 2 == 2, look_up(a2, along), along)
    along = jnp.where(times & 4 == 4, look_up(a4, along), along)
    column = jnp.zeros((8, COLS), jnp.int32)
    for bit, table in ((1, b1), (2, b2), (4, b4), (8, b8)):
        column = jnp.where(place & bit == bit, look_up(table, column), column)
    column = jnp.where(place // PZ == times, look_up(along, column), 0)
    column = jnp.sum(column, axis=0, keepdims=True)
    row = lax.broadcasted_iota(jnp.int32, (COLS, COLS), 0)
    hit = jnp.broadcast_to(column, (COLS, COLS)) == row
    one_hot = jnp.where(hit, 1.0, 0.0).astype(bf16)
    copies[1].wait()
    dt = lax.dot_general(
        basis_ref[...], one_hot, (((1,), (1,)), ((), ())), preferred_element_type=f32
    ).astype(bf16)
    dt_ref[...] = dt
    copies[2].wait()
    parts = []
    for l in range(4):
        for s in range(2):
            parts.append(x_ref[s, pl.ds(l, 64, stride=4), :])
    high, low = split(jnp.concatenate(parts, axis=0))
    result = lax.dot_general(
        jnp.concatenate([dt[:128], dt[:128], dt[128:]], axis=1),
        jnp.concatenate([high, low, high], axis=1),
        (((1,), (1,)), ((), ())), preferred_element_type=f32,
    )
    left = lax.broadcasted_iota(jnp.int32, (UNITS, COLS), 1) < 64
    for k in range(4):
        even = result[:UNITS, k * 128:(k + 1) * 128]
        odd = result[UNITS:, k * 128:(k + 1) * 128]
        out_ref[:, 2 * k, :] = jnp.where(left, even, pltpu.roll(odd, 64, 1))
        out_ref[:, 2 * k + 1, :] = jnp.where(left, pltpu.roll(even, 64, 1), odd)


def backward_kernel(z_ref, dt_ref, new_hbm, end_hbm, new_ref, end_ref, sems):
    zero = jnp.zeros((UNITS, COLS), bf16)

    def weight(dt):
        top, bottom = dt[:UNITS], dt[UNITS:]
        return jnp.concatenate(
            [
                jnp.concatenate([top, zero], axis=1),
                jnp.concatenate([zero, top], axis=1),
                jnp.concatenate([bottom, zero], axis=1),
                jnp.concatenate([zero, bottom], axis=1),
            ],
            axis=0,
        )

    high_dt, low_dt = weight(dt_ref[0:128, :]), weight(dt_ref[128:256, :])
    weights = jnp.concatenate([high_dt, high_dt, low_dt], axis=0)
    copies = []
    for o, (ref, hbm) in enumerate(((new_ref, new_hbm), (end_ref, end_hbm))):
        rows = []
        for l in range(4):
            pair = 4 * o + l
            block = jnp.concatenate([z_ref[:, 2 * pair, :], z_ref[:, 2 * pair + 1, :]], axis=0)
            turned = block.T
            rows.append(jnp.concatenate([turned[:64], turned[64:]], axis=1))
        for half in range(2):
            part = slice(half * 32, half * 32 + 32)
            high, low = split(jnp.concatenate([row[part] for row in rows], axis=0))
            result = jnp.dot(
                jnp.concatenate([high, low, high], axis=1), weights, preferred_element_type=f32
            )
            for l in range(4):
                for s in range(2):
                    ref[s, pl.ds(half * 128 + l, 32, stride=4), :] = result[
                        l * 32:(l + 1) * 32, s * 128:(s + 1) * 128
                    ]
            lines = pl.ds(half * 128, 128)
            copies.append(
                pltpu.make_async_copy(
                    ref.at[:, lines], hbm.at[:, lines], sems.at[2 * o + half]
                )
            )
            copies[-1].start()
    for copy in copies:
        copy.wait()


def chunks(first, last, most=34):
    count = last - first
    size = -(-count // -(-count // most))
    size += size % 2
    return [(at, min(size, last - at)) for at in range(first, last, size)]


def prepare_kernel(vol_ref, face_ref, table_ref, place_ref, wa_ref, wb_ref, ends_ref):
    unit = place_ref[0, 0]
    fa, fb = face_ref[2] + face_ref[3], face_ref[4] + face_ref[5]
    ga, gb = face_ref[3] - face_ref[2], face_ref[5] - face_ref[4]
    vol = vol_ref[...]
    mcc = vol + table_ref[unit, 0] * fa + table_ref[unit, 1] * fb
    mss = vol + table_ref[unit, 2] * fa + table_ref[unit, 3] * fb
    mcs = table_ref[unit, 4] * ga + table_ref[unit, 5] * gb
    zero = jnp.zeros((64, 64), f32)

    def block(a, b, c, d):
        return jnp.concatenate(
            [jnp.concatenate([a, b], axis=1), jnp.concatenate([c, d], axis=1)], axis=0
        ).T

    m_high, m_low = split(block(mcc, mcs, -mcs, mss))
    f0_high, f0_low = split(block(face_ref[0], zero, zero, face_ref[0]))
    f1_high, f1_low = split(block(face_ref[1], zero, zero, face_ref[1]))
    both = jnp.concatenate([f1_high, m_high], axis=1)
    wa_ref[0:128, :] = both
    wa_ref[128:256, :] = both
    wa_ref[256:384, :] = jnp.concatenate([f1_low, m_low], axis=1)
    wb_ref[0:128, :] = jnp.concatenate([f0_high, f0_low], axis=1)
    wb_ref[128:256, :] = jnp.concatenate([f0_high, jnp.zeros_like(f0_low)], axis=1)
    ends_ref[0:8, :] = jnp.full((8, 128), jnp.where(place_ref[0, 1] == 0, 1.0, 0.0))
    ends_ref[8:16, :] = jnp.full((8, 128), jnp.where(place_ref[0, 1] == 3, 1.0, 0.0))


WHOLE = ("s", "b", "q0", "q1", "q2")
RIMS = ("f", "d1", "d2", "v3", "w1", "w2", "w3", "g1", "g2", "p1", "p2", "v", "v2")
NAMES = WHOLE + RIMS + ("r", "lr")
RIM = 8
HANDED = (len(WHOLE) * OWN + len(RIMS) * 2 * RIM) * 8


def handed():
    at = 0
    for name in WHOLE:
        yield name, BASE * 8, at, OWN * 8
        at += OWN * 8
    for name in RIMS:
        for first in (BASE, BASE + OWN - RIM):
            yield name, first * 8, at, RIM * 8
            at += RIM * 8


class Sweeps:
    def __init__(self, wa_ref, wb_ref, bufs, ends_ref=None):
        self.wa, self.wb, self.ends = wa_ref, wb_ref, ends_ref
        self.bufs = dict(zip(NAMES, bufs))

    def at_ends(self):
        return self.ends[0:8, :] > 0.5, self.ends[8:16, :] > 0.5

    def fill(self, ref, at, count):
        for t in range(4):
            for l in range(4):
                for q in range(count):
                    row = (at + 4 * q + l) * 8 + 2 * t
                    self.bufs["s"][row:row + 2, :] = ref[t, q, 2 * l:2 * l + 2, :]

    def product(self, x):
        high, low = split(x)
        acc = jnp.dot(
            jnp.concatenate([high, low, high], axis=1), self.wa[...],
            preferred_element_type=f32,
        )
        up = jnp.dot(
            jnp.concatenate([high, low], axis=1), self.wb[...], preferred_element_type=f32
        )
        return acc[:, 128:], up[:, :128] + up[:, 128:], acc[:, :128]

    def pieces(self, take, first, last, then, most=34):
        edge = None
        for at, n in chunks(first - 1, last + 1, most):
            own, up, down = self.product(take(slice(at * 8, (at + n) * 8)))
            if self.ends is not None:
                up = cut(up, BASE - 1 - at, self.at_ends()[0])
                down = cut(down, BASE + OWN - at, self.at_ends()[1])
            if edge is None:
                here = slice((at + 1) * 8, (at + n - 1) * 8)
                y = own[8:-8] + up[:-16] + down[16:]
            else:
                here = slice((at - 1) * 8, (at + n - 1) * 8)
                y = (
                    jnp.concatenate([edge[0], own[:-8]], axis=0)
                    + jnp.concatenate([edge[1], up[:-16]], axis=0)
                    + down
                )
            edge = own[-8:], up[-16:]
            then(here, y)
            yield

    def batched(self, name, first, last, then):
        src = self.bufs[name]
        for _ in self.pieces(lambda i: src[i, :], first, last, then):
            pass

    def make_four(self, start, zeroth):
        S = sdc_tables()[1]
        h1, h2 = sdc_tables()[0][1:]
        B = self.bufs

        def four(i, y):
            g0, g1, g2 = B[zeroth][i, :], B["g1"][i, :], B["g2"][i, :]
            B["v"][i, :] = B[start][i, :] + (
                S[0][0] * g0 + S[0][1] * g1 + S[0][2] * g2 + S[0][3] * y
            )
            B["p1"][i, :] = S[1][0] * g0 + (S[1][1] - h1) * g1 + S[1][2] * g2 + S[1][3] * y
            B["p2"][i, :] = S[2][0] * g0 + S[2][1] * g1 + (S[2][2] - h2) * g2 + S[2][3] * y

        return four

    def first_iteration(self):
        (h0, h1, h2), S = sdc_tables()
        B = self.bufs

        def one(i, y):
            B["f"][i, :] = y
            B["w1"][i, :] = B["s"][i, :] + h0 * y

        def two(i, y):
            B["g1"][i, :] = y
            B["w2"][i, :] = B["w1"][i, :] + h1 * y

        def three(i, y):
            B["g2"][i, :] = y
            B["w3"][i, :] = B["w2"][i, :] + h2 * y

        def five(i, y):
            B["d1"][i, :] = y - B["f"][i, :]
            B["v2"][i, :] = B["v"][i, :] + (h1 * y + B["p1"][i, :])

        def six(i, y):
            B["d2"][i, :] = y - B["f"][i, :]
            v3 = B["v2"][i, :] + (h2 * y + B["p2"][i, :])
            B["v3"][i, :] = v3
            B["b"][i, :] = v3 - (B["s"][i, :] + TAU * B["f"][i, :])

        def seven(i, y):
            d1, d2, d3 = B["d1"][i, :], B["d2"][i, :], y - B["f"][i, :]
            B["q0"][i, :] = S[0][1] * d1 + S[0][2] * d2 + S[0][3] * d3
            B["q1"][i, :] = (S[1][1] - h1) * d1 + S[1][2] * d2 + S[1][3] * d3
            B["q2"][i, :] = S[2][1] * d1 + (S[2][2] - h2) * d2 + S[2][3] * d3

        return (
            ("s", one), ("w1", two), ("w2", three), ("w3", self.make_four("s", "f")),
            ("v", five), ("v2", six), ("v3", seven),
        )


def cut(rows, i, where):
    if not 0 <= i < rows.shape[0] // 8:
        return rows
    part = jnp.where(where, 0.0, rows[i * 8:i * 8 + 8])
    around = [rows[:i * 8], part, rows[i * 8 + 8:]]
    return jnp.concatenate([r for r in around if r.shape[0]], axis=0)


def inner_kernel(r_ref, wa_ref, wb_ref, out_ref, *bufs):
    sweeps = Sweeps(wa_ref, wb_ref, bufs)
    sweeps.fill(r_ref, BASE, OWN // 4)
    for m, (name, then) in enumerate(sweeps.first_iteration(), 1):
        sweeps.batched(name, BASE + m, BASE + OWN - m, then)
    rows_done = {"s": 0, "f": 1, "w1": 1, "g1": 2, "w2": 2, "g2": 3, "w3": 3, "v": 4,
                 "p1": 4, "p2": 4, "d1": 5, "v2": 5, "d2": 6, "v3": 6, "b": 6,
                 "q0": 7, "q1": 7, "q2": 7}
    for name, row, at, count in handed():
        low = max(row, (BASE + rows_done[name]) * 8)
        high = min(row + count, (BASE + OWN - rows_done[name]) * 8)
        if low > row:
            out_ref[at:at + low - row, :] = jnp.zeros((low - row, 128), f32)
        out_ref[at + low - row:at + high - row, :] = sweeps.bufs[name][low:high, :]
        if high < row + count:
            rest = row + count - high
            out_ref[at + count - rest:at + count, :] = jnp.zeros((rest, 128), f32)


def middle_kernel(done_ref, lo_ref, hi_ref, wa_ref, wb_ref, ends_ref, out_ref, *bufs):
    widths, S = sdc_tables()
    h0, h1, h2 = widths
    sweeps = Sweeps(wa_ref, wb_ref, bufs, ends_ref)
    at_bottom, at_top = sweeps.at_ends()
    product, batched, pieces = sweeps.product, sweeps.batched, sweeps.pieces
    s_, b_, q0_, q1_, q2_, f_ = bufs[:6]
    v3_, w1_, w2_, w3_, g1_, g2_, p1_, p2_, v_, v2_, r_, lr_ = bufs[8:]
    b_[...] = jnp.zeros_like(b_)
    for name, row, at, count in handed():
        sweeps.bufs[name][row:row + count, :] = done_ref[at:at + count, :]
    sweeps.fill(lo_ref, PAD, HALO // 4)
    sweeps.fill(hi_ref, BASE + OWN, HALO // 4)

    steps = sweeps.first_iteration()
    for m, (name, then) in enumerate(steps, 1):
        if m < len(steps):
            batched(name, BASE - 18 + m, BASE + m, then)
            batched(name, BASE + OWN - m, BASE + OWN + 18 - m, then)

    def last_of_one(n):
        m = len(steps)
        if n == 1:
            batched(steps[-1][0], BASE - 18 + m, BASE + m, steps[-1][1])
        if n == 3:
            batched(steps[-1][0], BASE + OWN - m, BASE + OWN + 18 - m, steps[-1][1])

    def chain(reach, steps, addend, store, beside):
        runs = (OWN + 2 * reach) // 8
        base = (BASE - reach) * 8

        def rows(q, n):
            return pl.ds(base + q * 8 + n, 8, stride=runs * 8)

        def take(ref, n):
            return jnp.concatenate([ref[rows(q, n), :] for q in range(runs)], axis=0)

        sublane = lax.broadcasted_iota(jnp.int32, (8, 128), 0)

        def cut_one(rows, layer, ends):
            return cut(rows, layer % runs, ends & (sublane == layer // runs))

        value = take(s_, 0)
        for n in range(steps):
            beside(n)
            own, up, down = product(value)
            up = cut_one(up, reach - 1, at_bottom)
            down = cut_one(down, reach + OWN, at_top)
            up = jnp.concatenate([pltpu.roll(up[-8:], 1, 0), up[:-8]], axis=0)
            down = jnp.concatenate([down[8:], pltpu.roll(down[:8], 7, 0)], axis=0)
            y = own + up + down
            for q in range(runs):
                store(rows(q, n), value[q * 8:(q + 1) * 8], y[q * 8:(q + 1) * 8])
            if n < 7:
                value = (value + take(addend, n)) + TAU * y
        return value, rows, runs

    def keep_first(i, value, y):
        r_[i, :] = value
        lr_[i, :] = y

    chain(CHAIN1, 8, b_, keep_first, last_of_one)

    def eight(i, y):
        g1_[i, :] = y
        w2_[i, :] = w3_[i, :] + (h1 * y + q1_[i, :])

    def nine(i, y):
        g2_[i, :] = y
        w1_[i, :] = w2_[i, :] + (h2 * y + q2_[i, :])

    def eleven(i, y):
        v2_[i, :] = v_[i, :] + (h1 * y + p1_[i, :])

    def twelve(i, y):
        v3 = v2_[i, :] + (h2 * y + p2_[i, :])
        v3_[i, :] = v3
        b_[i, :] = v3 - (r_[i, :] + TAU * lr_[i, :])

    def first_value(i):
        value = r_[i, :] + (h0 * lr_[i, :] + q0_[i, :])
        w3_[i, :] = value
        return value

    for _ in pieces(first_value, BASE - 10, BASE + OWN + 10, eight):
        pass
    batched("w2", BASE - 9, BASE + OWN + 9, nine)
    batched("w1", BASE - 8, BASE + OWN + 8, sweeps.make_four("r", "lr"))
    batched("v", BASE - 7, BASE + OWN + 7, eleven)
    batched("v2", BASE - 6, BASE + OWN + 6, twelve)

    def keep_second(i, value, y):
        f_[i, :] = value

    def deliver(o, ref, t):
        for l in range(4):
            for q in range(OWN // 4):
                row = (BASE + 4 * q + l) * 8 + 2 * t
                out_ref[t, q, o * 8 + 2 * l:o * 8 + 2 * l + 2, :] = ref[row:row + 2, :]

    def ends(n):
        if n < 4:
            deliver(1, v3_, n)

    value, rows, runs = chain(CHAIN2, 7, b_, keep_second, ends)
    for q in range(runs):
        f_[rows(q, 7), :] = value[q * 8:(q + 1) * 8]
    for t in range(4):
        deliver(0, f_, t)


def vmem():
    return pl.BlockSpec(memory_space=pltpu.VMEM)


def smem():
    return pl.BlockSpec(memory_space=pltpu.SMEM)


def anywhere():
    return pl.BlockSpec(memory_space=pl.ANY)


def grant(mib):
    return pltpu.CompilerParams(vmem_limit_bytes=mib * 1024 * 1024)


def shards(basis, table, starts, volume_op, face_ops, neighbours):
    unit = lax.axis_index("tm") * 16 + lax.axis_index("zx")
    place = jnp.stack([unit, lax.axis_index("y")]).astype(jnp.int32).reshape(1, 2)

    sent, dt = pl.pallas_call(
        forward_kernel,
        out_shape=(
            jax.ShapeDtypeStruct((UNITS, 8, 128), f32),
            jax.ShapeDtypeStruct((2 * COLS, COLS), bf16),
        ),
        in_specs=[anywhere()] * 3,
        out_specs=(vmem(), vmem()),
        scratch_shapes=[
            pltpu.VMEM((2, 256, 128), f32),
            pltpu.VMEM((4, COLS), jnp.int32),
            pltpu.VMEM((2 * COLS, COLS), bf16),
            pltpu.SemaphoreType.DMA((3,)),
        ],
        name="forward",
    )(starts.reshape(2, 256, 128), neighbours, jnp.asarray(basis))
    wa, wb, ends = pl.pallas_call(
        prepare_kernel,
        out_shape=(
            jax.ShapeDtypeStruct((384, 256), bf16),
            jax.ShapeDtypeStruct((256, 256), bf16),
            jax.ShapeDtypeStruct((16, 128), f32),
        ),
        in_specs=[vmem(), vmem(), smem(), smem()],
        out_specs=(vmem(),) * 3,
        compiler_params=grant(8),
        cost_estimate=pl.CostEstimate(
            flops=2 * 10**9, bytes_accessed=4 * 10**6, transcendentals=0
        ),
        name="prepare",
    )(volume_op, face_ops, jnp.asarray(table), place)
    got = lax.all_to_all(sent, ("tm", "zx"), 0, 0, tiled=True).reshape(4, 16, 8, 128)
    got, wa, wb, ends = lax.optimization_barrier((got, wa, wb, ends))
    count = HALO // 4
    odd = lax.axis_index("y") % 2 == 1
    low, high = got[:, :count], got[:, 16 - count:]
    first = lax.ppermute(jnp.where(odd, low, high), "y", [(0, 1), (1, 0), (2, 3), (3, 2)])
    second = lax.ppermute(jnp.where(odd, high, low), "y", [(1, 2), (2, 1), (3, 0), (0, 3)])
    below, above = jnp.where(odd, first, second), jnp.where(odd, second, first)
    done = pl.pallas_call(
        inner_kernel,
        out_shape=jax.ShapeDtypeStruct((HANDED, 128), f32),
        in_specs=[vmem()] * 3,
        out_specs=vmem(),
        scratch_shapes=[pltpu.VMEM((LAYERS * 8, 128), f32)] * len(NAMES),
        compiler_params=grant(16),
        cost_estimate=pl.CostEstimate(
            flops=3 * 10**9, bytes_accessed=8 * 10**6, transcendentals=0
        ),
        name="inner",
    )(got, wa, wb)
    back = pl.pallas_call(
        middle_kernel,
        out_shape=jax.ShapeDtypeStruct((4, 16, 16, 128), f32),
        in_specs=[vmem()] * 6,
        out_specs=vmem(),
        scratch_shapes=[pltpu.VMEM((LAYERS * 8, 128), f32)] * len(NAMES),
        compiler_params=grant(16),
        name="sweeps",
    )(done, below, above, wa, wb, ends)
    home = lax.all_to_all(back.reshape(UNITS, 16, 128), ("tm", "zx"), 0, 0, tiled=True)
    new, end = pl.pallas_call(
        backward_kernel,
        out_shape=(jax.ShapeDtypeStruct((2, 256, 128), f32),) * 2,
        in_specs=[vmem()] * 2,
        out_specs=(anywhere(),) * 2,
        scratch_shapes=[
            pltpu.VMEM((2, 256, 128), f32),
            pltpu.VMEM((2, 256, 128), f32),
            pltpu.SemaphoreType.DMA((4,)),
        ],
        compiler_params=grant(8),
        name="backward",
    )(home, dt)
    return new.reshape(2, 64, 4, 128), end.reshape(2, 64, 4, 128)


def solution(mesh):
    finer = Mesh(mesh.devices.reshape(4, 4, 16), ("tm", "y", "zx"))
    basis, table = modes()
    placed = P("tm", None, ("y", "zx"), None)
    return jax.shard_map(
        functools.partial(shards, basis, table),
        mesh=finer,
        in_specs=(placed, P(), P(), P()),
        out_specs=(placed, placed),
        check_vma=False,
    )
```

```python
import functools
import math

import jax
import jax.numpy as jnp
import ml_dtypes
import numpy as np
from jax import lax
from jax.experimental import pallas as pl
from jax.experimental.pallas import tpu as pltpu
from jax.sharding import Mesh
from jax.sharding import PartitionSpec as P

PY, PZ = 8, 16
COLS = PY * PZ
UNITS = 64
SLICES = 8
OWN = 64
HALO = 20
WIN = OWN + 2 * HALO
PAD = 2
LAYERS = WIN + 2 * PAD
BASE = PAD + HALO
CHAIN1 = 16
CHAIN2 = 8
TAU = 0.25
f32, bf16 = jnp.float32, jnp.bfloat16


def lagrange_integral(points, which, lower, upper):
    coefficients = [1.0]
    divisor = 1.0
    for other in range(4):
        if other != which:
            product = [0.0] * (len(coefficients) + 1)
            for power in range(len(coefficients)):
                product[power + 1] = product[power + 1] + coefficients[power]
                product[power] = product[power] - coefficients[power] * points[other]
            coefficients = product
            divisor = divisor * (points[which] - points[other])
    integral = 0.0
    for power in range(len(coefficients)):
        integral = integral + coefficients[power] * (
            upper ** (power + 1) - lower ** (power + 1)
        ) / (power + 1)
    return integral / divisor


def sdc_tables():
    offset = 0.5 / math.sqrt(5.0)
    points = [0.0, 0.5 - offset, 0.5 + offset, 1.0]
    widths = [TAU * (points[m + 1] - points[m]) for m in range(3)]
    weights = [
        [float(TAU * lagrange_integral(points, j, points[m], points[m + 1])) for j in range(4)]
        for m in range(3)
    ]
    return widths, weights


def modes():
    pairs = [(ka, kb) for kb in range(1, PZ // 2) for ka in range(PY)]
    pairs += [(ka, kb) for kb in (0, PZ // 2) for ka in range(1, PY // 2)]
    single = [((0, 0), (PY // 2, 0)), ((0, PZ // 2), (PY // 2, PZ // 2))]
    places = np.arange(COLS)
    a, b = places // PZ, places % PZ

    def angle(k):
        return 2.0 * np.pi * (((k[0] * a * (PZ // PY) + k[1] * b) % PZ) / PZ)

    def turn(k):
        return 2.0 * np.pi * k[0] / PY, 2.0 * np.pi * k[1] / PZ

    basis = np.zeros((2 * UNITS, COLS))
    table = np.zeros((UNITS, 8))
    for u, k in enumerate(pairs):
        scale = math.sqrt(2.0 / COLS)
        basis[u] = scale * np.cos(angle(k))
        basis[UNITS + u] = scale * np.sin(angle(k))
        al, be = turn(k)
        table[u, :6] = [np.cos(al), np.cos(be), np.cos(al), np.cos(be), np.sin(al), np.sin(be)]
    for i, (k, other) in enumerate(single):
        u = len(pairs) + i
        scale = math.sqrt(1.0 / COLS)
        basis[u] = scale * np.cos(angle(k))
        basis[UNITS + u] = scale * np.cos(angle(other))
        al, be = turn(k)
        al2, be2 = turn(other)
        table[u, :6] = [np.cos(al), np.cos(be), np.cos(al2), np.cos(be2), 0.0, 0.0]
    basis = basis.astype(np.float32)
    high = basis.astype(ml_dtypes.bfloat16)
    low = (basis - high.astype(np.float32)).astype(ml_dtypes.bfloat16)
    return np.concatenate([high, low], axis=0), table.astype(np.float32)


def look_up(table, index):
    return jnp.take_along_axis(table, index, axis=1)


def split(x):
    high = x.astype(bf16)
    low = (x - high.astype(f32)).astype(bf16)
    return high, low


def forward_kernel(x_hbm, nb_hbm, basis_hbm, out_ref, dt_ref, x_ref, nb_ref, basis_ref, sems):
    copies = [
        pltpu.make_async_copy(src, dst, sems.at[i])
        for i, (src, dst) in enumerate(
            ((nb_hbm, nb_ref), (basis_hbm, basis_ref), (x_hbm, x_ref))
        )
    ]
    for copy in copies:
        copy.start()
    copies[0].wait()
    a1 = jnp.broadcast_to(nb_ref[1:2, :], (8, COLS))
    b1 = jnp.broadcast_to(nb_ref[3:4, :], (8, COLS))
    place = lax.broadcasted_iota(jnp.int32, (8, COLS), 1)
    times = lax.broadcasted_iota(jnp.int32, (8, COLS), 0)
    a2, b2 = look_up(a1, a1), look_up(b1, b1)
    a4, b4 = look_up(a2, a2), look_up(b2, b2)
    b8 = look_up(b4, b4)
    along = jnp.where(times & 1 == 1, a1, place)
    along = jnp.where(times & 2 == 2, look_up(a2, along), along)
    along = jnp.where(times & 4 == 4, look_up(a4, along), along)
    column = jnp.zeros((8, COLS), jnp.int32)
    for bit, table in ((1, b1), (2, b2), (4, b4), (8, b8)):
        column = jnp.where(place & bit == bit, look_up(table, column), column)
    column = jnp.where(place // PZ == times, look_up(along, column), 0)
    column = jnp.sum(column, axis=0, keepdims=True)
    row = lax.broadcasted_iota(jnp.int32, (COLS, COLS), 0)
    hit = jnp.broadcast_to(column, (COLS, COLS)) == row
    one_hot = jnp.where(hit, 1.0, 0.0).astype(bf16)
    copies[1].wait()
    dt = lax.dot_general(
        basis_ref[...], one_hot, (((1,), (1,)), ((), ())), preferred_element_type=f32
    ).astype(bf16)
    dt_ref[...] = dt
    copies[2].wait()
    parts = []
    for l in range(4):
        for s in range(2):
            parts.append(x_ref[s, pl.ds(l, 64, stride=4), :])
    high, low = split(jnp.concatenate(parts, axis=0))
    result = lax.dot_general(
        jnp.concatenate([dt[:128], dt[:128], dt[128:]], axis=1),
        jnp.concatenate([high, low, high], axis=1),
        (((1,), (1,)), ((), ())), preferred_element_type=f32,
    )
    left = lax.broadcasted_iota(jnp.int32, (UNITS, COLS), 1) < 64
    for k in range(4):
        even = result[:UNITS, k * 128:(k + 1) * 128]
        odd = result[UNITS:, k * 128:(k + 1) * 128]
        out_ref[:, 2 * k, :] = jnp.where(left, even, pltpu.roll(odd, 64, 1))
        out_ref[:, 2 * k + 1, :] = jnp.where(left, pltpu.roll(even, 64, 1), odd)


def backward_kernel(z_ref, wt_ref, new_hbm, end_hbm, new_ref, end_ref, sems):
    copies = []
    for o, (ref, hbm) in enumerate(((new_ref, new_hbm), (end_ref, end_hbm))):
        rows = []
        for l in range(4):
            pair = 4 * o + l
            block = jnp.concatenate([z_ref[:, 2 * pair, :], z_ref[:, 2 * pair + 1, :]], axis=0)
            turned = block.T
            rows.append(jnp.concatenate([turned[:64], turned[64:]], axis=1))
        for half in range(2):
            part = slice(half * 32, half * 32 + 32)
            high, low = split(jnp.concatenate([row[part] for row in rows], axis=0))
            result = jnp.dot(
                jnp.concatenate([high, low, high], axis=1), wt_ref[...],
                preferred_element_type=f32,
            )
            for l in range(4):
                for s in range(2):
                    ref[s, pl.ds(half * 128 + l, 32, stride=4), :] = result[
                        l * 32:(l + 1) * 32, s * 128:(s + 1) * 128
                    ]
            lines = pl.ds(half * 128, 128)
            copies.append(
                pltpu.make_async_copy(
                    ref.at[:, lines], hbm.at[:, lines], sems.at[2 * o + half]
                )
            )
            copies[-1].start()
    for copy in copies:
        copy.wait()


def chunks(first, last, most=34):
    count = last - first
    size = -(-count // -(-count // most))
    size += size % 2
    return [(at, min(size, last - at)) for at in range(first, last, size)]


def prepare_kernel(
    vol_ref, face_ref, dt_ref, table_ref, place_ref, wa_ref, wb_ref, ends_ref, wt_ref
):
    unit = place_ref[0, 0]
    fa, fb = face_ref[2] + face_ref[3], face_ref[4] + face_ref[5]
    ga, gb = face_ref[3] - face_ref[2], face_ref[5] - face_ref[4]
    vol = vol_ref[...]
    mcc = vol + table_ref[unit, 0] * fa + table_ref[unit, 1] * fb
    mss = vol + table_ref[unit, 2] * fa + table_ref[unit, 3] * fb
    mcs = table_ref[unit, 4] * ga + table_ref[unit, 5] * gb
    zero = jnp.zeros((64, 64), f32)

    def block(a, b, c, d):
        return jnp.concatenate(
            [jnp.concatenate([a, b], axis=1), jnp.concatenate([c, d], axis=1)], axis=0
        ).T

    m_high, m_low = split(block(mcc, mcs, -mcs, mss))
    f0_high, f0_low = split(block(face_ref[0], zero, zero, face_ref[0]))
    f1_high, f1_low = split(block(face_ref[1], zero, zero, face_ref[1]))
    both = jnp.concatenate([f1_high, m_high], axis=1)
    wa_ref[0:128, :] = both
    wa_ref[128:256, :] = both
    wa_ref[256:384, :] = jnp.concatenate([f1_low, m_low], axis=1)
    wb_ref[0:128, :] = jnp.concatenate([f0_high, f0_low], axis=1)
    wb_ref[128:256, :] = jnp.concatenate([f0_high, jnp.zeros_like(f0_low)], axis=1)
    blank = jnp.zeros((UNITS, COLS), bf16)
    for i, first in enumerate((0, 0, COLS)):
        for part in range(2):
            dt = dt_ref[first + part * UNITS:first + (part + 1) * UNITS, :]
            at = i * 2 * COLS + part * COLS
            wt_ref[at:at + UNITS, :] = jnp.concatenate([dt, blank], axis=1)
            wt_ref[at + UNITS:at + COLS, :] = jnp.concatenate([blank, dt], axis=1)
    ends_ref[0:8, :] = jnp.full((8, 128), jnp.where(place_ref[0, 1] == 0, 1.0, 0.0))
    ends_ref[8:16, :] = jnp.full((8, 128), jnp.where(place_ref[0, 1] == 3, 1.0, 0.0))


WHOLE = ("s", "b", "q0", "q1", "q2")
RIMS = ("f", "d1", "d2", "v3", "w1", "w2", "w3", "g1", "g2", "p1", "p2", "v", "v2")
NAMES = WHOLE + RIMS + ("r", "lr")
RIM = 8
REACH = (5, 4, 4, 3)
SLABS = [(t, q) for t in range(4) for q in range(REACH[t])]
HANDED = (len(WHOLE) * OWN + len(RIMS) * 2 * RIM) * 8


def handed():
    at = 0
    for name in WHOLE:
        yield name, BASE * 8, at, OWN * 8
        at += OWN * 8
    for name in RIMS:
        for first in (BASE, BASE + OWN - RIM):
            yield name, first * 8, at, RIM * 8
            at += RIM * 8


class Sweeps:
    def __init__(self, wa_ref, wb_ref, bufs, ends_ref=None):
        self.wa, self.wb, self.ends = wa_ref, wb_ref, ends_ref
        self.bufs = dict(zip(NAMES, bufs))

    def at_ends(self):
        return self.ends[0:8, :] > 0.5, self.ends[8:16, :] > 0.5

    def fill(self, part, places):
        for i, (t, at) in enumerate(places):
            for l in range(4):
                row = (at + l) * 8 + 2 * t
                self.bufs["s"][row:row + 2, :] = part(i)[2 * l:2 * l + 2, :]

    def product(self, x):
        high, low = split(x)
        acc = jnp.dot(
            jnp.concatenate([high, low, high], axis=1), self.wa[...],
            preferred_element_type=f32,
        )
        up = jnp.dot(
            jnp.concatenate([high, low], axis=1), self.wb[...], preferred_element_type=f32
        )
        return acc[:, 128:], up[:, :128] + up[:, 128:], acc[:, :128]

    def pieces(self, take, first, last, then, most=34):
        edge = None
        for at, n in chunks(first - 1, last + 1, most):
            own, up, down = self.product(take(slice(at * 8, (at + n) * 8)))
            if self.ends is not None:
                up = cut(up, BASE - 1 - at, self.at_ends()[0])
                down = cut(down, BASE + OWN - at, self.at_ends()[1])
            if edge is None:
                here = slice((at + 1) * 8, (at + n - 1) * 8)
                y = own[8:-8] + up[:-16] + down[16:]
            else:
                here = slice((at - 1) * 8, (at + n - 1) * 8)
                y = (
                    jnp.concatenate([edge[0], own[:-8]], axis=0)
                    + jnp.concatenate([edge[1], up[:-16]], axis=0)
                    + down
                )
            edge = own[-8:], up[-16:]
            then(here, y)
            yield

    def batched(self, name, first, last, then):
        src = self.bufs[name]
        for _ in self.pieces(lambda i: src[i, :], first, last, then):
            pass

    def make_four(self, start, zeroth):
        S = sdc_tables()[1]
        h1, h2 = sdc_tables()[0][1:]
        B = self.bufs

        def four(i, y):
            g0, g1, g2 = B[zeroth][i, :], B["g1"][i, :], B["g2"][i, :]
            B["v"][i, :] = B[start][i, :] + (
                S[0][0] * g0 + S[0][1] * g1 + S[0][2] * g2 + S[0][3] * y
            )
            B["p1"][i, :] = S[1][0] * g0 + (S[1][1] - h1) * g1 + S[1][2] * g2 + S[1][3] * y
            B["p2"][i, :] = S[2][0] * g0 + S[2][1] * g1 + (S[2][2] - h2) * g2 + S[2][3] * y

        return four

    def first_iteration(self):
        (h0, h1, h2), S = sdc_tables()
        B = self.bufs

        def one(i, y):
            B["f"][i, :] = y
            B["w1"][i, :] = B["s"][i, :] + h0 * y

        def two(i, y):
            B["g1"][i, :] = y
            B["w2"][i, :] = B["w1"][i, :] + h1 * y

        def three(i, y):
            B["g2"][i, :] = y
            B["w3"][i, :] = B["w2"][i, :] + h2 * y

        def five(i, y):
            B["d1"][i, :] = y - B["f"][i, :]
            B["v2"][i, :] = B["v"][i, :] + (h1 * y + B["p1"][i, :])

        def six(i, y):
            B["d2"][i, :] = y - B["f"][i, :]
            v3 = B["v2"][i, :] + (h2 * y + B["p2"][i, :])
            B["v3"][i, :] = v3
            B["b"][i, :] = v3 - (B["s"][i, :] + TAU * B["f"][i, :])

        def seven(i, y):
            d1, d2, d3 = B["d1"][i, :], B["d2"][i, :], y - B["f"][i, :]
            B["q0"][i, :] = S[0][1] * d1 + S[0][2] * d2 + S[0][3] * d3
            B["q1"][i, :] = (S[1][1] - h1) * d1 + S[1][2] * d2 + S[1][3] * d3
            B["q2"][i, :] = S[2][1] * d1 + (S[2][2] - h2) * d2 + S[2][3] * d3

        return (
            ("s", one), ("w1", two), ("w2", three), ("w3", self.make_four("s", "f")),
            ("v", five), ("v2", six), ("v3", seven),
        )


def cut(rows, i, where):
    if not 0 <= i < rows.shape[0] // 8:
        return rows
    part = jnp.where(where, 0.0, rows[i * 8:i * 8 + 8])
    around = [rows[:i * 8], part, rows[i * 8 + 8:]]
    return jnp.concatenate([r for r in around if r.shape[0]], axis=0)


def inner_kernel(r_ref, wa_ref, wb_ref, out_ref, *bufs):
    sweeps = Sweeps(wa_ref, wb_ref, bufs)
    own = [(t, BASE + 4 * q) for t in range(4) for q in range(OWN // 4)]
    sweeps.fill(lambda i: r_ref.at[i // 16, i % 16], own)
    for m, (name, then) in enumerate(sweeps.first_iteration(), 1):
        sweeps.batched(name, BASE + m, BASE + OWN - m, then)
    rows_done = {"s": 0, "f": 1, "w1": 1, "g1": 2, "w2": 2, "g2": 3, "w3": 3, "v": 4,
                 "p1": 4, "p2": 4, "d1": 5, "v2": 5, "d2": 6, "v3": 6, "b": 6,
                 "q0": 7, "q1": 7, "q2": 7}
    for name, row, at, count in handed():
        low = max(row, (BASE + rows_done[name]) * 8)
        high = min(row + count, (BASE + OWN - rows_done[name]) * 8)
        if low > row:
            out_ref[at:at + low - row, :] = jnp.zeros((low - row, 128), f32)
        out_ref[at + low - row:at + high - row, :] = sweeps.bufs[name][low:high, :]
        if high < row + count:
            rest = row + count - high
            out_ref[at + count - rest:at + count, :] = jnp.zeros((rest, 128), f32)


def middle_kernel(done_ref, lo_ref, hi_ref, wa_ref, wb_ref, ends_ref, out_ref, *bufs):
    widths, S = sdc_tables()
    h0, h1, h2 = widths
    sweeps = Sweeps(wa_ref, wb_ref, bufs, ends_ref)
    at_bottom, at_top = sweeps.at_ends()
    product, batched, pieces = sweeps.product, sweeps.batched, sweeps.pieces
    s_, b_, q0_, q1_, q2_, f_ = bufs[:6]
    v3_, w1_, w2_, w3_, g1_, g2_, p1_, p2_, v_, v2_, r_, lr_ = bufs[8:]
    b_[...] = jnp.zeros_like(b_)
    for name, row, at, count in handed():
        sweeps.bufs[name][row:row + count, :] = done_ref[at:at + count, :]
    for at in (0, BASE + OWN):
        s_[at * 8:(at + BASE) * 8, :] = jnp.zeros((BASE * 8, 128), f32)
    sweeps.fill(lambda i: lo_ref.at[i], [(t, BASE - 4 * (REACH[t] - q)) for t, q in SLABS])
    sweeps.fill(lambda i: hi_ref.at[i], [(t, BASE + OWN + 4 * q) for t, q in SLABS])

    steps = sweeps.first_iteration()
    for m, (name, then) in enumerate(steps, 1):
        if m < len(steps):
            batched(name, BASE - 18 + m, BASE + m, then)
            batched(name, BASE + OWN - m, BASE + OWN + 18 - m, then)

    def last_of_one(n):
        m = len(steps)
        if n == 1:
            batched(steps[-1][0], BASE - 18 + m, BASE + m, steps[-1][1])
        if n == 3:
            batched(steps[-1][0], BASE + OWN - m, BASE + OWN + 18 - m, steps[-1][1])

    def chain(reach, steps, addend, store, beside):
        runs = (OWN + 2 * reach) // 8
        base = (BASE - reach) * 8

        def rows(q, n):
            return pl.ds(base + q * 8 + n, 8, stride=runs * 8)

        def take(ref, n):
            return jnp.concatenate([ref[rows(q, n), :] for q in range(runs)], axis=0)

        sublane = lax.broadcasted_iota(jnp.int32, (8, 128), 0)

        def cut_one(rows, layer, ends):
            return cut(rows, layer % runs, ends & (sublane == layer // runs))

        value = take(s_, 0)
        for n in range(steps):
            beside(n)
            own, up, down = product(value)
            up = cut_one(up, reach - 1, at_bottom)
            down = cut_one(down, reach + OWN, at_top)
            up = jnp.concatenate([pltpu.roll(up[-8:], 1, 0), up[:-8]], axis=0)
            down = jnp.concatenate([down[8:], pltpu.roll(down[:8], 7, 0)], axis=0)
            y = own + up + down
            store(n, rows, runs, value, y)
            if n < 7:
                value = (value + take(addend, n)) + TAU * y
        return value, rows, runs

    def keep_first(n, rows, runs, value, y):
        here = slice(n * runs * 8, (n + 1) * runs * 8)
        v_[here, :] = value
        w1_[here, :] = y

    chain(CHAIN1, 8, b_, keep_first, last_of_one)

    runs = (OWN + 2 * CHAIN1) // 8
    for src, ref in ((v_, r_), (w1_, lr_)):
        for q in range(runs):
            parts = [src[(n * runs + q) * 8:(n * runs + q + 1) * 8, :] for n in range(8)]
            turned = jnp.swapaxes(jnp.stack(parts, axis=0), 0, 1)
            for j in range(8):
                row = (BASE - CHAIN1 + j * runs + q) * 8
                ref[row:row + 8, :] = turned[j]

    def eight(i, y):
        g1_[i, :] = y
        w2_[i, :] = w3_[i, :] + (h1 * y + q1_[i, :])

    def nine(i, y):
        g2_[i, :] = y
        w1_[i, :] = w2_[i, :] + (h2 * y + q2_[i, :])

    def eleven(i, y):
        v2_[i, :] = v_[i, :] + (h1 * y + p1_[i, :])

    def twelve(i, y):
        v3 = v2_[i, :] + (h2 * y + p2_[i, :])
        v3_[i, :] = v3
        b_[i, :] = v3 - (r_[i, :] + TAU * lr_[i, :])

    def first_value(i):
        value = r_[i, :] + (h0 * lr_[i, :] + q0_[i, :])
        w3_[i, :] = value
        return value

    for _ in pieces(first_value, BASE - 10, BASE + OWN + 10, eight):
        pass
    batched("w2", BASE - 9, BASE + OWN + 9, nine)
    batched("w1", BASE - 8, BASE + OWN + 8, sweeps.make_four("r", "lr"))
    batched("v", BASE - 7, BASE + OWN + 7, eleven)
    batched("v2", BASE - 6, BASE + OWN + 6, twelve)

    def keep_second(n, rows, runs, value, y):
        for q in range(runs):
            f_[rows(q, n), :] = value[q * 8:(q + 1) * 8]

    def deliver(o, ref, t):
        for l in range(4):
            for q in range(OWN // 4):
                row = (BASE + 4 * q + l) * 8 + 2 * t
                out_ref[t, q, o * 8 + 2 * l:o * 8 + 2 * l + 2, :] = ref[row:row + 2, :]

    turns = ((1, v3_, 0), (1, v3_, 1), (0, f_, 0), (1, v3_, 2), (0, f_, 1), (1, v3_, 3), (0, f_, 2))
    value, rows, runs = chain(CHAIN2, 7, b_, keep_second, lambda n: deliver(*turns[n]))
    for q in range(runs):
        f_[rows(q, 7), :] = value[q * 8:(q + 1) * 8]
    deliver(0, f_, 3)


def vmem():
    return pl.BlockSpec(memory_space=pltpu.VMEM)


def smem():
    return pl.BlockSpec(memory_space=pltpu.SMEM)


def anywhere():
    return pl.BlockSpec(memory_space=pl.ANY)


def grant(mib):
    return pltpu.CompilerParams(vmem_limit_bytes=mib * 1024 * 1024)


def shards(basis, table, starts, volume_op, face_ops, neighbours):
    unit = lax.axis_index("tm") * 16 + lax.axis_index("zx")
    place = jnp.stack([unit, lax.axis_index("y")]).astype(jnp.int32).reshape(1, 2)

    sent, dt = pl.pallas_call(
        forward_kernel,
        out_shape=(
            jax.ShapeDtypeStruct((UNITS, 8, 128), f32),
            jax.ShapeDtypeStruct((2 * COLS, COLS), bf16),
        ),
        in_specs=[anywhere()] * 3,
        out_specs=(vmem(), vmem()),
        scratch_shapes=[
            pltpu.VMEM((2, 256, 128), f32),
            pltpu.VMEM((4, COLS), jnp.int32),
            pltpu.VMEM((2 * COLS, COLS), bf16),
            pltpu.SemaphoreType.DMA((3,)),
        ],
        name="forward",
    )(starts.reshape(2, 256, 128), neighbours, jnp.asarray(basis))
    wa, wb, ends, wt = pl.pallas_call(
        prepare_kernel,
        out_shape=(
            jax.ShapeDtypeStruct((384, 256), bf16),
            jax.ShapeDtypeStruct((256, 256), bf16),
            jax.ShapeDtypeStruct((16, 128), f32),
            jax.ShapeDtypeStruct((6 * COLS, 2 * COLS), bf16),
        ),
        in_specs=[vmem(), vmem(), vmem(), smem(), smem()],
        out_specs=(vmem(),) * 4,
        compiler_params=grant(8),
        cost_estimate=pl.CostEstimate(
            flops=2 * 10**9, bytes_accessed=4 * 10**6, transcendentals=0
        ),
        name="prepare",
    )(volume_op, face_ops, dt, jnp.asarray(table), place)
    got = lax.all_to_all(sent, ("tm", "zx"), 0, 0, tiled=True).reshape(4, 16, 8, 128)
    got, wa, wb, ends = lax.optimization_barrier((got, wa, wb, ends))
    odd = lax.axis_index("y") % 2 == 1
    low = jnp.concatenate([got[t, :REACH[t]] for t in range(4)], axis=0)
    high = jnp.concatenate([got[t, 16 - REACH[t]:] for t in range(4)], axis=0)
    first = lax.ppermute(jnp.where(odd, low, high), "y", [(0, 1), (1, 0), (2, 3), (3, 2)])
    second = lax.ppermute(jnp.where(odd, high, low), "y", [(1, 2), (2, 1), (3, 0), (0, 3)])
    below, above = jnp.where(odd, first, second), jnp.where(odd, second, first)
    done = pl.pallas_call(
        inner_kernel,
        out_shape=jax.ShapeDtypeStruct((HANDED, 128), f32),
        in_specs=[vmem()] * 3,
        out_specs=vmem(),
        scratch_shapes=[pltpu.VMEM((LAYERS * 8, 128), f32)] * len(NAMES),
        compiler_params=grant(16),
        cost_estimate=pl.CostEstimate(
            flops=3 * 10**9, bytes_accessed=8 * 10**6, transcendentals=0
        ),
        name="inner",
    )(got, wa, wb)
    back = pl.pallas_call(
        middle_kernel,
        out_shape=jax.ShapeDtypeStruct((4, 16, 16, 128), f32),
        in_specs=[vmem()] * 6,
        out_specs=vmem(),
        scratch_shapes=[pltpu.VMEM((LAYERS * 8, 128), f32)] * len(NAMES),
        compiler_params=grant(16),
        name="sweeps",
    )(done, below, above, wa, wb, ends)
    home = lax.all_to_all(back.reshape(UNITS, 16, 128), ("tm", "zx"), 0, 0, tiled=True)
    new, end = pl.pallas_call(
        backward_kernel,
        out_shape=(jax.ShapeDtypeStruct((2, 256, 128), f32),) * 2,
        in_specs=[vmem()] * 2,
        out_specs=(anywhere(),) * 2,
        scratch_shapes=[
            pltpu.VMEM((2, 256, 128), f32),
            pltpu.VMEM((2, 256, 128), f32),
            pltpu.SemaphoreType.DMA((4,)),
        ],
        compiler_params=grant(8),
        name="backward",
    )(home, wt)
    return new.reshape(2, 64, 4, 128), end.reshape(2, 64, 4, 128)


def solution(mesh):
    finer = Mesh(mesh.devices.reshape(4, 4, 16), ("tm", "y", "zx"))
    basis, table = modes()
    placed = P("tm", None, ("y", "zx"), None)
    return jax.shard_map(
        functools.partial(shards, basis, table),
        mesh=finer,
        in_specs=(placed, P(), P(), P()),
        out_specs=(placed, placed),
        check_vma=False,
    )
```

```python
import functools
import math

import jax
import jax.numpy as jnp
import ml_dtypes
import numpy as np
from jax import lax
from jax.experimental import pallas as pl
from jax.experimental.pallas import tpu as pltpu
from jax.sharding import Mesh
from jax.sharding import PartitionSpec as P

PY, PZ = 8, 16
COLS = PY * PZ
UNITS = 64
SLICES = 8
OWN = 64
HALO = 20
WIN = OWN + 2 * HALO
PAD = 2
LAYERS = WIN + 2 * PAD
BASE = PAD + HALO
CHAIN1 = 16
CHAIN2 = 8
TAU = 0.25
f32, bf16 = jnp.float32, jnp.bfloat16


def lagrange_integral(points, which, lower, upper):
    coefficients = [1.0]
    divisor = 1.0
    for other in range(4):
        if other != which:
            product = [0.0] * (len(coefficients) + 1)
            for power in range(len(coefficients)):
                product[power + 1] = product[power + 1] + coefficients[power]
                product[power] = product[power] - coefficients[power] * points[other]
            coefficients = product
            divisor = divisor * (points[which] - points[other])
    integral = 0.0
    for power in range(len(coefficients)):
        integral = integral + coefficients[power] * (
            upper ** (power + 1) - lower ** (power + 1)
        ) / (power + 1)
    return integral / divisor


def sdc_tables():
    offset = 0.5 / math.sqrt(5.0)
    points = [0.0, 0.5 - offset, 0.5 + offset, 1.0]
    widths = [TAU * (points[m + 1] - points[m]) for m in range(3)]
    weights = [
        [float(TAU * lagrange_integral(points, j, points[m], points[m + 1])) for j in range(4)]
        for m in range(3)
    ]
    return widths, weights


def modes():
    pairs = [(ka, kb) for kb in range(1, PZ // 2) for ka in range(PY)]
    pairs += [(ka, kb) for kb in (0, PZ // 2) for ka in range(1, PY // 2)]
    single = [((0, 0), (PY // 2, 0)), ((0, PZ // 2), (PY // 2, PZ // 2))]
    places = np.arange(COLS)
    a, b = places // PZ, places % PZ

    def angle(k):
        return 2.0 * np.pi * (((k[0] * a * (PZ // PY) + k[1] * b) % PZ) / PZ)

    def turn(k):
        return 2.0 * np.pi * k[0] / PY, 2.0 * np.pi * k[1] / PZ

    basis = np.zeros((2 * UNITS, COLS))
    table = np.zeros((UNITS, 8))
    for u, k in enumerate(pairs):
        scale = math.sqrt(2.0 / COLS)
        basis[u] = scale * np.cos(angle(k))
        basis[UNITS + u] = scale * np.sin(angle(k))
        al, be = turn(k)
        table[u, :6] = [np.cos(al), np.cos(be), np.cos(al), np.cos(be), np.sin(al), np.sin(be)]
    for i, (k, other) in enumerate(single):
        u = len(pairs) + i
        scale = math.sqrt(1.0 / COLS)
        basis[u] = scale * np.cos(angle(k))
        basis[UNITS + u] = scale * np.cos(angle(other))
        al, be = turn(k)
        al2, be2 = turn(other)
        table[u, :6] = [np.cos(al), np.cos(be), np.cos(al2), np.cos(be2), 0.0, 0.0]
    basis = basis.astype(np.float32)
    high = basis.astype(ml_dtypes.bfloat16)
    low = (basis - high.astype(np.float32)).astype(ml_dtypes.bfloat16)
    return np.concatenate([high, low], axis=0), table.astype(np.float32)


def look_up(table, index):
    return jnp.take_along_axis(table, index, axis=1)


def split(x):
    high = x.astype(bf16)
    low = (x - high.astype(f32)).astype(bf16)
    return high, low


def turn(blocks):
    return jnp.swapaxes(jnp.stack(blocks, axis=0), 0, 1)


def forward_kernel(x_hbm, nb_hbm, basis_hbm, out_ref, dt_ref, x_ref, nb_ref, basis_ref, sems):
    copies = [
        pltpu.make_async_copy(src, dst, sems.at[i])
        for i, (src, dst) in enumerate(
            ((nb_hbm, nb_ref), (basis_hbm, basis_ref), (x_hbm, x_ref))
        )
    ]
    for copy in copies:
        copy.start()
    copies[0].wait()
    a1 = jnp.broadcast_to(nb_ref[1:2, :], (8, COLS))
    b1 = jnp.broadcast_to(nb_ref[3:4, :], (8, COLS))
    place = lax.broadcasted_iota(jnp.int32, (8, COLS), 1)
    times = lax.broadcasted_iota(jnp.int32, (8, COLS), 0)
    a2, b2 = look_up(a1, a1), look_up(b1, b1)
    a4, b4 = look_up(a2, a2), look_up(b2, b2)
    b8 = look_up(b4, b4)
    along = jnp.where(times & 1 == 1, a1, place)
    along = jnp.where(times & 2 == 2, look_up(a2, along), along)
    along = jnp.where(times & 4 == 4, look_up(a4, along), along)
    column = jnp.zeros((8, COLS), jnp.int32)
    for bit, table in ((1, b1), (2, b2), (4, b4), (8, b8)):
        column = jnp.where(place & bit == bit, look_up(table, column), column)
    column = jnp.where(place // PZ == times, look_up(along, column), 0)
    column = jnp.sum(column, axis=0, keepdims=True)
    row = lax.broadcasted_iota(jnp.int32, (COLS, COLS), 0)
    hit = jnp.broadcast_to(column, (COLS, COLS)) == row
    one_hot = jnp.where(hit, 1.0, 0.0).astype(bf16)
    copies[1].wait()
    dt = lax.dot_general(
        basis_ref[...], one_hot, (((1,), (1,)), ((), ())), preferred_element_type=f32
    ).astype(bf16)
    dt_ref[...] = dt
    copies[2].wait()
    parts = []
    for l in range(4):
        for s in range(2):
            parts.append(x_ref[s, pl.ds(l, 64, stride=4), :])
    high, low = split(jnp.concatenate(parts, axis=0))
    result = lax.dot_general(
        jnp.concatenate([dt[:128], dt[:128], dt[128:]], axis=1),
        jnp.concatenate([high, low, high], axis=1),
        (((1,), (1,)), ((), ())), preferred_element_type=f32,
    )
    left = lax.broadcasted_iota(jnp.int32, (UNITS, COLS), 1) < 64
    lines = []
    for k in range(4):
        even = result[:UNITS, k * 128:(k + 1) * 128]
        odd = result[UNITS:, k * 128:(k + 1) * 128]
        lines.append(jnp.where(left, even, pltpu.roll(odd, 64, 1)))
        lines.append(jnp.where(left, pltpu.roll(even, 64, 1), odd))
    for u in range(0, UNITS, 8):
        out_ref[u:u + 8] = turn([line[u:u + 8] for line in lines])


def backward_kernel(z_ref, wt_ref, new_hbm, end_hbm, new_ref, end_ref, sems):
    copies = []
    for o, (ref, hbm) in enumerate(((new_ref, new_hbm), (end_ref, end_hbm))):
        rows = []
        lines = [
            turn([z_ref[u + i, 8 * o:8 * o + 8, :] for i in range(8)]) for u in range(0, UNITS, 8)
        ]
        for l in range(4):
            block = jnp.concatenate(
                [line[i] for i in (2 * l, 2 * l + 1) for line in lines], axis=0
            )
            turned = block.T
            rows.append(jnp.concatenate([turned[:64], turned[64:]], axis=1))
        for half in range(2):
            part = slice(half * 32, half * 32 + 32)
            high, low = split(jnp.concatenate([row[part] for row in rows], axis=0))
            result = jnp.dot(
                jnp.concatenate([high, low, high], axis=1), wt_ref[...],
                preferred_element_type=f32,
            )
            for l in range(4):
                for s in range(2):
                    ref[s, pl.ds(half * 128 + l, 32, stride=4), :] = result[
                        l * 32:(l + 1) * 32, s * 128:(s + 1) * 128
                    ]
            lines = pl.ds(half * 128, 128)
            copies.append(
                pltpu.make_async_copy(
                    ref.at[:, lines], hbm.at[:, lines], sems.at[2 * o + half]
                )
            )
            copies[-1].start()
    for copy in copies:
        copy.wait()


def chunks(first, last, most=34):
    count = last - first
    size = -(-count // -(-count // most))
    size += size % 2
    return [(at, min(size, last - at)) for at in range(first, last, size)]


def prepare_kernel(
    vol_ref, face_ref, dt_ref, table_ref, place_ref, wa_ref, wb_ref, ends_ref, wt_ref
):
    unit = place_ref[0, 0]
    fa, fb = face_ref[2] + face_ref[3], face_ref[4] + face_ref[5]
    ga, gb = face_ref[3] - face_ref[2], face_ref[5] - face_ref[4]
    vol = vol_ref[...]
    mcc = vol + table_ref[unit, 0] * fa + table_ref[unit, 1] * fb
    mss = vol + table_ref[unit, 2] * fa + table_ref[unit, 3] * fb
    mcs = table_ref[unit, 4] * ga + table_ref[unit, 5] * gb
    zero = jnp.zeros((64, 64), f32)

    def block(a, b, c, d):
        return jnp.concatenate(
            [jnp.concatenate([a, b], axis=1), jnp.concatenate([c, d], axis=1)], axis=0
        ).T

    m_high, m_low = split(block(mcc, mcs, -mcs, mss))
    f0_high, f0_low = split(block(face_ref[0], zero, zero, face_ref[0]))
    f1_high, f1_low = split(block(face_ref[1], zero, zero, face_ref[1]))
    both = jnp.concatenate([f1_high, m_high], axis=1)
    wa_ref[0:128, :] = both
    wa_ref[128:256, :] = both
    wa_ref[256:384, :] = jnp.concatenate([f1_low, m_low], axis=1)
    wb_ref[0:128, :] = jnp.concatenate([f0_high, f0_low], axis=1)
    wb_ref[128:256, :] = jnp.concatenate([f0_high, jnp.zeros_like(f0_low)], axis=1)
    blank = jnp.zeros((UNITS, COLS), bf16)
    for i, first in enumerate((0, 0, COLS)):
        for part in range(2):
            dt = dt_ref[first + part * UNITS:first + (part + 1) * UNITS, :]
            at = i * 2 * COLS + part * COLS
            wt_ref[at:at + UNITS, :] = jnp.concatenate([dt, blank], axis=1)
            wt_ref[at + UNITS:at + COLS, :] = jnp.concatenate([blank, dt], axis=1)
    ends_ref[0:8, :] = jnp.full((8, 128), jnp.where(place_ref[0, 1] == 0, 1.0, 0.0))
    ends_ref[8:16, :] = jnp.full((8, 128), jnp.where(place_ref[0, 1] == 3, 1.0, 0.0))


WHOLE = ("s", "b", "q0", "q1", "q2")
RIMS = ("f", "d1", "d2", "v3", "w1", "w2", "w3", "g1", "g2", "p1", "p2", "v", "v2")
NAMES = WHOLE + RIMS + ("r", "lr")
RIM = 8
REACH = (5, 4, 4, 3)
SLABS = [(t, q) for t in range(4) for q in range(REACH[t])]
HANDED = (len(WHOLE) * OWN + len(RIMS) * 2 * RIM) * 8


def handed():
    at = 0
    for name in WHOLE:
        yield name, BASE * 8, at, OWN * 8
        at += OWN * 8
    for name in RIMS:
        for first in (BASE, BASE + OWN - RIM):
            yield name, first * 8, at, RIM * 8
            at += RIM * 8


class Sweeps:
    def __init__(self, wa_ref, wb_ref, bufs, ends_ref=None):
        self.wa, self.wb, self.ends = wa_ref, wb_ref, ends_ref
        self.bufs = dict(zip(NAMES, bufs))

    def at_ends(self):
        return self.ends[0:8, :] > 0.5, self.ends[8:16, :] > 0.5

    def fill(self, part, places):
        for i, (t, at) in enumerate(places):
            for l in range(4):
                row = (at + l) * 8 + 2 * t
                self.bufs["s"][row:row + 2, :] = part(i)[2 * l:2 * l + 2, :]

    def product(self, x):
        high, low = split(x)
        acc = jnp.dot(
            jnp.concatenate([high, low, high], axis=1), self.wa[...],
            preferred_element_type=f32,
        )
        up = jnp.dot(
            jnp.concatenate([high, low], axis=1), self.wb[...], preferred_element_type=f32
        )
        return acc[:, 128:], up[:, :128] + up[:, 128:], acc[:, :128]

    def pieces(self, take, first, last, then, most=34):
        edge = None
        for at, n in chunks(first - 1, last + 1, most):
            own, up, down = self.product(take(slice(at * 8, (at + n) * 8)))
            if self.ends is not None:
                up = cut(up, BASE - 1 - at, self.at_ends()[0])
                down = cut(down, BASE + OWN - at, self.at_ends()[1])
            if edge is None:
                here = slice((at + 1) * 8, (at + n - 1) * 8)
                y = own[8:-8] + up[:-16] + down[16:]
            else:
                here = slice((at - 1) * 8, (at + n - 1) * 8)
                y = (
                    jnp.concatenate([edge[0], own[:-8]], axis=0)
                    + jnp.concatenate([edge[1], up[:-16]], axis=0)
                    + down
                )
            edge = own[-8:], up[-16:]
            then(here, y)
            yield

    def batched(self, name, first, last, then):
        src = self.bufs[name]
        for _ in self.pieces(lambda i: src[i, :], first, last, then):
            pass

    def make_four(self, start, zeroth):
        S = sdc_tables()[1]
        h1, h2 = sdc_tables()[0][1:]
        B = self.bufs

        def four(i, y):
            g0, g1, g2 = B[zeroth][i, :], B["g1"][i, :], B["g2"][i, :]
            B["v"][i, :] = B[start][i, :] + (
                S[0][0] * g0 + S[0][1] * g1 + S[0][2] * g2 + S[0][3] * y
            )
            B["p1"][i, :] = S[1][0] * g0 + (S[1][1] - h1) * g1 + S[1][2] * g2 + S[1][3] * y
            B["p2"][i, :] = S[2][0] * g0 + S[2][1] * g1 + (S[2][2] - h2) * g2 + S[2][3] * y

        return four

    def first_iteration(self):
        (h0, h1, h2), S = sdc_tables()
        B = self.bufs

        def one(i, y):
            B["f"][i, :] = y
            B["w1"][i, :] = B["s"][i, :] + h0 * y

        def two(i, y):
            B["g1"][i, :] = y
            B["w2"][i, :] = B["w1"][i, :] + h1 * y

        def three(i, y):
            B["g2"][i, :] = y
            B["w3"][i, :] = B["w2"][i, :] + h2 * y

        def five(i, y):
            B["d1"][i, :] = y - B["f"][i, :]
            B["v2"][i, :] = B["v"][i, :] + (h1 * y + B["p1"][i, :])

        def six(i, y):
            B["d2"][i, :] = y - B["f"][i, :]
            v3 = B["v2"][i, :] + (h2 * y + B["p2"][i, :])
            B["v3"][i, :] = v3
            B["b"][i, :] = v3 - (B["s"][i, :] + TAU * B["f"][i, :])

        def seven(i, y):
            d1, d2, d3 = B["d1"][i, :], B["d2"][i, :], y - B["f"][i, :]
            B["q0"][i, :] = S[0][1] * d1 + S[0][2] * d2 + S[0][3] * d3
            B["q1"][i, :] = (S[1][1] - h1) * d1 + S[1][2] * d2 + S[1][3] * d3
            B["q2"][i, :] = S[2][1] * d1 + (S[2][2] - h2) * d2 + S[2][3] * d3

        return (
            ("s", one), ("w1", two), ("w2", three), ("w3", self.make_four("s", "f")),
            ("v", five), ("v2", six), ("v3", seven),
        )


def cut(rows, i, where):
    if not 0 <= i < rows.shape[0] // 8:
        return rows
    part = jnp.where(where, 0.0, rows[i * 8:i * 8 + 8])
    around = [rows[:i * 8], part, rows[i * 8 + 8:]]
    return jnp.concatenate([r for r in around if r.shape[0]], axis=0)


def inner_kernel(r_ref, wa_ref, wb_ref, out_ref, *bufs):
    sweeps = Sweeps(wa_ref, wb_ref, bufs)
    own = [(t, BASE + 4 * q) for t in range(4) for q in range(OWN // 4)]
    sweeps.fill(lambda i: r_ref.at[i // 16, i % 16], own)
    for m, (name, then) in enumerate(sweeps.first_iteration(), 1):
        sweeps.batched(name, BASE + m, BASE + OWN - m, then)
    rows_done = {"s": 0, "f": 1, "w1": 1, "g1": 2, "w2": 2, "g2": 3, "w3": 3, "v": 4,
                 "p1": 4, "p2": 4, "d1": 5, "v2": 5, "d2": 6, "v3": 6, "b": 6,
                 "q0": 7, "q1": 7, "q2": 7}
    for name, row, at, count in handed():
        low = max(row, (BASE + rows_done[name]) * 8)
        high = min(row + count, (BASE + OWN - rows_done[name]) * 8)
        if low > row:
            out_ref[at:at + low - row, :] = jnp.zeros((low - row, 128), f32)
        out_ref[at + low - row:at + high - row, :] = sweeps.bufs[name][low:high, :]
        if high < row + count:
            rest = row + count - high
            out_ref[at + count - rest:at + count, :] = jnp.zeros((rest, 128), f32)


def middle_kernel(done_ref, lo_ref, hi_ref, wa_ref, wb_ref, ends_ref, out_ref, *bufs):
    widths, S = sdc_tables()
    h0, h1, h2 = widths
    sweeps = Sweeps(wa_ref, wb_ref, bufs, ends_ref)
    at_bottom, at_top = sweeps.at_ends()
    product, batched, pieces = sweeps.product, sweeps.batched, sweeps.pieces
    s_, b_, q0_, q1_, q2_, f_ = bufs[:6]
    v3_, w1_, w2_, w3_, g1_, g2_, p1_, p2_, v_, v2_, r_, lr_ = bufs[8:]
    b_[...] = jnp.zeros_like(b_)
    for name, row, at, count in handed():
        sweeps.bufs[name][row:row + count, :] = done_ref[at:at + count, :]
    for at in (0, BASE + OWN):
        s_[at * 8:(at + BASE) * 8, :] = jnp.zeros((BASE * 8, 128), f32)
    sweeps.fill(lambda i: lo_ref.at[i], [(t, BASE - 4 * (REACH[t] - q)) for t, q in SLABS])
    sweeps.fill(lambda i: hi_ref.at[i], [(t, BASE + OWN + 4 * q) for t, q in SLABS])

    steps = sweeps.first_iteration()
    for m, (name, then) in enumerate(steps, 1):
        if m < len(steps):
            batched(name, BASE - 18 + m, BASE + m, then)
            batched(name, BASE + OWN - m, BASE + OWN + 18 - m, then)

    def last_of_one(n):
        m = len(steps)
        if n == 1:
            batched(steps[-1][0], BASE - 18 + m, BASE + m, steps[-1][1])
        if n == 3:
            batched(steps[-1][0], BASE + OWN - m, BASE + OWN + 18 - m, steps[-1][1])

    def chain(reach, steps, addend, store, beside):
        runs = (OWN + 2 * reach) // 8
        base = (BASE - reach) * 8

        def rows(q, n):
            return pl.ds(base + q * 8 + n, 8, stride=runs * 8)

        def take(ref, n):
            return jnp.concatenate([ref[rows(q, n), :] for q in range(runs)], axis=0)

        sublane = lax.broadcasted_iota(jnp.int32, (8, 128), 0)

        def cut_one(rows, layer, ends):
            return cut(rows, layer % runs, ends & (sublane == layer // runs))

        value = take(s_, 0)
        for n in range(steps):
            beside(n)
            own, up, down = product(value)
            up = cut_one(up, reach - 1, at_bottom)
            down = cut_one(down, reach + OWN, at_top)
            up = jnp.concatenate([pltpu.roll(up[-8:], 1, 0), up[:-8]], axis=0)
            down = jnp.concatenate([down[8:], pltpu.roll(down[:8], 7, 0)], axis=0)
            y = own + up + down
            store(n, rows, runs, value, y)
            if n < 7:
                value = (value + take(addend, n)) + TAU * y
        return value, rows, runs

    def keep_first(n, rows, runs, value, y):
        here = slice(n * runs * 8, (n + 1) * runs * 8)
        v_[here, :] = value
        w1_[here, :] = y

    chain(CHAIN1, 8, b_, keep_first, last_of_one)

    runs = (OWN + 2 * CHAIN1) // 8
    for src, ref in ((v_, r_), (w1_, lr_)):
        for q in range(runs):
            parts = [src[(n * runs + q) * 8:(n * runs + q + 1) * 8, :] for n in range(8)]
            turned = turn(parts)
            for j in range(8):
                row = (BASE - CHAIN1 + j * runs + q) * 8
                ref[row:row + 8, :] = turned[j]

    def eight(i, y):
        g1_[i, :] = y
        w2_[i, :] = w3_[i, :] + (h1 * y + q1_[i, :])

    def nine(i, y):
        g2_[i, :] = y
        w1_[i, :] = w2_[i, :] + (h2 * y + q2_[i, :])

    def eleven(i, y):
        v2_[i, :] = v_[i, :] + (h1 * y + p1_[i, :])

    def twelve(i, y):
        v3 = v2_[i, :] + (h2 * y + p2_[i, :])
        v3_[i, :] = v3
        b_[i, :] = v3 - (r_[i, :] + TAU * lr_[i, :])

    def first_value(i):
        value = r_[i, :] + (h0 * lr_[i, :] + q0_[i, :])
        w3_[i, :] = value
        return value

    for _ in pieces(first_value, BASE - 10, BASE + OWN + 10, eight):
        pass
    batched("w2", BASE - 9, BASE + OWN + 9, nine)
    batched("w1", BASE - 8, BASE + OWN + 8, sweeps.make_four("r", "lr"))
    batched("v", BASE - 7, BASE + OWN + 7, eleven)
    batched("v2", BASE - 6, BASE + OWN + 6, twelve)

    def keep_second(n, rows, runs, value, y):
        for q in range(runs):
            f_[rows(q, n), :] = value[q * 8:(q + 1) * 8]

    def deliver(o, ref, t):
        for l in range(4):
            for q in range(OWN // 4):
                row = (BASE + 4 * q + l) * 8 + 2 * t
                out_ref[t, q, o * 8 + 2 * l:o * 8 + 2 * l + 2, :] = ref[row:row + 2, :]

    turns = ((1, v3_, 0), (1, v3_, 1), (0, f_, 0), (1, v3_, 2), (0, f_, 1), (1, v3_, 3), (0, f_, 2))
    value, rows, runs = chain(CHAIN2, 7, b_, keep_second, lambda n: deliver(*turns[n]))
    for q in range(runs):
        f_[rows(q, 7), :] = value[q * 8:(q + 1) * 8]
    deliver(0, f_, 3)


def vmem():
    return pl.BlockSpec(memory_space=pltpu.VMEM)


def smem():
    return pl.BlockSpec(memory_space=pltpu.SMEM)


def anywhere():
    return pl.BlockSpec(memory_space=pl.ANY)


def grant(mib):
    return pltpu.CompilerParams(vmem_limit_bytes=mib * 1024 * 1024)


def shards(basis, table, starts, volume_op, face_ops, neighbours):
    unit = lax.axis_index("tm") * 16 + lax.axis_index("zx")
    place = jnp.stack([unit, lax.axis_index("y")]).astype(jnp.int32).reshape(1, 2)

    sent, dt = pl.pallas_call(
        forward_kernel,
        out_shape=(
            jax.ShapeDtypeStruct((UNITS, 8, 128), f32),
            jax.ShapeDtypeStruct((2 * COLS, COLS), bf16),
        ),
        in_specs=[anywhere()] * 3,
        out_specs=(vmem(), vmem()),
        scratch_shapes=[
            pltpu.VMEM((2, 256, 128), f32),
            pltpu.VMEM((4, COLS), jnp.int32),
            pltpu.VMEM((2 * COLS, COLS), bf16),
            pltpu.SemaphoreType.DMA((3,)),
        ],
        name="forward",
    )(starts.reshape(2, 256, 128), neighbours, jnp.asarray(basis))
    wa, wb, ends, wt = pl.pallas_call(
        prepare_kernel,
        out_shape=(
            jax.ShapeDtypeStruct((384, 256), bf16),
            jax.ShapeDtypeStruct((256, 256), bf16),
            jax.ShapeDtypeStruct((16, 128), f32),
            jax.ShapeDtypeStruct((6 * COLS, 2 * COLS), bf16),
        ),
        in_specs=[vmem(), vmem(), vmem(), smem(), smem()],
        out_specs=(vmem(),) * 4,
        compiler_params=grant(8),
        cost_estimate=pl.CostEstimate(
            flops=2 * 10**9, bytes_accessed=4 * 10**6, transcendentals=0
        ),
        name="prepare",
    )(volume_op, face_ops, dt, jnp.asarray(table), place)
    got = lax.all_to_all(sent, ("tm", "zx"), 0, 0, tiled=True).reshape(4, 16, 8, 128)
    got, wa, wb, ends = lax.optimization_barrier((got, wa, wb, ends))
    odd = lax.axis_index("y") % 2 == 1
    low = jnp.concatenate([got[t, :REACH[t]] for t in range(4)], axis=0)
    high = jnp.concatenate([got[t, 16 - REACH[t]:] for t in range(4)], axis=0)
    first = lax.ppermute(jnp.where(odd, low, high), "y", [(0, 1), (1, 0), (2, 3), (3, 2)])
    second = lax.ppermute(jnp.where(odd, high, low), "y", [(1, 2), (2, 1), (3, 0), (0, 3)])
    below, above = jnp.where(odd, first, second), jnp.where(odd, second, first)
    done = pl.pallas_call(
        inner_kernel,
        out_shape=jax.ShapeDtypeStruct((HANDED, 128), f32),
        in_specs=[vmem()] * 3,
        out_specs=vmem(),
        scratch_shapes=[pltpu.VMEM((LAYERS * 8, 128), f32)] * len(NAMES),
        compiler_params=grant(16),
        cost_estimate=pl.CostEstimate(
            flops=3 * 10**9, bytes_accessed=8 * 10**6, transcendentals=0
        ),
        name="inner",
    )(got, wa, wb)
    back = pl.pallas_call(
        middle_kernel,
        out_shape=jax.ShapeDtypeStruct((4, 16, 16, 128), f32),
        in_specs=[vmem()] * 6,
        out_specs=vmem(),
        scratch_shapes=[pltpu.VMEM((LAYERS * 8, 128), f32)] * len(NAMES),
        compiler_params=grant(16),
        name="sweeps",
    )(done, below, above, wa, wb, ends)
    home = lax.all_to_all(back.reshape(UNITS, 16, 128), ("tm", "zx"), 0, 0, tiled=True)
    new, end = pl.pallas_call(
        backward_kernel,
        out_shape=(jax.ShapeDtypeStruct((2, 256, 128), f32),) * 2,
        in_specs=[vmem()] * 2,
        out_specs=(anywhere(),) * 2,
        scratch_shapes=[
            pltpu.VMEM((2, 256, 128), f32),
            pltpu.VMEM((2, 256, 128), f32),
            pltpu.SemaphoreType.DMA((4,)),
        ],
        compiler_params=grant(8),
        name="backward",
    )(home, wt)
    return new.reshape(2, 64, 4, 128), end.reshape(2, 64, 4, 128)


def solution(mesh):
    finer = Mesh(mesh.devices.reshape(4, 4, 16), ("tm", "y", "zx"))
    basis, table = modes()
    placed = P("tm", None, ("y", "zx"), None)
    return jax.shard_map(
        functools.partial(shards, basis, table),
        mesh=finer,
        in_specs=(placed, P(), P(), P()),
        out_specs=(placed, placed),
        check_vma=False,
    )
```

```python
import functools
import math

import jax
import jax.numpy as jnp
import ml_dtypes
import numpy as np
from jax import lax
from jax.experimental import pallas as pl
from jax.experimental.pallas import tpu as pltpu
from jax.sharding import Mesh
from jax.sharding import PartitionSpec as P

PY, PZ = 8, 16
COLS = PY * PZ
UNITS = 64
SLICES = 8
OWN = 64
HALO = 20
WIN = OWN + 2 * HALO
PAD = 2
LAYERS = WIN + 2 * PAD
BASE = PAD + HALO
CHAIN1 = 16
CHAIN2 = 8
TAU = 0.25
f32, bf16 = jnp.float32, jnp.bfloat16


def lagrange_integral(points, which, lower, upper):
    coefficients = [1.0]
    divisor = 1.0
    for other in range(4):
        if other != which:
            product = [0.0] * (len(coefficients) + 1)
            for power in range(len(coefficients)):
                product[power + 1] = product[power + 1] + coefficients[power]
                product[power] = product[power] - coefficients[power] * points[other]
            coefficients = product
            divisor = divisor * (points[which] - points[other])
    integral = 0.0
    for power in range(len(coefficients)):
        integral = integral + coefficients[power] * (
            upper ** (power + 1) - lower ** (power + 1)
        ) / (power + 1)
    return integral / divisor


def sdc_tables():
    offset = 0.5 / math.sqrt(5.0)
    points = [0.0, 0.5 - offset, 0.5 + offset, 1.0]
    widths = [TAU * (points[m + 1] - points[m]) for m in range(3)]
    weights = [
        [float(TAU * lagrange_integral(points, j, points[m], points[m + 1])) for j in range(4)]
        for m in range(3)
    ]
    return widths, weights


def modes():
    pairs = [(ka, kb) for kb in range(1, PZ // 2) for ka in range(PY)]
    pairs += [(ka, kb) for kb in (0, PZ // 2) for ka in range(1, PY // 2)]
    single = [((0, 0), (PY // 2, 0)), ((0, PZ // 2), (PY // 2, PZ // 2))]
    places = np.arange(COLS)
    a, b = places // PZ, places % PZ

    def angle(k):
        return 2.0 * np.pi * (((k[0] * a * (PZ // PY) + k[1] * b) % PZ) / PZ)

    def turn(k):
        return 2.0 * np.pi * k[0] / PY, 2.0 * np.pi * k[1] / PZ

    basis = np.zeros((2 * UNITS, COLS))
    table = np.zeros((UNITS, 8))
    for u, k in enumerate(pairs):
        scale = math.sqrt(2.0 / COLS)
        basis[u] = scale * np.cos(angle(k))
        basis[UNITS + u] = scale * np.sin(angle(k))
        al, be = turn(k)
        table[u, :6] = [np.cos(al), np.cos(be), np.cos(al), np.cos(be), np.sin(al), np.sin(be)]
    for i, (k, other) in enumerate(single):
        u = len(pairs) + i
        scale = math.sqrt(1.0 / COLS)
        basis[u] = scale * np.cos(angle(k))
        basis[UNITS + u] = scale * np.cos(angle(other))
        al, be = turn(k)
        al2, be2 = turn(other)
        table[u, :6] = [np.cos(al), np.cos(be), np.cos(al2), np.cos(be2), 0.0, 0.0]
    basis = basis.astype(np.float32)
    high = basis.astype(ml_dtypes.bfloat16)
    low = (basis - high.astype(np.float32)).astype(ml_dtypes.bfloat16)
    return np.concatenate([high, low], axis=0), table.astype(np.float32)


def look_up(table, index):
    return jnp.take_along_axis(table, index, axis=1)


def split(x):
    high = x.astype(bf16)
    low = (x - high.astype(f32)).astype(bf16)
    return high, low


def turn(blocks):
    return jnp.swapaxes(jnp.stack(blocks, axis=0), 0, 1)


def forward_kernel(x_hbm, nb_hbm, basis_hbm, out_ref, dt_ref, x_ref, nb_ref, basis_ref, sems):
    copies = [
        pltpu.make_async_copy(src, dst, sems.at[i])
        for i, (src, dst) in enumerate(
            ((nb_hbm, nb_ref), (basis_hbm, basis_ref), (x_hbm, x_ref))
        )
    ]
    for copy in copies:
        copy.start()
    copies[0].wait()
    a1 = jnp.broadcast_to(nb_ref[1:2, :], (8, COLS))
    b1 = jnp.broadcast_to(nb_ref[3:4, :], (8, COLS))
    place = lax.broadcasted_iota(jnp.int32, (8, COLS), 1)
    times = lax.broadcasted_iota(jnp.int32, (8, COLS), 0)
    a2, b2 = look_up(a1, a1), look_up(b1, b1)
    a4, b4 = look_up(a2, a2), look_up(b2, b2)
    b8 = look_up(b4, b4)
    along = jnp.where(times & 1 == 1, a1, place)
    along = jnp.where(times & 2 == 2, look_up(a2, along), along)
    along = jnp.where(times & 4 == 4, look_up(a4, along), along)
    column = jnp.zeros((8, COLS), jnp.int32)
    for bit, table in ((1, b1), (2, b2), (4, b4), (8, b8)):
        column = jnp.where(place & bit == bit, look_up(table, column), column)
    column = jnp.where(place // PZ == times, look_up(along, column), 0)
    column = jnp.sum(column, axis=0, keepdims=True)
    row = lax.broadcasted_iota(jnp.int32, (COLS, COLS), 0)
    hit = jnp.broadcast_to(column, (COLS, COLS)) == row
    one_hot = jnp.where(hit, 1.0, 0.0).astype(bf16)
    copies[1].wait()
    dt = lax.dot_general(
        basis_ref[...], one_hot, (((1,), (1,)), ((), ())), preferred_element_type=f32
    ).astype(bf16)
    dt_ref[...] = dt
    copies[2].wait()
    parts = []
    for l in range(4):
        for s in range(2):
            parts.append(x_ref[s, pl.ds(l, 64, stride=4), :])
    high, low = split(jnp.concatenate(parts, axis=0))
    result = lax.dot_general(
        jnp.concatenate([dt[:128], dt[:128], dt[128:]], axis=1),
        jnp.concatenate([high, low, high], axis=1),
        (((1,), (1,)), ((), ())), preferred_element_type=f32,
    )
    left = lax.broadcasted_iota(jnp.int32, (UNITS, COLS), 1) < 64
    lines = []
    for k in range(4):
        even = result[:UNITS, k * 128:(k + 1) * 128]
        odd = result[UNITS:, k * 128:(k + 1) * 128]
        lines.append(jnp.where(left, even, pltpu.roll(odd, 64, 1)))
        lines.append(jnp.where(left, pltpu.roll(even, 64, 1), odd))
    for u in range(0, UNITS, 8):
        out_ref[u:u + 8] = turn([line[u:u + 8] for line in lines])


def backward_kernel(z_ref, wt_ref, new_hbm, end_hbm, new_ref, end_ref, sems):
    copies = []
    for o, (ref, hbm) in enumerate(((new_ref, new_hbm), (end_ref, end_hbm))):
        rows = []
        lines = [
            turn([z_ref[u + i, 8 * o:8 * o + 8, :] for i in range(8)]) for u in range(0, UNITS, 8)
        ]
        for l in range(4):
            block = jnp.concatenate(
                [line[i] for i in (2 * l, 2 * l + 1) for line in lines], axis=0
            )
            turned = block.T
            rows.append(jnp.concatenate([turned[:64], turned[64:]], axis=1))
        for half in range(2):
            part = slice(half * 32, half * 32 + 32)
            high, low = split(jnp.concatenate([row[part] for row in rows], axis=0))
            result = jnp.dot(
                jnp.concatenate([high, low, high], axis=1), wt_ref[...],
                preferred_element_type=f32,
            )
            for l in range(4):
                for s in range(2):
                    ref[s, pl.ds(half * 128 + l, 32, stride=4), :] = result[
                        l * 32:(l + 1) * 32, s * 128:(s + 1) * 128
                    ]
            lines = pl.ds(half * 128, 128)
            copies.append(
                pltpu.make_async_copy(
                    ref.at[:, lines], hbm.at[:, lines], sems.at[2 * o + half]
                )
            )
            copies[-1].start()
    for copy in copies:
        copy.wait()


def chunks(first, last, most=34):
    count = last - first
    size = -(-count // -(-count // most))
    size += size % 2
    return [(at, min(size, last - at)) for at in range(first, last, size)]


def prepare_kernel(
    vol_ref, face_ref, dt_ref, table_ref, place_ref, wa_ref, wb_ref, ends_ref, wt_ref
):
    unit = place_ref[0, 0]
    fa, fb = face_ref[2] + face_ref[3], face_ref[4] + face_ref[5]
    ga, gb = face_ref[3] - face_ref[2], face_ref[5] - face_ref[4]
    vol = vol_ref[...]
    mcc = vol + table_ref[unit, 0] * fa + table_ref[unit, 1] * fb
    mss = vol + table_ref[unit, 2] * fa + table_ref[unit, 3] * fb
    mcs = table_ref[unit, 4] * ga + table_ref[unit, 5] * gb
    zero = jnp.zeros((64, 64), f32)

    def block(a, b, c, d):
        return jnp.concatenate(
            [jnp.concatenate([a, b], axis=1), jnp.concatenate([c, d], axis=1)], axis=0
        ).T

    m_high, m_low = split(block(mcc, mcs, -mcs, mss))
    f0_high, f0_low = split(block(face_ref[0], zero, zero, face_ref[0]))
    f1_high, f1_low = split(block(face_ref[1], zero, zero, face_ref[1]))
    both = jnp.concatenate([f1_high, m_high], axis=1)
    wa_ref[0:128, :] = both
    wa_ref[128:256, :] = both
    wa_ref[256:384, :] = jnp.concatenate([f1_low, m_low], axis=1)
    wb_ref[0:128, :] = jnp.concatenate([f0_high, f0_low], axis=1)
    wb_ref[128:256, :] = jnp.concatenate([f0_high, jnp.zeros_like(f0_low)], axis=1)
    blank = jnp.zeros((UNITS, COLS), bf16)
    for i, first in enumerate((0, 0, COLS)):
        for part in range(2):
            dt = dt_ref[first + part * UNITS:first + (part + 1) * UNITS, :]
            at = i * 2 * COLS + part * COLS
            wt_ref[at:at + UNITS, :] = jnp.concatenate([dt, blank], axis=1)
            wt_ref[at + UNITS:at + COLS, :] = jnp.concatenate([blank, dt], axis=1)
    ends_ref[0:8, :] = jnp.full((8, 128), jnp.where(place_ref[0, 1] == 0, 1.0, 0.0))
    ends_ref[8:16, :] = jnp.full((8, 128), jnp.where(place_ref[0, 1] == 3, 1.0, 0.0))


WHOLE = ("s", "b", "q0", "q1", "q2")
RIMS = ("k1", "k2", "k3", "k4", "k5", "k6")
NAMES = WHOLE + RIMS + (
    "k7", "w1", "w2", "w3", "g1", "g2", "p1", "p2", "v", "v2", "v3", "r", "lr"
)
RIM = 8
REACH = (5, 4, 4, 3)
SLABS = [(t, q) for t in range(4) for q in range(REACH[t])]
HANDED = (len(WHOLE) * OWN + len(RIMS) * 2 * RIM) * 8


def handed():
    at = 0
    for name in WHOLE:
        yield name, BASE * 8, at, OWN * 8
        at += OWN * 8
    for name in RIMS:
        for first in (BASE, BASE + OWN - RIM):
            yield name, first * 8, at, RIM * 8
            at += RIM * 8


def first_iteration():
    (h0, h1, h2), S = sdc_tables()

    def x(p):
        return np.concatenate([[0.0], p[:-1]])

    one = np.zeros(8)
    one[0] = 1.0
    w1 = one + h0 * x(one)
    w2 = w1 + h1 * x(w1)
    w3 = w2 + h2 * x(w2)
    g = [x(one), x(w1), x(w2), x(w3)]
    add = [sum(S[m][j] * g[j] for j in range(4)) for m in range(3)]
    v1 = one + add[0]
    v2 = v1 + h1 * (x(v1) - g[1]) + add[1]
    v3 = v2 + h2 * (x(v2) - g[2]) + add[2]
    d1, d2, d3 = x(v1 - one), x(v2 - one), x(v3 - one)
    out = {
        "b": v3 - one - TAU * x(one),
        "q0": S[0][1] * d1 + S[0][2] * d2 + S[0][3] * d3,
        "q1": (S[1][1] - h1) * d1 + S[1][2] * d2 + S[1][3] * d3,
        "q2": S[2][1] * d1 + (S[2][2] - h2) * d2 + S[2][3] * d3,
    }
    return {name: [float(c) for c in p] for name, p in out.items()}


class Sweeps:
    def __init__(self, wa_ref, wb_ref, bufs, ends_ref=None):
        self.wa, self.wb, self.ends = wa_ref, wb_ref, ends_ref
        self.bufs = dict(zip(NAMES, bufs))

    def at_ends(self):
        return self.ends[0:8, :] > 0.5, self.ends[8:16, :] > 0.5

    def fill(self, part, places):
        for i, (t, at) in enumerate(places):
            for l in range(4):
                row = (at + l) * 8 + 2 * t
                self.bufs["s"][row:row + 2, :] = part(i)[2 * l:2 * l + 2, :]

    def product(self, x):
        high, low = split(x)
        acc = jnp.dot(
            jnp.concatenate([high, low, high], axis=1), self.wa[...],
            preferred_element_type=f32,
        )
        up = jnp.dot(
            jnp.concatenate([high, low], axis=1), self.wb[...], preferred_element_type=f32
        )
        return acc[:, 128:], up[:, :128] + up[:, 128:], acc[:, :128]

    def pieces(self, take, first, last, then, most=34):
        edge = None
        for at, n in chunks(first - 1, last + 1, most):
            own, up, down = self.product(take(slice(at * 8, (at + n) * 8)))
            if self.ends is not None:
                up = cut(up, BASE - 1 - at, self.at_ends()[0])
                down = cut(down, BASE + OWN - at, self.at_ends()[1])
            if edge is None:
                here = slice((at + 1) * 8, (at + n - 1) * 8)
                y = own[8:-8] + up[:-16] + down[16:]
            else:
                here = slice((at - 1) * 8, (at + n - 1) * 8)
                y = (
                    jnp.concatenate([edge[0], own[:-8]], axis=0)
                    + jnp.concatenate([edge[1], up[:-16]], axis=0)
                    + down
                )
            edge = own[-8:], up[-16:]
            then(here, y)
            yield

    def batched(self, name, first, last, then):
        src = self.bufs[name]
        for _ in self.pieces(lambda i: src[i, :], first, last, then):
            pass

    def make_four(self, start, zeroth):
        S = sdc_tables()[1]
        h1, h2 = sdc_tables()[0][1:]
        B = self.bufs

        def four(i, y):
            g0, g1, g2 = B[zeroth][i, :], B["g1"][i, :], B["g2"][i, :]
            B["v"][i, :] = B[start][i, :] + (
                S[0][0] * g0 + S[0][1] * g1 + S[0][2] * g2 + S[0][3] * y
            )
            B["p1"][i, :] = S[1][0] * g0 + (S[1][1] - h1) * g1 + S[1][2] * g2 + S[1][3] * y
            B["p2"][i, :] = S[2][0] * g0 + S[2][1] * g1 + (S[2][2] - h2) * g2 + S[2][3] * y

        return four

    def power(self, m, first, last):
        def then(i, y):
            self.bufs["k%d" % m][i, :] = y

        self.batched("k%d" % (m - 1) if m > 1 else "s", first, last, then)

    def combine(self, names, first, last):
        i = slice(first * 8, last * 8)
        powers = {}
        for name in names:
            total = None
            for m, c in enumerate(first_iteration()[name]):
                if c != 0.0:
                    if m not in powers:
                        powers[m] = self.bufs["k%d" % m][i, :]
                    total = powers[m] * c if total is None else total + powers[m] * c
            self.bufs[name][i, :] = total


def cut(rows, i, where):
    if not 0 <= i < rows.shape[0] // 8:
        return rows
    part = jnp.where(where, 0.0, rows[i * 8:i * 8 + 8])
    around = [rows[:i * 8], part, rows[i * 8 + 8:]]
    return jnp.concatenate([r for r in around if r.shape[0]], axis=0)


def inner_kernel(r_ref, wa_ref, wb_ref, out_ref, *bufs):
    sweeps = Sweeps(wa_ref, wb_ref, bufs)
    own = [(t, BASE + 4 * q) for t in range(4) for q in range(OWN // 4)]
    sweeps.fill(lambda i: r_ref.at[i // 16, i % 16], own)
    for m in range(1, 8):
        sweeps.power(m, BASE + m, BASE + OWN - m)
    sweeps.combine(("b",), BASE + 6, BASE + OWN - 6)
    sweeps.combine(("q0", "q1", "q2"), BASE + 7, BASE + OWN - 7)
    rows_done = {"s": 0, "b": 6, "q0": 7, "q1": 7, "q2": 7}
    rows_done.update(("k%d" % m, m) for m in range(1, 7))
    for name, row, at, count in handed():
        low = max(row, (BASE + rows_done[name]) * 8)
        high = min(row + count, (BASE + OWN - rows_done[name]) * 8)
        if low > row:
            out_ref[at:at + low - row, :] = jnp.zeros((low - row, 128), f32)
        out_ref[at + low - row:at + high - row, :] = sweeps.bufs[name][low:high, :]
        if high < row + count:
            rest = row + count - high
            out_ref[at + count - rest:at + count, :] = jnp.zeros((rest, 128), f32)


def middle_kernel(done_ref, lo_ref, hi_ref, wa_ref, wb_ref, ends_ref, out_ref, *bufs):
    widths, S = sdc_tables()
    h0, h1, h2 = widths
    sweeps = Sweeps(wa_ref, wb_ref, bufs, ends_ref)
    at_bottom, at_top = sweeps.at_ends()
    product, batched, pieces = sweeps.product, sweeps.batched, sweeps.pieces
    s_, b_, q0_, q1_, q2_ = bufs[:5]
    w1_, w2_, w3_, g1_, g2_, p1_, p2_, v_, v2_, v3_, r_, lr_ = bufs[12:]
    b_[...] = jnp.zeros_like(b_)
    for name, row, at, count in handed():
        sweeps.bufs[name][row:row + count, :] = done_ref[at:at + count, :]
    for at in (0, BASE + OWN):
        s_[at * 8:(at + BASE) * 8, :] = jnp.zeros((BASE * 8, 128), f32)
    sweeps.fill(lambda i: lo_ref.at[i], [(t, BASE - 4 * (REACH[t] - q)) for t, q in SLABS])
    sweeps.fill(lambda i: hi_ref.at[i], [(t, BASE + OWN + 4 * q) for t, q in SLABS])

    def strips(m):
        return (BASE - 18 + m, BASE + m), (BASE + OWN - m, BASE + OWN + 18 - m)

    for m in range(1, 7):
        for first, last in strips(m):
            sweeps.power(m, first, last)
    for first, last in strips(6):
        sweeps.combine(("b",), first, last)

    def last_of_one(n):
        if n in (1, 3):
            first, last = strips(7)[n // 2]
            sweeps.power(7, first, last)
            sweeps.combine(("q0", "q1", "q2"), first, last)

    def chain(reach, steps, addend, store, beside):
        runs = (OWN + 2 * reach) // 8
        base = (BASE - reach) * 8

        def rows(q, n):
            return pl.ds(base + q * 8 + n, 8, stride=runs * 8)

        def take(ref, n):
            return jnp.concatenate([ref[rows(q, n), :] for q in range(runs)], axis=0)

        sublane = lax.broadcasted_iota(jnp.int32, (8, 128), 0)

        def cut_one(rows, layer, ends):
            return cut(rows, layer % runs, ends & (sublane == layer // runs))

        value = take(s_, 0)
        for n in range(steps):
            beside(n)
            own, up, down = product(value)
            up = cut_one(up, reach - 1, at_bottom)
            down = cut_one(down, reach + OWN, at_top)
            up = jnp.concatenate([pltpu.roll(up[-8:], 1, 0), up[:-8]], axis=0)
            down = jnp.concatenate([down[8:], pltpu.roll(down[:8], 7, 0)], axis=0)
            y = own + up + down
            store(n, rows, runs, value, y)
            if n < 7:
                value = (value + take(addend, n)) + TAU * y
        return value, rows, runs

    def keep_first(n, rows, runs, value, y):
        here = slice(n * runs * 8, (n + 1) * runs * 8)
        v_[here, :] = value
        w1_[here, :] = y

    chain(CHAIN1, 8, b_, keep_first, last_of_one)

    runs = (OWN + 2 * CHAIN1) // 8
    for src, ref in ((v_, r_), (w1_, lr_)):
        for q in range(runs):
            parts = [src[(n * runs + q) * 8:(n * runs + q + 1) * 8, :] for n in range(8)]
            turned = turn(parts)
            for j in range(8):
                row = (BASE - CHAIN1 + j * runs + q) * 8
                ref[row:row + 8, :] = turned[j]

    def eight(i, y):
        g1_[i, :] = y
        w2_[i, :] = w3_[i, :] + (h1 * y + q1_[i, :])

    def nine(i, y):
        g2_[i, :] = y
        w1_[i, :] = w2_[i, :] + (h2 * y + q2_[i, :])

    def eleven(i, y):
        v2_[i, :] = v_[i, :] + (h1 * y + p1_[i, :])

    def twelve(i, y):
        v3 = v2_[i, :] + (h2 * y + p2_[i, :])
        v3_[i, :] = v3
        b_[i, :] = v3 - (r_[i, :] + TAU * lr_[i, :])

    def first_value(i):
        value = r_[i, :] + (h0 * lr_[i, :] + q0_[i, :])
        w3_[i, :] = value
        return value

    for _ in pieces(first_value, BASE - 10, BASE + OWN + 10, eight):
        pass
    batched("w2", BASE - 9, BASE + OWN + 9, nine)
    batched("w1", BASE - 8, BASE + OWN + 8, sweeps.make_four("r", "lr"))
    batched("v", BASE - 7, BASE + OWN + 7, eleven)
    batched("v2", BASE - 6, BASE + OWN + 6, twelve)

    def keep_second(n, rows, runs, value, y):
        for q in range(runs):
            g1_[rows(q, n), :] = value[q * 8:(q + 1) * 8]

    def deliver(o, ref, t):
        for l in range(4):
            for q in range(OWN // 4):
                row = (BASE + 4 * q + l) * 8 + 2 * t
                out_ref[t, q, o * 8 + 2 * l:o * 8 + 2 * l + 2, :] = ref[row:row + 2, :]

    turns = (
        (1, v3_, 0), (1, v3_, 1), (0, g1_, 0), (1, v3_, 2), (0, g1_, 1), (1, v3_, 3), (0, g1_, 2),
    )
    value, rows, runs = chain(CHAIN2, 7, b_, keep_second, lambda n: deliver(*turns[n]))
    for q in range(runs):
        g1_[rows(q, 7), :] = value[q * 8:(q + 1) * 8]
    deliver(0, g1_, 3)


def vmem():
    return pl.BlockSpec(memory_space=pltpu.VMEM)


def smem():
    return pl.BlockSpec(memory_space=pltpu.SMEM)


def anywhere():
    return pl.BlockSpec(memory_space=pl.ANY)


def grant(mib):
    return pltpu.CompilerParams(vmem_limit_bytes=mib * 1024 * 1024)


def shards(basis, table, starts, volume_op, face_ops, neighbours):
    unit = lax.axis_index("tm") * 16 + lax.axis_index("zx")
    place = jnp.stack([unit, lax.axis_index("y")]).astype(jnp.int32).reshape(1, 2)

    sent, dt = pl.pallas_call(
        forward_kernel,
        out_shape=(
            jax.ShapeDtypeStruct((UNITS, 8, 128), f32),
            jax.ShapeDtypeStruct((2 * COLS, COLS), bf16),
        ),
        in_specs=[anywhere()] * 3,
        out_specs=(vmem(), vmem()),
        scratch_shapes=[
            pltpu.VMEM((2, 256, 128), f32),
            pltpu.VMEM((4, COLS), jnp.int32),
            pltpu.VMEM((2 * COLS, COLS), bf16),
            pltpu.SemaphoreType.DMA((3,)),
        ],
        name="forward",
    )(starts.reshape(2, 256, 128), neighbours, jnp.asarray(basis))
    wa, wb, ends, wt = pl.pallas_call(
        prepare_kernel,
        out_shape=(
            jax.ShapeDtypeStruct((384, 256), bf16),
            jax.ShapeDtypeStruct((256, 256), bf16),
            jax.ShapeDtypeStruct((16, 128), f32),
            jax.ShapeDtypeStruct((6 * COLS, 2 * COLS), bf16),
        ),
        in_specs=[vmem(), vmem(), vmem(), smem(), smem()],
        out_specs=(vmem(),) * 4,
        compiler_params=grant(8),
        cost_estimate=pl.CostEstimate(
            flops=2 * 10**9, bytes_accessed=4 * 10**6, transcendentals=0
        ),
        name="prepare",
    )(volume_op, face_ops, dt, jnp.asarray(table), place)
    got = lax.all_to_all(sent, ("tm", "zx"), 0, 0, tiled=True).reshape(4, 16, 8, 128)
    got, wa, wb, ends = lax.optimization_barrier((got, wa, wb, ends))
    odd = lax.axis_index("y") % 2 == 1
    low = jnp.concatenate([got[t, :REACH[t]] for t in range(4)], axis=0)
    high = jnp.concatenate([got[t, 16 - REACH[t]:] for t in range(4)], axis=0)
    first = lax.ppermute(jnp.where(odd, low, high), "y", [(0, 1), (1, 0), (2, 3), (3, 2)])
    second = lax.ppermute(jnp.where(odd, high, low), "y", [(1, 2), (2, 1), (3, 0), (0, 3)])
    below, above = jnp.where(odd, first, second), jnp.where(odd, second, first)
    done = pl.pallas_call(
        inner_kernel,
        out_shape=jax.ShapeDtypeStruct((HANDED, 128), f32),
        in_specs=[vmem()] * 3,
        out_specs=vmem(),
        scratch_shapes=[pltpu.VMEM((LAYERS * 8, 128), f32)] * len(NAMES),
        compiler_params=grant(16),
        cost_estimate=pl.CostEstimate(
            flops=3 * 10**9, bytes_accessed=8 * 10**6, transcendentals=0
        ),
        name="inner",
    )(got, wa, wb)
    back = pl.pallas_call(
        middle_kernel,
        out_shape=jax.ShapeDtypeStruct((4, 16, 16, 128), f32),
        in_specs=[vmem()] * 6,
        out_specs=vmem(),
        scratch_shapes=[pltpu.VMEM((LAYERS * 8, 128), f32)] * len(NAMES),
        compiler_params=grant(16),
        name="sweeps",
    )(done, below, above, wa, wb, ends)
    home = lax.all_to_all(back.reshape(UNITS, 16, 128), ("tm", "zx"), 0, 0, tiled=True)
    new, end = pl.pallas_call(
        backward_kernel,
        out_shape=(jax.ShapeDtypeStruct((2, 256, 128), f32),) * 2,
        in_specs=[vmem()] * 2,
        out_specs=(anywhere(),) * 2,
        scratch_shapes=[
            pltpu.VMEM((2, 256, 128), f32),
            pltpu.VMEM((2, 256, 128), f32),
            pltpu.SemaphoreType.DMA((4,)),
        ],
        compiler_params=grant(8),
        name="backward",
    )(home, wt)
    return new.reshape(2, 64, 4, 128), end.reshape(2, 64, 4, 128)


def solution(mesh):
    finer = Mesh(mesh.devices.reshape(4, 4, 16), ("tm", "y", "zx"))
    basis, table = modes()
    placed = P("tm", None, ("y", "zx"), None)
    return jax.shard_map(
        functools.partial(shards, basis, table),
        mesh=finer,
        in_specs=(placed, P(), P(), P()),
        out_specs=(placed, placed),
        check_vma=False,
    )
```
